128 devices in a mesh: section: 2 (over core), fsdp: 4 (over x), ctx: 16 (over y, z).
Axes of the slice: x: 4, y: 4, z: 4, core: 2. Of those that a mesh axis runs over, the one named last changes fastest.
Arguments:
- boundary: bfloat16 [2, 2, 4, 1024, 768], P('section', None, 'fsdp', 'ctx'), may hold values from -6 to 6
- block_order: int32 [32], replicated, may hold values from 0 to 31, each once
- qkv_weight: bfloat16 [2, 768, 2304], P('section', ('fsdp', 'ctx')), may hold values from -0.21875 to 0.21875
- out_weight: bfloat16 [2, 768, 768], P('section', ('fsdp', 'ctx')), may hold values from -2.5 to 2.5
- fc_weight: bfloat16 [2, 768, 3072], P('section', ('fsdp', 'ctx')), may hold values from -0.21875 to 0.21875
- proj_weight: bfloat16 [2, 3072, 768], P('section', ('fsdp', 'ctx')), may hold values from -0.109375 to 0.109375
- gains: bfloat16 [2, 2, 768], P('section', None, ('fsdp', 'ctx')), may hold values from 0.099609375 to 1.8984375
- biases: bfloat16 [2, 6, 768], P('section', None, ('fsdp', 'ctx')), may hold values from -3 to 3
- fc_bias: bfloat16 [2, 3072], P('section', ('fsdp', 'ctx')), may hold values from -3 to 3
Outputs:
- ends: float32 [2, 2, 4, 1024, 768], P('section', None, 'fsdp', 'ctx')
- qkv_grad: float32 [2, 768, 2304], P('section', ('fsdp', 'ctx'))
- out_grad: float32 [2, 768, 768], P('section', ('fsdp', 'ctx'))
- fc_grad: float32 [2, 768, 3072], P('section', ('fsdp', 'ctx'))
- proj_grad: float32 [2, 3072, 768], P('section', ('fsdp', 'ctx'))
- gains_grad: float32 [2, 2, 768], P('section', None, ('fsdp', 'ctx'))
- biases_grad: float32 [2, 6, 768], P('section', None, ('fsdp', 'ctx'))
- fc_bias_grad: float32 [2, 3072], P('section', ('fsdp', 'ctx'))
The draws below stay inside these ranges and needn't reach their ends.
Inputs may be any that keep to these rules, and one draw needn't show every extreme that they name: `block_order`: a permutation of the 32 block numbers, the same for every sequence.
All inputs are finite; a program needn't handle non-finite values.
Results may differ from the reference program's by a relative error of at most 0.014.
Values may be sent and summed in bfloat16 or wider, within the bound.
A program may use at most 192 MiB of HBM per device.

```python
import jax
import jax.numpy as jnp
from jax import lax

D = 768
HEADS = 12
HD = 64
FF = 3072
SEQ_LEN = 1024
MICRO = 2
GROUP_SEQS = 4
BLOCKS = 32


def block_levels(key, extent, cuts, smallest, high):
    level = 1.0
    for dim, shards_of in cuts:
        heights = jax.random.uniform(jax.random.fold_in(jax.random.fold_in(key, 6), dim), (shards_of,), jnp.float32, smallest / len(cuts), high / len(cuts))
        level = level * jnp.repeat(jnp.exp(heights), extent[dim] // shards_of).reshape((-1,) + (1,) * (len(extent) - 1 - dim))
    return level


def normal_values(own_key, shape, deviation, limit, split=(), held_as=jnp.bfloat16):
    factor_of = block_levels(own_key, shape, split, -0.22, 0.18) if split else 1.0
    result = jax.random.normal(own_key, shape, jnp.float32) * deviation * factor_of
    return jnp.minimum(jnp.maximum(result, -limit), limit).astype(held_as)


def setup_inputs(seed: int = 0) -> dict:
    streams_of = jax.random.split(jax.random.key(seed), 10)
    boundary = normal_values(streams_of[0], (2, MICRO, GROUP_SEQS, SEQ_LEN, D), 1.0, 6.0, ((0, 2), (2, 4), (3, 16)))
    block_order = jax.random.permutation(streams_of[1], BLOCKS).astype(jnp.int32)
    qkv_weight = normal_values(streams_of[2], (2, D, 3 * D), D ** -0.5, 0.21875, ((0, 2), (1, 64)))
    out_weight = normal_values(streams_of[3], (2, D, D), (max(1, 8 * D // SEQ_LEN)) ** -0.5, 2.5, ((0, 2), (1, 64)))
    fc_weight = normal_values(streams_of[4], (2, D, FF), D ** -0.5, 0.21875, ((0, 2), (1, 64)))
    proj_weight = normal_values(streams_of[5], (2, FF, D), FF ** -0.5, 0.109375, ((0, 2), (1, 64)))
    gains = jnp.clip(1.0 + 0.18 * jax.random.normal(streams_of[6], (2, 2, D), jnp.float32), 0.099609375, 1.8984375).astype(jnp.bfloat16)
    biases = normal_values(streams_of[7], (2, 6, D), 0.5, 3.0, ((0, 2), (2, 64)))
    fc_bias = normal_values(streams_of[8], (2, FF), 0.5, 3.0, ((0, 2), (1, 64)))
    return {"boundary": boundary, "block_order": block_order, "qkv_weight": qkv_weight, "out_weight": out_weight, "fc_weight": fc_weight, "proj_weight": proj_weight, "gains": gains, "biases": biases, "fc_bias": fc_bias}


EPS = 1e-05
ROOT = 0.7978845608028654
CUBIC = 0.044715
HIGH = lax.Precision.HIGHEST

@jax.custom_vjp
def low(v):
    return lax.optimization_barrier(v.astype(jnp.bfloat16)).astype(jnp.float32)

@jax.custom_vjp
def low_back(v):
    return v

def low_keep(v):
    return (low(v), None)

def low_pass(kept, grad):
    return (grad,)

def back_keep(v):
    return (v, None)

def back_low(kept, grad):
    return (low(grad),)
low.defvjp(low_keep, low_pass)
low_back.defvjp(back_keep, back_low)

def layer_norm(values, gain, shift):
    centre = values - lax.optimization_barrier(jnp.mean(values, -1, keepdims=True))
    spread = lax.optimization_barrier(jnp.mean(centre * centre, -1, keepdims=True))
    return centre * lax.rsqrt(spread + EPS) * gain + shift

def gelu_tanh(values):
    return 0.5 * values * (1.0 + jnp.tanh(ROOT * (values + CUBIC * values * values * values)))

def matmul(left, right):
    return jnp.dot(left, right, precision=HIGH, preferred_element_type=jnp.float32)

def attend(queries, key_rows, value_rows, key_pos):
    score_scale = HD ** (-0.5)
    block_rows = min(512, SEQ_LEN)
    block_count = SEQ_LEN // block_rows
    key_heads = key_rows.reshape(SEQ_LEN, HEADS, HD)
    value_heads = value_rows.reshape(SEQ_LEN, HEADS, HD)

    def one_block(pair):
        query_part, pos_part = pair
        raw_scores = low_back(jnp.einsum('qhd,khd->hqk', query_part, key_heads, precision=HIGH))
        allowed = key_pos[None, None, :] <= pos_part[None, :, None]
        scores = jnp.where(allowed, raw_scores * score_scale, -1e+30)
        row_top = lax.optimization_barrier(jnp.max(scores, -1, keepdims=True))
        exponent = jnp.exp(scores - row_top)
        soft = low(exponent / lax.optimization_barrier(jnp.sum(exponent, -1, keepdims=True)))
        return jnp.einsum('hqk,khd->qhd', soft, value_heads, precision=HIGH)
    blocks = lax.map(jax.checkpoint(one_block), (queries.reshape(block_count, block_rows, HEADS, HD), key_pos.reshape(block_count, block_rows)))
    return blocks.reshape(SEQ_LEN, D)

def layer(params, level, inputs, key_pos):
    query_key_value_weight, output_weight, w_fc, w_proj, gain_rows, bias_rows, fc_shift = [member[level] for member in params]
    normalized_input = low(layer_norm(inputs, gain_rows[0], bias_rows[0]))
    projected_output = matmul(normalized_input, query_key_value_weight)
    queries = low(low_back(projected_output[:, :D] + bias_rows[1]))
    key_rows = low(low_back(projected_output[:, D:2 * D]))
    value_rows = low(low_back(projected_output[:, 2 * D:] + bias_rows[2]))
    attention_output = low(low_back(attend(queries, key_rows, value_rows, key_pos)))
    branch = low_back(matmul(attention_output, output_weight) + bias_rows[3])
    resid = inputs + branch
    second = low(layer_norm(resid, gain_rows[1], bias_rows[4]))
    pre_act = low_back(matmul(second, w_fc) + fc_shift)
    activ = low(gelu_tanh(pre_act))
    mlp_out = low_back(matmul(activ, w_proj) + bias_rows[5])
    return resid + mlp_out

def reference(boundary, block_order, qkv_weight, out_weight, fc_weight, proj_weight, gains, biases, fc_bias):
    seq_count = MICRO * GROUP_SEQS
    inputs = boundary[0].astype(jnp.float32).reshape(seq_count, SEQ_LEN, D)
    cotangent = boundary[1].astype(jnp.float32).reshape(seq_count, SEQ_LEN, D)
    block_len = SEQ_LEN // BLOCKS
    index = jnp.arange(SEQ_LEN, dtype=jnp.int32)
    key_pos = (block_order[index // block_len] * block_len + index % block_len).astype(jnp.int32)
    params = tuple((member.astype(jnp.float32) for member in (qkv_weight, out_weight, fc_weight, proj_weight, gains, biases, fc_bias)))

    def forward(weights_all, sequences):

        def one_sequence(sequence):
            first = layer(weights_all, 0, sequence, key_pos)
            return layer(weights_all, 1, low(low_back(first)), key_pos)
        return lax.map(one_sequence, sequences)
    outputs, pullback = jax.vjp(forward, params, inputs)
    grads, grad_in = pullback(cotangent)
    ends = jnp.stack([grad_in, outputs]).reshape(2, MICRO, GROUP_SEQS, SEQ_LEN, D)
    return (ends, grads[0], grads[1], grads[2], grads[3], grads[4], grads[5], grads[6])
```

```python
import functools
import jax, jax.numpy as jnp
from jax import lax
from jax.experimental import pallas as pl
from jax.experimental.pallas import tpu as pltpu
from jax.sharding import PartitionSpec as P

MESH = pl.DeviceIdType.MESH
ORDERS = ((0, 1, 2), (1, 2, 0), (2, 0, 1))


def coordinates():
    ctx = lax.axis_index("ctx")
    return (lax.axis_index("fsdp"), ctx // 4, lax.rem(ctx, 4))


def device_at(section, spot):
    return (section, spot[0], spot[1] * 4 + spot[2])


def shifted(spot, axis, by):
    moved = list(spot)
    moved[axis] = lax.rem(spot[axis] + by, 4)
    return tuple(moved)


def slab(order, stage, spot, value, half=None, rows=None):
    index = [None, None, None]
    for t in range(3):
        axis = order[t]
        if t < stage:
            index[axis] = pl.ds(0, 4)
        elif t == stage:
            index[axis] = value
        else:
            index[axis] = spot[axis]
    if half is None:
        return tuple(index)
    if stage == 0:
        cut = rows // 2 // 16 * 16
        return tuple(index) + (pl.ds(0, cut) if half == 0 else pl.ds(cut, rows - cut),)
    index[order[0]] = pl.ds(2 * half, 2)
    return tuple(index)


def gather_kernel(priority, a_ref, b_ref, c_ref, ga, gb, gc, local_sem, send_sem, recv_sem, turn_sem):
    section = lax.axis_index("section")
    spot = coordinates()
    ins, outs = (a_ref, b_ref, c_ref), (ga, gb, gc)
    barrier = pltpu.get_barrier_semaphore()
    for axis in range(3):
        for by in (1, 3):
            pl.semaphore_signal(barrier, inc=1, device_id=device_at(section, shifted(spot, axis, by)), device_id_type=MESH)
    if priority:
        pl.semaphore_signal(barrier, inc=1, device_id=device_at(1 - section, spot), device_id_type=MESH)
    pl.semaphore_wait(barrier, 7 if priority else 6)
    if priority:
        @pl.when(section == 1)
        def _():
            pl.semaphore_wait(turn_sem, 1)
    own = []
    for part in range(3):
        copy = pltpu.make_async_copy(ins[part], outs[part].at[spot], local_sem.at[part])
        copy.start()
        own.append(copy)

    def remote(part, src, dst, stage, way, by):
        order = ORDERS[part]
        return pltpu.make_async_remote_copy(
            src_ref=src, dst_ref=dst,
            send_sem=send_sem.at[part, stage, way], recv_sem=recv_sem.at[part, stage, way],
            device_id=device_at(section, shifted(spot, order[stage], by)), device_id_type=MESH)

    pending = []
    for stage in range(3):
        first = []
        for part in range(3):
            order = ORDERS[part]
            mine = spot[order[stage]]
            idx = slab(order, stage, spot, mine)
            src = ins[part] if stage == 0 else outs[part].at[idx]
            for way, by in ((0, 1), (1, 3)):
                copy = remote(part, src, outs[part].at[idx], stage, way, by)
                copy.start()
                pending.append(copy)
        if stage == 0:
            for copy in own:
                copy.wait()
        for part in range(3):
            order = ORDERS[part]
            rows = ins[part].shape[0]
            mine = spot[order[stage]]
            for way, by, back in ((0, 1, 3), (1, 3, 1)):
                came = lax.rem(mine + back, 4)
                idx = slab(order, stage, spot, came)
                remote(part, outs[part].at[idx], outs[part].at[idx], stage, way, by).wait_recv()
                idx = slab(order, stage, spot, came, way, rows)
                copy = remote(part, outs[part].at[idx], outs[part].at[idx], stage, way + 2, by)
                copy.start()
                pending.append(copy)
        for part in range(3):
            order = ORDERS[part]
            rows = ins[part].shape[0]
            far = lax.rem(spot[order[stage]] + 2, 4)
            for way, by in ((0, 1), (1, 3)):
                idx = slab(order, stage, spot, far, way, rows)
                remote(part, outs[part].at[idx], outs[part].at[idx], stage, way + 2, by).wait_recv()
    if priority:
        @pl.when(section == 0)
        def _():
            pl.semaphore_signal(turn_sem, inc=1, device_id=device_at(1, spot), device_id_type=MESH)
    for copy in pending:
        copy.wait_send()


def gather_all(a, b, c, priority=True):
    return pl.pallas_call(
        functools.partial(gather_kernel, priority),
        out_shape=[jax.ShapeDtypeStruct((4, 4, 4) + x.shape, x.dtype) for x in (a, b, c)],
        in_specs=[pl.BlockSpec(memory_space=pl.ANY)] * 3,
        out_specs=[pl.BlockSpec(memory_space=pl.ANY)] * 3,
        scratch_shapes=[
            pltpu.SemaphoreType.DMA((3,)),
            pltpu.SemaphoreType.DMA((3, 3, 4)),
            pltpu.SemaphoreType.DMA((3, 3, 4)),
            pltpu.SemaphoreType.REGULAR,
        ],
        compiler_params=pltpu.CompilerParams(collective_id=0, has_side_effects=True),
    )(a, b, c)


def half_of(ref, stage, half):
    if stage < 2:
        return ref.at[pl.ds(2 * half, 2)]
    rows = ref.shape[0]
    cut = rows // 2 // 16 * 16
    return ref.at[pl.ds(0, cut)] if half == 0 else ref.at[pl.ds(cut, rows - cut)]


def each_chunk(stage, half, rows, body):
    if stage == 0:
        lo, size = (0, 4) if half is None else (2 * half, 2)

        def step(i, carry):
            body((lo + i // 4, lax.rem(i, 4)))
            return carry

        lax.fori_loop(0, size * 4, step, 0)
    elif stage == 1:
        lo, size = (0, 4) if half is None else (2 * half, 2)

        def step(i, carry):
            body((lo + i,))
            return carry

        lax.fori_loop(0, size, step, 0)
    else:
        cut = rows // 2 // 16 * 16
        body((pl.ds(0, rows) if half is None else (pl.ds(0, cut) if half == 0 else pl.ds(cut, rows - cut)),))


def wide(ref, index):
    return ref[index].astype(jnp.float32)


def scatter_kernel(*refs):
    ins, outs = refs[:3], refs[3:6]
    inbox = refs[6:33]
    own, mid, work1, work2 = refs[33:36], refs[36:39], refs[39:42], refs[42:45]
    local_sem, send_sem, recv_sem = refs[45:48]
    section = lax.axis_index("section")
    spot = coordinates()
    barrier = pltpu.get_barrier_semaphore()
    for axis in range(3):
        for by in (1, 3):
            pl.semaphore_signal(barrier, inc=1, device_id=device_at(section, shifted(spot, axis, by)), device_id_type=MESH)
    pl.semaphore_wait(barrier, 6)

    def box(part, stage, which):
        return inbox[(part * 3 + stage) * 3 + which]

    def source(part, stage, value):
        axis = ORDERS[part][stage]
        if stage == 0:
            index = [pl.ds(0, 4)] * 3
            index[axis] = value
            return ins[part].at[tuple(index)]
        if stage == 1:
            return work1[part].at[:, value] if part == 1 else work1[part].at[value]
        return work2[part].at[value]

    def remote(part, stage, kind, way, src, dst):
        by = 1 if way == 0 else 3
        return pltpu.make_async_remote_copy(
            src_ref=src, dst_ref=dst,
            send_sem=send_sem.at[part, stage, 2 * kind + way], recv_sem=recv_sem.at[part, stage, 2 * kind + way],
            device_id=device_at(section, shifted(spot, ORDERS[part][stage], by)), device_id_type=MESH)

    pending = []
    loads = {}

    def place(part, stage):
        return spot[ORDERS[part][stage]]

    def start(part, stage):
        here = place(part, stage)
        far = source(part, stage, lax.rem(here + 2, 4))
        near = (source(part, stage, lax.rem(here + 1, 4)), source(part, stage, lax.rem(here + 3, 4)))
        for way in (0, 1):
            copy = remote(part, stage, 0, way, half_of(far, stage, way), half_of(box(part, stage, 0), stage, way))
            copy.start()
            pending.append(copy)
        for way in (0, 1):
            copy = remote(part, stage, 1, way, half_of(near[way], stage, 1 - way), half_of(box(part, stage, 1 + way), stage, 1 - way))
            copy.start()
            pending.append(copy)
        if stage == 0:
            copies = [pltpu.make_async_copy(half_of(near[way], 0, way), half_of(mid[part], 0, way), local_sem.at[part, way]) for way in (0, 1)]
            copies.append(pltpu.make_async_copy(source(part, 0, here), own[part], local_sem.at[part, 2]))
            for copy in copies:
                copy.start()
            loads[part] = copies

    def middle(part, stage):
        here = place(part, stage)
        rows = outs[part].shape[0]
        fwd = box(part, stage, 0)
        for way in (0, 1):
            got = half_of(fwd, stage, way)
            remote(part, stage, 0, way, got, got).wait_recv()
            if stage == 0:
                loads[part][way].wait()
                add = mid[part]
            else:
                add = source(part, stage, lax.rem(here + (1 if way == 0 else 3), 4))

            def body(index):
                fwd[index] = (wide(fwd, index) + wide(add, index)).astype(fwd.dtype)

            each_chunk(stage, way, rows, body)
            copy = remote(part, stage, 2, way, got, half_of(box(part, stage, 1 + way), stage, way))
            copy.start()
            pending.append(copy)

    def finish(part, stage):
        here = place(part, stage)
        rows = outs[part].shape[0]
        left, right = box(part, stage, 1), box(part, stage, 2)
        for way in (0, 1):
            got = half_of(box(part, stage, 1 + way), stage, 1 - way)
            remote(part, stage, 1, way, got, got).wait_recv()
            got = half_of(box(part, stage, 1 + way), stage, way)
            remote(part, stage, 2, way, got, got).wait_recv()
        if stage == 0:
            loads[part][2].wait()
            mine = own[part]
        else:
            mine = source(part, stage, here)
        into = (work1, work2, outs)[stage][part]

        def body(index):
            into[index] = (wide(mine, index) + wide(left, index) + wide(right, index)).astype(into.dtype)

        each_chunk(stage, None, rows, body)

    for part in range(3):
        start(part, 0)
    for stage in range(3):
        for part in range(3):
            middle(part, stage)
        for part in range(3):
            finish(part, stage)
            if stage < 2:
                start(part, stage + 1)
    for copy in pending:
        copy.wait_send()


def scatter_all(a, b, c):
    rows = [x.shape[3] for x in (a, b, c)]
    shapes = lambda r: ((4, 4, r, 768), (4, r, 768), (r, 768))
    scratch = []
    for r in rows:
        for s in range(3):
            scratch += [pltpu.VMEM(shapes(r)[s], jnp.bfloat16)] * 3
    for level in (0, 0, 0, 1):
        scratch += [pltpu.VMEM(shapes(r)[level], jnp.bfloat16) for r in rows]
    return pl.pallas_call(
        scatter_kernel,
        out_shape=[jax.ShapeDtypeStruct((r, 768), jnp.float32) for r in rows],
        in_specs=[pl.BlockSpec(memory_space=pl.ANY)] * 3,
        out_specs=[pl.BlockSpec(memory_space=pltpu.VMEM)] * 3,
        scratch_shapes=scratch + [
            pltpu.SemaphoreType.DMA((3, 3)),
            pltpu.SemaphoreType.DMA((3, 3, 6)),
            pltpu.SemaphoreType.DMA((3, 3, 6)),
        ],
        compiler_params=pltpu.CompilerParams(collective_id=1, has_side_effects=True, vmem_limit_bytes=56 * 2**20),
    )(a, b, c)


def to_heads_kernel(units, x_ref, y_ref, local_sem, send_sem, recv_sem):
    section, fsdp, me = lax.axis_index("section"), lax.axis_index("fsdp"), lax.axis_index("ctx")
    rows = x_ref.shape[2]
    barrier = pltpu.get_barrier_semaphore()

    def mine(at):
        return pl.ds(pl.multiple_of(at * rows, rows), rows)

    def remote(unit, sender):
        return pltpu.make_async_remote_copy(
            src_ref=x_ref.at[unit], dst_ref=y_ref.at[:, mine(sender)],
            send_sem=send_sem.at[unit], recv_sem=recv_sem.at[sender],
            device_id=(section, fsdp, unit), device_id_type=MESH)

    @pl.when(me < units)
    def _():
        for other in range(16):
            @pl.when(me != other)
            def _():
                pl.semaphore_signal(barrier, inc=1, device_id=(section, fsdp, other), device_id_type=MESH)
        pl.semaphore_wait(barrier, units - 1)

    @pl.when(me >= units)
    def _():
        pl.semaphore_wait(barrier, units)

    for unit in range(units):
        @pl.when(me != unit)
        def _():
            remote(unit, me).start()

        @pl.when(me == unit)
        def _():
            pltpu.make_async_copy(x_ref.at[unit], y_ref.at[:, mine(me)], local_sem).start()

    @pl.when(me < units)
    def _():
        pltpu.make_async_copy(x_ref.at[me], y_ref.at[:, mine(me)], local_sem).wait()
        for sender in range(16):
            @pl.when(me != sender)
            def _():
                remote(0, sender).wait_recv()

    for unit in range(units):
        @pl.when(me != unit)
        def _():
            remote(unit, me).wait_send()


def to_heads(x, ident):
    units, n, rows, lanes = x.shape
    return pl.pallas_call(
        functools.partial(to_heads_kernel, units),
        out_shape=jax.ShapeDtypeStruct((n, 16 * rows, lanes), x.dtype),
        in_specs=[pl.BlockSpec(memory_space=pl.ANY)],
        out_specs=pl.BlockSpec(memory_space=pl.ANY),
        scratch_shapes=[
            pltpu.SemaphoreType.DMA,
            pltpu.SemaphoreType.DMA((units,)),
            pltpu.SemaphoreType.DMA((16,)),
        ],
        compiler_params=pltpu.CompilerParams(collective_id=ident, has_side_effects=True),
    )(x)


def from_heads_kernel(units, y_ref, x_ref, local_sem, send_sem, recv_sem):
    section, fsdp, me = lax.axis_index("section"), lax.axis_index("fsdp"), lax.axis_index("ctx")
    rows = x_ref.shape[2]
    barrier = pltpu.get_barrier_semaphore()

    def mine(at):
        return pl.ds(pl.multiple_of(at * rows, rows), rows)

    def remote(unit, target):
        return pltpu.make_async_remote_copy(
            src_ref=y_ref.at[:, mine(target)], dst_ref=x_ref.at[unit],
            send_sem=send_sem.at[target], recv_sem=recv_sem.at[unit],
            device_id=(section, fsdp, target), device_id_type=MESH)

    for unit in range(units):
        @pl.when(me != unit)
        def _():
            pl.semaphore_signal(barrier, inc=1, device_id=(section, fsdp, unit), device_id_type=MESH)

    @pl.when(me < units)
    def _():
        pl.semaphore_wait(barrier, 15)
        for target in range(16):
            @pl.when(me != target)
            def _():
                remote(me, target).start()
        pltpu.make_async_copy(y_ref.at[:, mine(me)], x_ref.at[me], local_sem).start()
        pltpu.make_async_copy(y_ref.at[:, mine(me)], x_ref.at[me], local_sem).wait()

    for unit in range(units):
        @pl.when(me != unit)
        def _():
            remote(unit, 0).wait_recv()

    @pl.when(me < units)
    def _():
        for target in range(16):
            @pl.when(me != target)
            def _():
                remote(me, target).wait_send()


def from_heads(y, units, ident):
    n, total, lanes = y.shape
    return pl.pallas_call(
        functools.partial(from_heads_kernel, units),
        out_shape=jax.ShapeDtypeStruct((units, n, total // 16, lanes), y.dtype),
        in_specs=[pl.BlockSpec(memory_space=pl.ANY)],
        out_specs=pl.BlockSpec(memory_space=pl.ANY),
        scratch_shapes=[
            pltpu.SemaphoreType.DMA,
            pltpu.SemaphoreType.DMA((16,)),
            pltpu.SemaphoreType.DMA((units,)),
        ],
        compiler_params=pltpu.CompilerParams(collective_id=ident, has_side_effects=True),
    )(y)


EPS = 1e-05
ROOT = 0.7978845608028654
CUBIC = 0.044715
UNITS = 12
WIDTH = 768
PADDED = 1024
FF = 3072
ROWS = 128
HD = 64
BF = jnp.bfloat16
F32 = jnp.float32


def dot(left, right, over=((1,), (0,))):
    return lax.dot_general(left, right, (over, ((), ())), preferred_element_type=F32)


NT = ((1,), (1,))
TN = ((0,), (0,))


def ones_lane():
    return (lax.rem(lax.broadcasted_iota(jnp.int32, (1, PADDED), 1), 16) == 12).astype(F32)


def padded(rows, spread):
    return (dot(rows, spread) + ones_lane()).astype(BF)


def unpadded(rows, spread):
    high = rows.astype(BF)
    low = (rows - high.astype(F32)).astype(BF)
    return dot(high, spread, NT) + dot(low, spread, NT)


def extras(weight):
    lane = lax.rem(lax.broadcasted_iota(jnp.int32, (16, PADDED), 1), 16)
    row = lax.broadcasted_iota(jnp.int32, (16, PADDED), 0)
    return dot(((lane == row + 13) & (row < 3)).astype(F32).astype(BF), weight)


def normal(values):
    centre = values - jnp.mean(values, -1, keepdims=True)
    scale = lax.rsqrt(jnp.mean(centre * centre, -1, keepdims=True) + EPS)
    return centre * scale, scale


def norm_back(grad, n, scale):
    return scale * (grad - jnp.mean(grad, -1, keepdims=True) - n * jnp.mean(grad * n, -1, keepdims=True))


def flat(block):
    return block.reshape(PADDED, WIDTH)


def joined(ref):
    return jnp.concatenate(
        [jnp.concatenate([ref[m * 6 + h, 0] for h in range(6)], axis=1) for m in range(2)], axis=0)


def split_into(ref, rows):
    for m in range(2):
        for h in range(6):
            ref[m * 6 + h, 0] = rows[m * 64:(m + 1) * 64, h * 128:(h + 1) * 128]


def qkv_kernel(u_ref, w_ref, e_ref, x_ref, apad):
    weight = flat(w_ref[...])

    @pl.when(pl.program_id(0) == 0)
    def _():
        more = extras(weight)
        n, scale = normal(u_ref[...].astype(F32))
        apad[...] = padded((n * more[0:1] + more[1:2]).astype(BF), e_ref[...])

    split_into(x_ref, dot(apad[...], weight).astype(BF))


def whole(shape):
    return pl.BlockSpec(shape, lambda *i: (0,) * len(shape))


VMEM_LIMIT = 56 * 2**20


def qkv_call(u, ga, spread):
    return pl.pallas_call(
        qkv_kernel,
        grid=(3,),
        out_shape=jax.ShapeDtypeStruct((UNITS, 3, 64, 128), BF),
        in_specs=[whole((ROWS, WIDTH)), pl.BlockSpec((64, 16, WIDTH), lambda p: (0, p, 0)), whole((WIDTH, PADDED))],
        out_specs=pl.BlockSpec((UNITS, 1, 64, 128), lambda p: (0, p, 0, 0)),
        scratch_shapes=[pltpu.VMEM((ROWS, PADDED), BF)],
        compiler_params=pltpu.CompilerParams(vmem_limit_bytes=VMEM_LIMIT),
    )(u, ga, spread)


def gelu_parts(f):
    t = jnp.tanh(ROOT * (f + CUBIC * f * f * f))
    return t, 0.5 * f * (1.0 + t)


def mlp_kernel(o_ref, u_ref, wo_ref, wf_ref, wp_ref, e_ref, y_ref, r_ref, f_ref, bpad):
    @pl.when(pl.program_id(0) == 0)
    def _():
        wo = flat(wo_ref[...])
        more = extras(wo)
        r = u_ref[...].astype(F32) + dot(padded(joined(o_ref), e_ref[...]), wo)
        r_ref[...] = r
        n, scale = normal(r)
        bpad[...] = padded((n * more[0:1] + more[1:2]).astype(BF), e_ref[...])
        y_ref[...] = r + more[2:3]

    f = dot(bpad[...], flat(wf_ref[...]))
    f_ref[...] = f
    y_ref[...] += dot(gelu_parts(f)[1].astype(BF), wp_ref[...])


def mlp_call(o, u, ga, gb, gc, spread):
    piece = lambda p: pl.BlockSpec((64, 16, WIDTH), p)
    return pl.pallas_call(
        mlp_kernel,
        grid=(4,),
        out_shape=[
            jax.ShapeDtypeStruct((ROWS, WIDTH), F32),
            jax.ShapeDtypeStruct((ROWS, WIDTH), F32),
            jax.ShapeDtypeStruct((ROWS, FF), F32),
        ],
        in_specs=[
            whole((UNITS, 1, 64, 128)), whole((ROWS, WIDTH)), piece(lambda k: (0, 3, 0)),
            piece(lambda k: (0, k, 0)), pl.BlockSpec((WIDTH, WIDTH), lambda k: (k, 0)), whole((WIDTH, PADDED)),
        ],
        out_specs=[whole((ROWS, WIDTH)), whole((ROWS, WIDTH)), pl.BlockSpec((ROWS, WIDTH), lambda k: (0, k))],
        scratch_shapes=[pltpu.VMEM((ROWS, PADDED), BF)],
        compiler_params=pltpu.CompilerParams(vmem_limit_bytes=VMEM_LIMIT),
    )(o, u, ga, gb, gc, spread)


def mlp_back_kernel(full, g_ref, f_ref, r_ref, wo_ref, wf_ref, wp_ref, e_ref, *refs):
    if full:
        do_ref, dr_ref, small_ref, db_ref, dc_ref, bpad, dbacc = refs
    else:
        do_ref, dr_ref, dbacc = refs
    k = pl.program_id(0)

    @pl.when(k == 0)
    def _():
        dbacc[...] = jnp.zeros_like(dbacc)
        if full:
            more = extras(flat(wo_ref[...]))
            n, scale = normal(r_ref[...])
            bpad[...] = padded((n * more[0:1] + more[1:2]).astype(BF), e_ref[...])

    dm = g_ref[...]
    f = f_ref[...]
    t, act = gelu_parts(f)
    slope = 0.5 * (1.0 + t) + 0.5 * f * (1.0 - t * t) * (ROOT * (1.0 + 3 * CUBIC * f * f))
    df = (dot(dm, wp_ref[...], NT) * slope).astype(BF)
    if full:
        dc_ref[...] = dot(act.astype(BF), dm, TN).astype(BF)
        db_ref[...] = dot(bpad[...], df, TN).astype(BF).reshape(64, 16, WIDTH)
    dbacc[...] += dot(df, flat(wf_ref[...]), NT)

    @pl.when(k == 3)
    def _():
        wo = flat(wo_ref[...])
        more = extras(wo)
        n, scale = normal(r_ref[...])
        db = unpadded(dbacc[...], e_ref[...])
        dr = dm.astype(F32) + norm_back(more[0:1] * db, n, scale)
        dr_ref[...] = dr
        do = dot(dr.astype(BF), wo, NT).astype(BF)
        split_into(do_ref, dot(do, e_ref[...], NT).astype(BF))
        if full:
            small_ref[0:1] = jnp.sum(db * n, 0, keepdims=True)
            small_ref[1:2] = jnp.sum(db, 0, keepdims=True)
            small_ref[2:3] = jnp.sum(dm.astype(F32), 0, keepdims=True)
            small_ref[3:8] = jnp.zeros((5, WIDTH), F32)


def mlp_back_call(full, g, f, r, ga, gb, gc, spread):
    piece = lambda p: pl.BlockSpec((64, 16, WIDTH), p)
    out_shape = [jax.ShapeDtypeStruct((UNITS, 1, 64, 128), BF), jax.ShapeDtypeStruct((ROWS, WIDTH), F32)]
    out_specs = [whole((UNITS, 1, 64, 128)), whole((ROWS, WIDTH))]
    scratch = [pltpu.VMEM((ROWS, PADDED), F32)]
    if full:
        out_shape += [
            jax.ShapeDtypeStruct((8, WIDTH), F32),
            jax.ShapeDtypeStruct((64, 64, WIDTH), BF),
            jax.ShapeDtypeStruct((FF, WIDTH), BF),
        ]
        out_specs += [whole((8, WIDTH)), piece(lambda k: (0, k, 0)), pl.BlockSpec((WIDTH, WIDTH), lambda k: (k, 0))]
        scratch = [pltpu.VMEM((ROWS, PADDED), BF)] + scratch
    return pl.pallas_call(
        functools.partial(mlp_back_kernel, full),
        grid=(4,),
        out_shape=out_shape,
        in_specs=[
            whole((ROWS, WIDTH)), pl.BlockSpec((ROWS, WIDTH), lambda k: (0, k)), whole((ROWS, WIDTH)),
            piece(lambda k: (0, 3, 0)), piece(lambda k: (0, k, 0)),
            pl.BlockSpec((WIDTH, WIDTH), lambda k: (k, 0)), whole((WIDTH, PADDED)),
        ],
        out_specs=out_specs,
        scratch_shapes=scratch,
        compiler_params=pltpu.CompilerParams(vmem_limit_bytes=VMEM_LIMIT),
    )(g, f, r, ga, gb, gc, spread)


def qkv_back_kernel(full, dx_ref, w_ref, u_ref, dr_ref, e_ref, *refs):
    if full:
        o_ref, small_ref, gu_ref, da_ref, gain, daacc, apad = refs
    else:
        gu_ref, gain, daacc = refs
    p = pl.program_id(0)

    @pl.when(p == 0)
    def _():
        more = extras(flat(w_ref[...]))
        gain[...] = jnp.broadcast_to(more[0:1], gain.shape)
        daacc[...] = jnp.zeros_like(daacc)
        if full:
            n, scale = normal(u_ref[...].astype(F32))
            apad[...] = padded((n * more[0:1] + more[1:2]).astype(BF), e_ref[...])

    def stored(grad, rows):
        grad = grad.reshape(64, 16, WIDTH)
        if rows is not None:
            at = lax.broadcasted_iota(jnp.int32, (16, WIDTH), 0)
            add = jnp.zeros((16, WIDTH), F32)
            for i, row in enumerate(rows):
                add = add + jnp.where(at == 13 + i, row, 0.0)
            grad = grad + add[None]
        da_ref[...] = grad.astype(BF)

    @pl.when(p < 3)
    def _():
        dx = joined(dx_ref)
        daacc[...] += dot(dx, flat(w_ref[...]), NT)
        if full:
            grad = dot(apad[...], dx, TN)

            @pl.when(p == 0)
            def _():
                stored(grad, [small_ref[i:i + 1] for i in range(3)])

            @pl.when(p > 0)
            def _():
                stored(grad, None)

    @pl.when(p == (3 if full else 2))
    def _():
        n, scale = normal(u_ref[...].astype(F32))
        da = unpadded(daacc[...], e_ref[...])
        gu_ref[...] = dr_ref[...] + norm_back(gain[0:1] * da, n, scale)
        if full:
            grad = dot(padded(joined(o_ref), e_ref[...]), dr_ref[...].astype(BF), TN)
            stored(grad, [jnp.sum(da * n, 0, keepdims=True), jnp.sum(da, 0, keepdims=True)])


def qkv_back_call(full, dx, ga, u, dr, spread, o=None, small=None):
    last = lambda p: jnp.minimum(p, 2)
    in_specs = [
        pl.BlockSpec((UNITS, 1, 64, 128), lambda p: (0, last(p), 0, 0)),
        pl.BlockSpec((64, 16, WIDTH), lambda p: (0, last(p), 0)),
        whole((ROWS, WIDTH)), whole((ROWS, WIDTH)), whole((WIDTH, PADDED)),
    ]
    args = [dx, ga, u, dr, spread]
    out_shape = [jax.ShapeDtypeStruct((ROWS, WIDTH), F32)]
    out_specs = [whole((ROWS, WIDTH))]
    scratch = [pltpu.VMEM((8, WIDTH), F32), pltpu.VMEM((ROWS, PADDED), F32)]
    if full:
        in_specs += [whole((UNITS, 1, 64, 128)), whole((8, WIDTH))]
        args += [o, small]
        out_shape += [jax.ShapeDtypeStruct((64, 64, WIDTH), BF)]
        out_specs += [pl.BlockSpec((64, 16, WIDTH), lambda p: (0, p, 0))]
        scratch += [pltpu.VMEM((ROWS, PADDED), BF)]
    return pl.pallas_call(
        functools.partial(qkv_back_kernel, full),
        grid=(4 if full else 3,),
        out_shape=out_shape, in_specs=in_specs, out_specs=out_specs, scratch_shapes=scratch,
        compiler_params=pltpu.CompilerParams(vmem_limit_bytes=VMEM_LIMIT),
    )(*args)


SEQ = 1024
QB = 256


def head_mask(rows, head):
    lane = lax.broadcasted_iota(jnp.int32, rows.shape, 1)
    return jnp.where((lane >= 64 * head) & (lane < 64 * head + 64), rows, jnp.zeros_like(rows))


def scores_of(keys, query, kpos_ref, qpos):
    raw = dot(keys, query, NT)
    return jnp.where(kpos_ref[...] <= qpos, raw, -1e30)


def attend_kernel(x_ref, kpos_ref, qpos_ref, q_ref, o_ref, lse_ref, vt):
    @pl.when(pl.program_id(0) == 0)
    def _():
        vt[...] = x_ref[2].astype(F32).T.astype(BF)

    keys = x_ref[1]
    qpos = qpos_ref[...]
    query = q_ref[0] * jnp.array(0.125, BF)
    parts, stats = [], []
    for head in range(2):
        s = scores_of(keys, head_mask(query, head), kpos_ref, qpos)
        top = jnp.max(s, 0, keepdims=True)
        e = jnp.exp(s - top)
        total = jnp.sum(e, 0, keepdims=True)
        p = (e * (1.0 / total)).astype(BF)
        parts.append(dot(vt[64 * head:64 * head + 64], p))
        stats.append(top + jnp.log(total))
    o_ref[0] = jnp.concatenate(parts, 0).T.astype(BF)
    lse_ref[...] = jnp.concatenate(stats + [jnp.zeros((6, QB), F32)], 0)


def attend_call(x, kpos, qpos):
    return pl.pallas_call(
        attend_kernel,
        grid=(SEQ // QB,),
        out_shape=[jax.ShapeDtypeStruct((1, SEQ, 128), BF), jax.ShapeDtypeStruct((8, SEQ), F32)],
        in_specs=[
            whole((3, SEQ, 128)), whole((SEQ, 1)), pl.BlockSpec((1, QB), lambda i: (0, i)),
            pl.BlockSpec((1, QB, 128), lambda i: (0, i, 0)),
        ],
        out_specs=[pl.BlockSpec((1, QB, 128), lambda i: (0, i, 0)), pl.BlockSpec((8, QB), lambda i: (0, i))],
        scratch_shapes=[pltpu.VMEM((128, SEQ), BF)],
        compiler_params=pltpu.CompilerParams(vmem_limit_bytes=VMEM_LIMIT),
    )(x, kpos, qpos, x)


def attend_back_kernel(x_ref, kpos_ref, qpos_ref, q_ref, do_ref, lse_ref, out_ref, kt, dk, dv):
    i = pl.program_id(0)

    @pl.when(i == 0)
    def _():
        kt[...] = x_ref[1].astype(F32).T.astype(BF)
        dk[...] = jnp.zeros_like(dk)
        dv[...] = jnp.zeros_like(dv)

    keys, vals = x_ref[1], x_ref[2]
    qpos = qpos_ref[...]
    query, do = q_ref[0], do_ref[0]
    parts = []
    for head in range(2):
        q_own, do_own = head_mask(query, head), head_mask(do, head)
        s = scores_of(keys, q_own * jnp.array(0.125, BF), kpos_ref, qpos)
        p = jnp.exp(s - lse_ref[head:head + 1])
        dp = dot(vals, do_own, NT)
        delta = jnp.sum(p * dp, 0, keepdims=True)
        ds = (p * (dp - delta) * 0.125).astype(BF)
        dk[...] += dot(ds, q_own)
        dv[...] += dot(p.astype(BF), do_own)
        parts.append(dot(kt[64 * head:64 * head + 64], ds))
    at = pl.ds(pl.multiple_of(i * QB, QB), QB)
    out_ref[0, at] = jnp.concatenate(parts, 0).T.astype(BF)

    @pl.when(i == SEQ // QB - 1)
    def _():
        out_ref[1] = dk[...].astype(BF)
        out_ref[2] = dv[...].astype(BF)


def attend_back_call(x, kpos, qpos, do, lse):
    return pl.pallas_call(
        attend_back_kernel,
        grid=(SEQ // QB,),
        out_shape=jax.ShapeDtypeStruct((3, SEQ, 128), BF),
        in_specs=[
            whole((3, SEQ, 128)), whole((SEQ, 1)), pl.BlockSpec((1, QB), lambda i: (0, i)),
            pl.BlockSpec((1, QB, 128), lambda i: (0, i, 0)), pl.BlockSpec((1, QB, 128), lambda i: (0, i, 0)),
            pl.BlockSpec((8, QB), lambda i: (0, i)),
        ],
        out_specs=whole((3, SEQ, 128)),
        scratch_shapes=[pltpu.VMEM((128, SEQ), BF), pltpu.VMEM((SEQ, 128), F32), pltpu.VMEM((SEQ, 128), F32)],
        compiler_params=pltpu.CompilerParams(vmem_limit_bytes=VMEM_LIMIT),
    )(x, kpos, qpos, x, do, lse)


def positions(block_order):
    index = jnp.arange(SEQ, dtype=jnp.int32)
    blocks = block_order.shape[0]
    length = SEQ // blocks
    table = jnp.arange(blocks, dtype=jnp.int32)
    chosen = jnp.sum(jnp.where((index // length)[:, None] == table[None, :], block_order[None, :], 0), axis=1)
    return chosen * length + index % length


def packed(chunk, qkv, out, fc, gains, biases, fc_bias):
    wide_rows = lax.dynamic_update_slice(
        jnp.zeros((8, WIDTH), BF), jnp.concatenate([gains, biases], 0), (0, 12 * chunk))
    gain0, gain1 = wide_rows[0:1], wide_rows[1:2]
    bias = [wide_rows[2 + i:3 + i] for i in range(6)]
    none = jnp.zeros((1, WIDTH), BF)
    fc_rows = lax.dynamic_update_slice(jnp.zeros((FF,), BF), fc_bias, (48 * chunk,)).reshape(4, WIDTH)
    a = jnp.concatenate([
        qkv[:, :WIDTH], bias[1], gain0, bias[0], none,
        qkv[:, WIDTH:2 * WIDTH], none, none, none, none,
        qkv[:, 2 * WIDTH:], bias[2], none, none, none,
        out, bias[3], gain1, bias[4], bias[5],
    ], 0)
    rows = []
    for k in range(4):
        rows += [fc[:, k * WIDTH:(k + 1) * WIDTH], fc_rows[k:k + 1], none, none, none]
    return a, jnp.concatenate(rows, 0)


def local(boundary, block_order, qkv_weight, out_weight, fc_weight, proj_weight, gains, biases, fc_bias):
    section = lax.axis_index("section")
    chunk = lax.axis_index("fsdp") * 16 + lax.axis_index("ctx")
    key_pos = positions(block_order)
    kpos, qpos = key_pos[:, None], key_pos[None, :]
    source = lax.broadcasted_iota(jnp.int32, (WIDTH, PADDED), 0)
    target = lax.broadcasted_iota(jnp.int32, (WIDTH, PADDED), 1)
    spread = ((target // 16 == source // 12) & (target % 16 == source % 12)).astype(BF)

    a, b = packed(chunk, qkv_weight[0], out_weight[0], fc_weight[0], gains[0], biases[0], fc_bias[0])
    ga, gb, gc = gather_all(a, b, proj_weight[0], False)
    ga, gb, gc = ga.reshape(64, 64, WIDTH), gb.reshape(64, 64, WIDTH), gc.reshape(FF, WIDTH)

    def forward(u):
        x = to_heads(qkv_call(u, ga, spread), 2)
        attended, lse = attend_call(x, kpos, qpos)
        o = from_heads(attended, UNITS, 3)
        y, r, f = mlp_call(o, u, ga, gb, gc, spread)
        return y, (u, x, lse, o, r, f)

    def backward(full, saved, g):
        u, x, lse, o, r, f = saved
        do, dr, *more = mlp_back_call(full, g, f, r, ga, gb, gc, spread)
        dx = from_heads(attend_back_call(x, kpos, qpos, to_heads(do, 4), lse), UNITS, 5)
        if not full:
            return qkv_back_call(False, dx, ga, u, dr, spread)[0]
        small, grad_b, grad_c = more
        gu, grad_a = qkv_back_call(True, dx, ga, u, dr, spread, o, small)
        return gu, grad_a, grad_b, grad_c

    held = boundary[0].reshape(ROWS, WIDTH)
    first, _ = forward(held)
    sent = lax.ppermute(first.astype(BF), "section", [(0, 1)])
    y, saved = forward(jnp.where(section == 0, held, sent))
    back = backward(False, saved, held)
    returned = lax.ppermute(back.astype(BF), "section", [(1, 0)])
    gu, grad_a, grad_b, grad_c = backward(True, saved, jnp.where(section == 1, held, returned))
    ends = jnp.where(section == 0, gu, y).reshape(1, 2, 1, 64, WIDTH)
    ra, rb, rc = scatter_all(
        grad_a.reshape(4, 4, 4, 64, WIDTH), grad_b.reshape(4, 4, 4, 64, WIDTH), grad_c.reshape(4, 4, 4, 48, WIDTH))
    qkv_grad = jnp.concatenate([ra[0:12], ra[16:28], ra[32:44]], 1)
    fc_grad = jnp.concatenate([rb[16 * k:16 * k + 12] for k in range(4)], 1)
    small = jnp.stack([ra[61], ra[13], ra[62], ra[12], ra[44], ra[60], ra[14], ra[15]])
    small = lax.dynamic_slice(small, (0, 12 * chunk), (8, 12))
    fc_rows = jnp.concatenate([rb[16 * k + 12] for k in range(4)])
    fc_small = lax.dynamic_slice(fc_rows, (48 * chunk,), (48,))
    return (
        ends, qkv_grad[None], ra[48:60][None], fc_grad[None], rc[None],
        small[0:2][None], small[2:8][None], fc_small[None],
    )


def solution(mesh):
    rows = P("section", ("fsdp", "ctx"), None)
    lanes = P("section", None, ("fsdp", "ctx"))
    ends = P("section", None, "fsdp", "ctx", None)
    flat_rows = P("section", ("fsdp", "ctx"))
    return jax.shard_map(
        local, mesh=mesh,
        in_specs=(ends, P(), rows, rows, rows, rows, lanes, lanes, flat_rows),
        out_specs=(ends, rows, rows, rows, rows, lanes, lanes, flat_rows),
        check_vma=False)
```

```python
import functools
import jax
import jax.numpy as jnp
from jax import lax
from jax.experimental import pallas as pl
from jax.experimental.pallas import tpu as pltpu
from jax.sharding import PartitionSpec as P

MESH = pl.DeviceIdType.MESH
ORDERS = ((0, 1, 2), (1, 2, 0), (2, 0, 1))
ROWS_OF = (64, 64, 48)


def coordinates():
    ctx = lax.axis_index("ctx")
    return (lax.axis_index("fsdp"), ctx // 4, lax.rem(ctx, 4))


def device_at(section, spot):
    return (section, spot[0], spot[1] * 4 + spot[2])


def shifted(spot, axis, by):
    moved = list(spot)
    moved[axis] = lax.rem(spot[axis] + by, 4)
    return tuple(moved)


def cut_of(rows, half):
    cut = rows // 2 // 16 * 16
    return pl.ds(0, cut) if half == 0 else pl.ds(cut, rows - cut)


def greet_neighbours(section, spot):
    barrier = pltpu.get_barrier_semaphore()
    for axis in range(3):
        for by in (1, 3):
            pl.semaphore_signal(barrier, inc=1, device_id=device_at(section, shifted(spot, axis, by)), device_id_type=MESH)
    pl.semaphore_wait(barrier, 6)


def gather_kernel(active, qkv_ref, out_ref, fc_ref, proj_ref, wide_ref, line_ref, *refs):
    @pl.when(lax.axis_index("section") == active)
    def _():
        gather_body(qkv_ref, out_ref, fc_ref, proj_ref, wide_ref, line_ref, *refs[-9:])


def gather_body(qkv_ref, out_ref, fc_ref, proj_ref, wide_ref, line_ref, ga, gb, gc,
                a_ref, b_ref, stage_ref, local_sem, send_sem, recv_sem):
    section = lax.axis_index("section")
    spot = coordinates()
    ins, outs = (a_ref, b_ref, proj_ref), (ga, gb, gc)

    none = jnp.zeros((1, 768), jnp.float32)

    def pack(into, piece, weight, rows):
        stage_ref[0:12] = weight.astype(jnp.float32)
        stage_ref[12:16] = jnp.concatenate([none if row is None else row for row in rows], 0)
        into[16 * piece:16 * piece + 16] = stage_ref[...].astype(into.dtype)

    row = [wide_ref[i:i + 1] for i in range(8)]
    pack(a_ref, 0, qkv_ref[:, 0:768], [row[3], row[0], row[2], None])
    pack(a_ref, 1, qkv_ref[:, 768:1536], [None] * 4)
    pack(a_ref, 2, qkv_ref[:, 1536:2304], [row[4], None, None, None])
    pack(a_ref, 3, out_ref[...], [row[5], row[1], row[6], row[7]])
    for k in range(4):
        pack(b_ref, k, fc_ref[:, 768 * k:768 * k + 768], [line_ref[k:k + 1], None, None, None])

    greet_neighbours(section, spot)
    own = []
    for part in range(3):
        copy = pltpu.make_async_copy(ins[part], outs[part].at[spot], local_sem.at[part])
        copy.start()
        own.append(copy)

    pending = []

    def at(part, first, second, third, rows=None):
        index = [None, None, None]
        for axis, value in zip(ORDERS[part], (first, second, third)):
            index[axis] = value
        return outs[part].at[tuple(index) if rows is None else tuple(index) + (rows,)]

    def here(part):
        return tuple(spot[axis] for axis in ORDERS[part])

    def near(value, by):
        return lax.rem(value + by, 4)

    full = pl.ds(0, 4)

    def halves(half):
        return pl.ds(2 * half, 2)

    def remote(part, axis, slot, way, src, dst):
        by = 1 if way == 0 else 3
        return pltpu.make_async_remote_copy(
            src_ref=src, dst_ref=dst, send_sem=send_sem.at[part, slot, way], recv_sem=recv_sem.at[part, slot, way],
            device_id=device_at(section, shifted(spot, ORDERS[part][axis], by)), device_id_type=MESH)

    def send(part, axis, slot, way, src, dst=None):
        copy = remote(part, axis, slot, way, src, src if dst is None else dst)
        copy.start()
        pending.append(copy)

    def came(part, axis, slot, way, ref):
        remote(part, axis, slot, way, ref, ref).wait_recv()

    BACK = (3, 1)

    def third_item(part, item, by):
        p1, p2, p3 = here(part)
        for way in (0, 1):
            send(part, 2, 4 + 2 * item, way, at(part, full, near(p2, by), p3))

    def third_pass(part, item, by):
        p1, p2, p3 = here(part)
        for way in (0, 1):
            came(part, 2, 4 + 2 * item, way, at(part, full, near(p2, by), near(p3, BACK[way])))
            send(part, 2, 5 + 2 * item, way, at(part, halves(way), near(p2, by), near(p3, BACK[way])))

    for part in range(3):
        p1, p2, p3 = here(part)
        for way in (0, 1):
            send(part, 0, 0, way, ins[part], at(part, p1, p2, p3))
    for part in range(3):
        p1, p2, p3 = here(part)
        for way in (0, 1):
            v = near(p1, BACK[way])
            came(part, 0, 0, way, at(part, v, p2, p3))
            send(part, 0, 1, way, at(part, v, p2, p3, cut_of(ROWS_OF[part], way)))
    for part in range(3):
        p1, p2, p3 = here(part)
        for way in (0, 1):
            came(part, 0, 1, way, at(part, near(p1, 2), p2, p3, cut_of(ROWS_OF[part], way)))
        own[part].wait()
        for way in (0, 1):
            send(part, 1, 2, way, at(part, full, p2, p3))
    for part in range(3):
        third_item(part, 0, 0)
    for part in range(3):
        p1, p2, p3 = here(part)
        for way in (0, 1):
            v = near(p2, BACK[way])
            came(part, 1, 2, way, at(part, full, v, p3))
            send(part, 1, 3, way, at(part, halves(way), v, p3))
    for part in range(3):
        third_item(part, 1, 3)
        third_item(part, 2, 1)
    for part in range(3):
        p1, p2, p3 = here(part)
        for way in (0, 1):
            came(part, 1, 3, way, at(part, halves(way), near(p2, 2), p3))
        third_item(part, 3, 2)
    for item, by in ((0, 0), (1, 3), (2, 1), (3, 2)):
        for part in range(3):
            third_pass(part, item, by)
    for item, by in ((0, 0), (1, 3), (2, 1), (3, 2)):
        for part in range(3):
            p1, p2, p3 = here(part)
            for way in (0, 1):
                came(part, 2, 5 + 2 * item, way, at(part, halves(way), near(p2, by), near(p3, 2)))
    for copy in pending:
        copy.wait_send()


def gather_all(active, ident, shards, held=()):
    vmem = pl.BlockSpec(memory_space=pltpu.VMEM)
    anywhere = pl.BlockSpec(memory_space=pl.ANY)
    return pl.pallas_call(
        functools.partial(gather_kernel, active),
        out_shape=[jax.ShapeDtypeStruct((4, 4, 4, r, 768), jnp.bfloat16) for r in ROWS_OF],
        in_specs=[vmem] * 6 + [anywhere] * len(held),
        out_specs=[anywhere] * 3,
        scratch_shapes=[
            pltpu.VMEM((64, 768), jnp.bfloat16),
            pltpu.VMEM((64, 768), jnp.bfloat16),
            pltpu.VMEM((16, 768), jnp.float32),
            pltpu.SemaphoreType.DMA((3,)),
            pltpu.SemaphoreType.DMA((3, 12, 2)),
            pltpu.SemaphoreType.DMA((3, 12, 2)),
        ],
        input_output_aliases={6: 0, 7: 1, 8: 2} if held else {},
        compiler_params=pltpu.CompilerParams(collective_id=ident, has_side_effects=True),
    )(*shards, *held)


def wide(ref, index):
    return ref[index].astype(jnp.float32)


def scatter_kernel(active, *refs):
    @pl.when(lax.axis_index("section") == active)
    def _():
        scatter_body(*refs)


def scatter_body(*refs):
    ins, outs = refs[:3], refs[3:6]
    box0, box1, box2 = refs[6:9], refs[9:12], refs[12:15]
    own, mid, work1, work2 = refs[15:18], refs[18:21], refs[21:24], refs[24:27]
    local_sem, send_sem, recv_sem = refs[27:30]
    section = lax.axis_index("section")
    spot = coordinates()
    greet_neighbours(section, spot)

    def here(part):
        return tuple(spot[axis] for axis in ORDERS[part])

    def near(value, by):
        return lax.rem(value + by, 4)

    def at(part, first, second, third=pl.ds(0, 4)):
        index = [None, None, None]
        for axis, value in zip(ORDERS[part], (first, second, third)):
            index[axis] = value
        return ins[part].at[tuple(index)]

    def halves(half):
        return pl.ds(2 * half, 2)

    def remote(part, axis, slot, way, src, dst):
        by = 1 if way == 0 else 3
        return pltpu.make_async_remote_copy(
            src_ref=src, dst_ref=dst, send_sem=send_sem.at[part, slot, way], recv_sem=recv_sem.at[part, slot, way],
            device_id=device_at(section, shifted(spot, ORDERS[part][axis], by)), device_id_type=MESH)

    pending = []

    def send(part, axis, slot, way, src, dst):
        copy = remote(part, axis, slot, way, src, dst)
        copy.start()
        pending.append(copy)

    def came(part, axis, slot, way, ref):
        remote(part, axis, slot, way, ref, ref).wait_recv()

    ITEMS = (2, 1, 3, 0)
    loads = {}

    def first_send(part, item):
        p1, p2, p3 = here(part)
        w = near(p2, ITEMS[item])
        for way in (0, 1):
            send(part, 0, 3 * item, way, at(part, near(p1, 2), w, halves(way)), box0[part].at[item, 0, halves(way)])
        for way in (0, 1):
            copy = pltpu.make_async_copy(
                at(part, near(p1, 1 + 2 * way), w, halves(way)), mid[part].at[item, halves(way)], local_sem.at[part, item, way])
            copy.start()
            loads[part, item, way] = copy
        copy = pltpu.make_async_copy(at(part, p1, w), own[part].at[item], local_sem.at[part, item, 2])
        copy.start()
        loads[part, item, 2] = copy
        for way in (0, 1):
            send(part, 0, 3 * item + 1, way, at(part, near(p1, 1 + 2 * way), w, halves(1 - way)),
                 box0[part].at[item, 1 + way, halves(1 - way)])

    def loop(count, body):
        def step(i, carry):
            body(i)
            return carry
        lax.fori_loop(0, count, step, 0)

    def first_middle(part, item):
        for way in (0, 1):
            got = box0[part].at[item, 0, halves(way)]
            came(part, 0, 3 * item, way, got)
            loads[part, item, way].wait()

            def body(i):
                f = box0[part]
                f[item, 0, 2 * way + i] = (wide(f, (item, 0, 2 * way + i)) + wide(mid[part], (item, 2 * way + i))).astype(f.dtype)

            loop(2, body)
            send(part, 0, 3 * item + 2, way, got, box0[part].at[item, 1 + way, halves(way)])

    def first_finish(part, item):
        box = box0[part]
        for way in (0, 1):
            came(part, 0, 3 * item + 1, way, box.at[item, 1 + way, halves(1 - way)])
            came(part, 0, 3 * item + 2, way, box.at[item, 1 + way, halves(way)])
        loads[part, item, 2].wait()

        def body(i):
            work1[part][item, i] = (
                wide(own[part], (item, i)) + wide(box, (item, 1, i)) + wide(box, (item, 2, i))).astype(box.dtype)

        loop(4, body)

    def second_far(part):
        for way in (0, 1):
            send(part, 1, 12, way, work1[part].at[0, halves(way)], box1[part].at[0, halves(way)])

    def second_raw(part):
        for way in (0, 1):
            send(part, 1, 13, way, work1[part].at[1 + way, halves(1 - way)], box1[part].at[1 + way, halves(1 - way)])

    def second_middle(part):
        for way in (0, 1):
            got = box1[part].at[0, halves(way)]
            came(part, 1, 12, way, got)

            def body(i):
                f = box1[part]
                f[0, 2 * way + i] = (wide(f, (0, 2 * way + i)) + wide(work1[part], (1 + way, 2 * way + i))).astype(f.dtype)

            loop(2, body)
            send(part, 1, 14, way, got, box1[part].at[1 + way, halves(way)])

    def second_finish(part):
        box = box1[part]
        for way in (0, 1):
            came(part, 1, 13, way, box.at[1 + way, halves(1 - way)])
            came(part, 1, 14, way, box.at[1 + way, halves(way)])

        def body(i):
            work2[part][i] = (wide(work1[part], (3, i)) + wide(box, (1, i)) + wide(box, (2, i))).astype(box.dtype)

        loop(4, body)

    def third_send(part):
        p1, p2, p3 = here(part)
        rows = ROWS_OF[part]
        for way in (0, 1):
            cut = cut_of(rows, way)
            send(part, 2, 15, way, work2[part].at[near(p3, 2), cut], box2[part].at[0, cut])
        for way in (0, 1):
            cut = cut_of(rows, 1 - way)
            send(part, 2, 16, way, work2[part].at[near(p3, 1 + 2 * way), cut], box2[part].at[1 + way, cut])

    def third_middle(part):
        p1, p2, p3 = here(part)
        rows = ROWS_OF[part]
        box = box2[part]
        for way in (0, 1):
            cut = cut_of(rows, way)
            came(part, 2, 15, way, box.at[0, cut])
            box[0, cut] = (wide(box, (0, cut)) + wide(work2[part], (near(p3, 1 + 2 * way), cut))).astype(box.dtype)
            send(part, 2, 17, way, box.at[0, cut], box.at[1 + way, cut])

    def third_finish(part):
        p1, p2, p3 = here(part)
        rows = ROWS_OF[part]
        box = box2[part]
        for way in (0, 1):
            came(part, 2, 16, way, box.at[1 + way, cut_of(rows, 1 - way)])
            came(part, 2, 17, way, box.at[1 + way, cut_of(rows, way)])
        outs[part][...] = wide(work2[part], p3) + wide(box, 1) + wide(box, 2)

    parts = range(3)
    for item in range(4):
        for part in parts:
            first_send(part, item)
    for item in range(4):
        for part in parts:
            first_middle(part, item)
    for part in parts:
        first_finish(part, 0)
        second_far(part)
    for part in parts:
        first_finish(part, 1)
        first_finish(part, 2)
        second_raw(part)
    for part in parts:
        second_middle(part)
    for part in parts:
        first_finish(part, 3)
    for part in parts:
        second_finish(part)
        third_send(part)
    for part in parts:
        third_middle(part)
    for part in parts:
        third_finish(part)
    for copy in pending:
        copy.wait_send()


def scatter_all(active, ident, a, b, c):
    scratch = []
    for shape in ((4, 3, 4), (3, 4), (3,), (4, 4), (4, 4), (4, 4), (4,)):
        scratch += [pltpu.VMEM(shape + (r, 768), jnp.bfloat16) for r in ROWS_OF]
    return pl.pallas_call(
        functools.partial(scatter_kernel, active),
        out_shape=[jax.ShapeDtypeStruct((r, 768), jnp.float32) for r in ROWS_OF],
        in_specs=[pl.BlockSpec(memory_space=pl.ANY)] * 3,
        out_specs=[pl.BlockSpec(memory_space=pltpu.VMEM)] * 3,
        scratch_shapes=scratch + [
            pltpu.SemaphoreType.DMA((3, 4, 3)),
            pltpu.SemaphoreType.DMA((3, 18, 2)),
            pltpu.SemaphoreType.DMA((3, 18, 2)),
        ],
        compiler_params=pltpu.CompilerParams(collective_id=ident, has_side_effects=True, vmem_limit_bytes=60 * 2**20),
    )(a, b, c)


def to_heads_kernel(units, x_ref, y_ref, local_sem, send_sem, recv_sem):
    section, fsdp, me = lax.axis_index("section"), lax.axis_index("fsdp"), lax.axis_index("ctx")
    rows = x_ref.shape[2]
    barrier = pltpu.get_barrier_semaphore()

    def mine(at):
        return pl.ds(pl.multiple_of(at * rows, rows), rows)

    def remote(unit, sender):
        return pltpu.make_async_remote_copy(
            src_ref=x_ref.at[unit], dst_ref=y_ref.at[:, mine(sender)],
            send_sem=send_sem.at[unit], recv_sem=recv_sem.at[sender],
            device_id=(section, fsdp, unit), device_id_type=MESH)

    @pl.when(me < units)
    def _():
        for other in range(16):
            @pl.when(me != other)
            def _():
                pl.semaphore_signal(barrier, inc=1, device_id=(section, fsdp, other), device_id_type=MESH)
        pl.semaphore_wait(barrier, units - 1)

    @pl.when(me >= units)
    def _():
        pl.semaphore_wait(barrier, units)

    for unit in range(units):
        @pl.when(me != unit)
        def _():
            remote(unit, me).start()

        @pl.when(me == unit)
        def _():
            pltpu.make_async_copy(x_ref.at[unit], y_ref.at[:, mine(me)], local_sem).start()

    @pl.when(me < units)
    def _():
        pltpu.make_async_copy(x_ref.at[me], y_ref.at[:, mine(me)], local_sem).wait()
        for sender in range(16):
            @pl.when(me != sender)
            def _():
                remote(0, sender).wait_recv()

    for unit in range(units):
        @pl.when(me != unit)
        def _():
            remote(unit, me).wait_send()


def to_heads(x, ident):
    units, n, rows, lanes = x.shape
    return pl.pallas_call(
        functools.partial(to_heads_kernel, units),
        out_shape=jax.ShapeDtypeStruct((n, 16 * rows, lanes), x.dtype),
        in_specs=[pl.BlockSpec(memory_space=pl.ANY)],
        out_specs=pl.BlockSpec(memory_space=pl.ANY),
        scratch_shapes=[
            pltpu.SemaphoreType.DMA,
            pltpu.SemaphoreType.DMA((units,)),
            pltpu.SemaphoreType.DMA((16,)),
        ],
        compiler_params=pltpu.CompilerParams(collective_id=ident, has_side_effects=True),
    )(x)


def from_heads_kernel(units, y_ref, x_ref, local_sem, send_sem, recv_sem):
    section, fsdp, me = lax.axis_index("section"), lax.axis_index("fsdp"), lax.axis_index("ctx")
    rows = x_ref.shape[2]
    barrier = pltpu.get_barrier_semaphore()

    def mine(at):
        return pl.ds(pl.multiple_of(at * rows, rows), rows)

    def remote(unit, target):
        return pltpu.make_async_remote_copy(
            src_ref=y_ref.at[:, mine(target)], dst_ref=x_ref.at[unit],
            send_sem=send_sem.at[target], recv_sem=recv_sem.at[unit],
            device_id=(section, fsdp, target), device_id_type=MESH)

    for unit in range(units):
        @pl.when(me != unit)
        def _():
            pl.semaphore_signal(barrier, inc=1, device_id=(section, fsdp, unit), device_id_type=MESH)

    @pl.when(me < units)
    def _():
        pl.semaphore_wait(barrier, 15)
        for target in range(16):
            @pl.when(me != target)
            def _():
                remote(me, target).start()
        pltpu.make_async_copy(y_ref.at[:, mine(me)], x_ref.at[me], local_sem).start()
        pltpu.make_async_copy(y_ref.at[:, mine(me)], x_ref.at[me], local_sem).wait()

    for unit in range(units):
        @pl.when(me != unit)
        def _():
            remote(unit, 0).wait_recv()

    @pl.when(me < units)
    def _():
        for target in range(16):
            @pl.when(me != target)
            def _():
                remote(me, target).wait_send()


def from_heads(y, units, ident):
    n, total, lanes = y.shape
    return pl.pallas_call(
        functools.partial(from_heads_kernel, units),
        out_shape=jax.ShapeDtypeStruct((units, n, total // 16, lanes), y.dtype),
        in_specs=[pl.BlockSpec(memory_space=pl.ANY)],
        out_specs=pl.BlockSpec(memory_space=pl.ANY),
        scratch_shapes=[
            pltpu.SemaphoreType.DMA,
            pltpu.SemaphoreType.DMA((16,)),
            pltpu.SemaphoreType.DMA((units,)),
        ],
        compiler_params=pltpu.CompilerParams(collective_id=ident, has_side_effects=True),
    )(y)


EPS = 1e-05
ROOT = 0.7978845608028654
CUBIC = 0.044715
UNITS = 12
WIDTH = 768
PADDED = 1024
FF = 3072
ROWS = 128
HD = 64
BF = jnp.bfloat16
F32 = jnp.float32


def dot(left, right, over=((1,), (0,))):
    return lax.dot_general(left, right, (over, ((), ())), preferred_element_type=F32)


NT = ((1,), (1,))
TN = ((0,), (0,))


def ones_lane():
    return (lax.rem(lax.broadcasted_iota(jnp.int32, (1, PADDED), 1), 16) == 12).astype(F32)


def padded(rows, spread):
    return (dot(rows, spread) + ones_lane()).astype(BF)


def unpadded(rows, spread):
    high = rows.astype(BF)
    low = (rows - high.astype(F32)).astype(BF)
    return dot(high, spread, NT) + dot(low, spread, NT)


def extras(weight):
    lane = lax.rem(lax.broadcasted_iota(jnp.int32, (16, PADDED), 1), 16)
    row = lax.broadcasted_iota(jnp.int32, (16, PADDED), 0)
    return dot(((lane == row + 13) & (row < 3)).astype(F32).astype(BF), weight)


def normal(values):
    centre = values - jnp.mean(values, -1, keepdims=True)
    scale = lax.rsqrt(jnp.mean(centre * centre, -1, keepdims=True) + EPS)
    return centre * scale, scale


def norm_back(grad, n, scale):
    return scale * (grad - jnp.mean(grad, -1, keepdims=True) - n * jnp.mean(grad * n, -1, keepdims=True))


def flat(block):
    return block.reshape(PADDED, WIDTH)


def joined(ref):
    return jnp.concatenate(
        [jnp.concatenate([ref[m * 6 + h, 0] for h in range(6)], axis=1) for m in range(2)], axis=0)


def split_into(ref, rows):
    for m in range(2):
        for h in range(6):
            ref[m * 6 + h, 0] = rows[m * 64:(m + 1) * 64, h * 128:(h + 1) * 128]


def qkv_kernel(u_ref, w_ref, e_ref, x_ref, apad):
    weight = flat(w_ref[...])

    @pl.when(pl.program_id(0) == 0)
    def _():
        more = extras(weight)
        n, scale = normal(u_ref[...].astype(F32))
        apad[...] = padded((n * more[0:1] + more[1:2]).astype(BF), e_ref[...])

    split_into(x_ref, dot(apad[...], weight).astype(BF))


def whole(shape):
    return pl.BlockSpec(shape, lambda *i: (0,) * len(shape))


VMEM_LIMIT = 56 * 2**20


def qkv_call(u, ga, spread):
    return pl.pallas_call(
        qkv_kernel,
        grid=(3,),
        out_shape=jax.ShapeDtypeStruct((UNITS, 3, 64, 128), BF),
        in_specs=[whole((ROWS, WIDTH)), pl.BlockSpec((64, 16, WIDTH), lambda p: (0, p, 0)), whole((WIDTH, PADDED))],
        out_specs=pl.BlockSpec((UNITS, 1, 64, 128), lambda p: (0, p, 0, 0)),
        scratch_shapes=[pltpu.VMEM((ROWS, PADDED), BF)],
        compiler_params=pltpu.CompilerParams(vmem_limit_bytes=VMEM_LIMIT),
    )(u, ga, spread)


def gelu_parts(f):
    t = jnp.tanh(ROOT * (f + CUBIC * f * f * f))
    return t, 0.5 * f * (1.0 + t)


def mlp_kernel(o_ref, u_ref, wo_ref, wf_ref, wp_ref, e_ref, y_ref, r_ref, f_ref, bpad):
    @pl.when(pl.program_id(0) == 0)
    def _():
        wo = flat(wo_ref[...])
        more = extras(wo)
        r = u_ref[...].astype(F32) + dot(padded(joined(o_ref), e_ref[...]), wo)
        r_ref[...] = r
        n, scale = normal(r)
        bpad[...] = padded((n * more[0:1] + more[1:2]).astype(BF), e_ref[...])
        y_ref[...] = r + more[2:3]

    f = dot(bpad[...], flat(wf_ref[...]))
    f_ref[...] = f
    y_ref[...] += dot(gelu_parts(f)[1].astype(BF), wp_ref[...])


def mlp_call(o, u, ga, gb, gc, spread):
    piece = lambda p: pl.BlockSpec((64, 16, WIDTH), p)
    return pl.pallas_call(
        mlp_kernel,
        grid=(4,),
        out_shape=[
            jax.ShapeDtypeStruct((ROWS, WIDTH), F32),
            jax.ShapeDtypeStruct((ROWS, WIDTH), F32),
            jax.ShapeDtypeStruct((ROWS, FF), F32),
        ],
        in_specs=[
            whole((UNITS, 1, 64, 128)), whole((ROWS, WIDTH)), piece(lambda k: (0, 3, 0)),
            piece(lambda k: (0, k, 0)), pl.BlockSpec((WIDTH, WIDTH), lambda k: (k, 0)), whole((WIDTH, PADDED)),
        ],
        out_specs=[whole((ROWS, WIDTH)), whole((ROWS, WIDTH)), pl.BlockSpec((ROWS, WIDTH), lambda k: (0, k))],
        scratch_shapes=[pltpu.VMEM((ROWS, PADDED), BF)],
        compiler_params=pltpu.CompilerParams(vmem_limit_bytes=VMEM_LIMIT),
    )(o, u, ga, gb, gc, spread)


def mlp_back_kernel(full, g_ref, f_ref, r_ref, wo_ref, wf_ref, wp_ref, e_ref, *refs):
    if full:
        do_ref, dr_ref, small_ref, db_ref, dc_ref, bpad, dbacc = refs
    else:
        do_ref, dr_ref, dbacc = refs
    k = pl.program_id(0)

    @pl.when(k == 0)
    def _():
        dbacc[...] = jnp.zeros_like(dbacc)
        if full:
            more = extras(flat(wo_ref[...]))
            n, scale = normal(r_ref[...])
            bpad[...] = padded((n * more[0:1] + more[1:2]).astype(BF), e_ref[...])

    dm = g_ref[...]
    f = f_ref[...]
    t, act = gelu_parts(f)
    slope = 0.5 * (1.0 + t) + 0.5 * f * (1.0 - t * t) * (ROOT * (1.0 + 3 * CUBIC * f * f))
    df = (dot(dm, wp_ref[...], NT) * slope).astype(BF)
    if full:
        dc_ref[...] = dot(act.astype(BF), dm, TN).astype(BF)
        db_ref[...] = dot(bpad[...], df, TN).astype(BF).reshape(64, 16, WIDTH)
    dbacc[...] += dot(df, flat(wf_ref[...]), NT)

    @pl.when(k == 3)
    def _():
        wo = flat(wo_ref[...])
        more = extras(wo)
        n, scale = normal(r_ref[...])
        db = unpadded(dbacc[...], e_ref[...])
        dr = dm.astype(F32) + norm_back(more[0:1] * db, n, scale)
        dr_ref[...] = dr
        do = dot(dr.astype(BF), wo, NT).astype(BF)
        split_into(do_ref, dot(do, e_ref[...], NT).astype(BF))
        if full:
            small_ref[0:1] = jnp.sum(db * n, 0, keepdims=True)
            small_ref[1:2] = jnp.sum(db, 0, keepdims=True)
            small_ref[2:3] = jnp.sum(dm.astype(F32), 0, keepdims=True)
            small_ref[3:8] = jnp.zeros((5, WIDTH), F32)


def mlp_back_call(full, g, f, r, ga, gb, gc, spread):
    piece = lambda p: pl.BlockSpec((64, 16, WIDTH), p)
    out_shape = [jax.ShapeDtypeStruct((UNITS, 1, 64, 128), BF), jax.ShapeDtypeStruct((ROWS, WIDTH), F32)]
    out_specs = [whole((UNITS, 1, 64, 128)), whole((ROWS, WIDTH))]
    scratch = [pltpu.VMEM((ROWS, PADDED), F32)]
    if full:
        out_shape += [
            jax.ShapeDtypeStruct((8, WIDTH), F32),
            jax.ShapeDtypeStruct((64, 64, WIDTH), BF),
            jax.ShapeDtypeStruct((FF, WIDTH), BF),
        ]
        out_specs += [whole((8, WIDTH)), piece(lambda k: (0, k, 0)), pl.BlockSpec((WIDTH, WIDTH), lambda k: (k, 0))]
        scratch = [pltpu.VMEM((ROWS, PADDED), BF)] + scratch
    return pl.pallas_call(
        functools.partial(mlp_back_kernel, full),
        grid=(4,),
        out_shape=out_shape,
        in_specs=[
            whole((ROWS, WIDTH)), pl.BlockSpec((ROWS, WIDTH), lambda k: (0, k)), whole((ROWS, WIDTH)),
            piece(lambda k: (0, 3, 0)), piece(lambda k: (0, k, 0)),
            pl.BlockSpec((WIDTH, WIDTH), lambda k: (k, 0)), whole((WIDTH, PADDED)),
        ],
        out_specs=out_specs,
        scratch_shapes=scratch,
        compiler_params=pltpu.CompilerParams(vmem_limit_bytes=VMEM_LIMIT),
    )(g, f, r, ga, gb, gc, spread)


def qkv_back_kernel(full, dx_ref, w_ref, u_ref, dr_ref, e_ref, *refs):
    if full:
        o_ref, small_ref, gu_ref, da_ref, gain, daacc, apad = refs
    else:
        gu_ref, gain, daacc = refs
    p = pl.program_id(0)

    @pl.when(p == 0)
    def _():
        more = extras(flat(w_ref[...]))
        gain[...] = jnp.broadcast_to(more[0:1], gain.shape)
        daacc[...] = jnp.zeros_like(daacc)
        if full:
            n, scale = normal(u_ref[...].astype(F32))
            apad[...] = padded((n * more[0:1] + more[1:2]).astype(BF), e_ref[...])

    def stored(grad, rows):
        grad = grad.reshape(64, 16, WIDTH)
        if rows is not None:
            at = lax.broadcasted_iota(jnp.int32, (16, WIDTH), 0)
            add = jnp.zeros((16, WIDTH), F32)
            for i, row in enumerate(rows):
                add = add + jnp.where(at == 13 + i, row, 0.0)
            grad = grad + add[None]
        da_ref[...] = grad.astype(BF)

    @pl.when(p < 3)
    def _():
        dx = joined(dx_ref)
        daacc[...] += dot(dx, flat(w_ref[...]), NT)
        if full:
            grad = dot(apad[...], dx, TN)

            @pl.when(p == 0)
            def _():
                stored(grad, [small_ref[i:i + 1] for i in range(3)])

            @pl.when(p > 0)
            def _():
                stored(grad, None)

    @pl.when(p == (3 if full else 2))
    def _():
        n, scale = normal(u_ref[...].astype(F32))
        da = unpadded(daacc[...], e_ref[...])
        gu_ref[...] = dr_ref[...] + norm_back(gain[0:1] * da, n, scale)
        if full:
            grad = dot(padded(joined(o_ref), e_ref[...]), dr_ref[...].astype(BF), TN)
            stored(grad, [jnp.sum(da * n, 0, keepdims=True), jnp.sum(da, 0, keepdims=True)])


def qkv_back_call(full, dx, ga, u, dr, spread, o=None, small=None):
    last = lambda p: jnp.minimum(p, 2)
    in_specs = [
        pl.BlockSpec((UNITS, 1, 64, 128), lambda p: (0, last(p), 0, 0)),
        pl.BlockSpec((64, 16, WIDTH), lambda p: (0, last(p), 0)),
        whole((ROWS, WIDTH)), whole((ROWS, WIDTH)), whole((WIDTH, PADDED)),
    ]
    args = [dx, ga, u, dr, spread]
    out_shape = [jax.ShapeDtypeStruct((ROWS, WIDTH), F32)]
    out_specs = [whole((ROWS, WIDTH))]
    scratch = [pltpu.VMEM((8, WIDTH), F32), pltpu.VMEM((ROWS, PADDED), F32)]
    if full:
        in_specs += [whole((UNITS, 1, 64, 128)), whole((8, WIDTH))]
        args += [o, small]
        out_shape += [jax.ShapeDtypeStruct((64, 64, WIDTH), BF)]
        out_specs += [pl.BlockSpec((64, 16, WIDTH), lambda p: (0, p, 0))]
        scratch += [pltpu.VMEM((ROWS, PADDED), BF)]
    return pl.pallas_call(
        functools.partial(qkv_back_kernel, full),
        grid=(4 if full else 3,),
        out_shape=out_shape, in_specs=in_specs, out_specs=out_specs, scratch_shapes=scratch,
        compiler_params=pltpu.CompilerParams(vmem_limit_bytes=VMEM_LIMIT),
    )(*args)


SEQ = 1024
QB = 256


def head_mask(rows, head):
    lane = lax.broadcasted_iota(jnp.int32, rows.shape, 1)
    return jnp.where((lane >= 64 * head) & (lane < 64 * head + 64), rows, jnp.zeros_like(rows))


def scores_of(keys, query, kpos_ref, qpos):
    raw = dot(keys, query, NT)
    return jnp.where(kpos_ref[...] <= qpos, raw, -1e30)


def attend_kernel(x_ref, kpos_ref, qpos_ref, q_ref, o_ref, lse_ref, vt):
    @pl.when(pl.program_id(0) == 0)
    def _():
        vt[...] = x_ref[2].astype(F32).T.astype(BF)

    keys = x_ref[1]
    qpos = qpos_ref[...]
    query = q_ref[0] * jnp.array(0.125, BF)
    parts, stats = [], []
    for head in range(2):
        s = scores_of(keys, head_mask(query, head), kpos_ref, qpos)
        top = jnp.max(s, 0, keepdims=True)
        e = jnp.exp(s - top)
        total = jnp.sum(e, 0, keepdims=True)
        p = (e * (1.0 / total)).astype(BF)
        parts.append(dot(vt[64 * head:64 * head + 64], p))
        stats.append(top + jnp.log(total))
    o_ref[0] = jnp.concatenate(parts, 0).T.astype(BF)
    lse_ref[...] = jnp.concatenate(stats + [jnp.zeros((6, QB), F32)], 0)


def attend_call(x, kpos, qpos):
    return pl.pallas_call(
        attend_kernel,
        grid=(SEQ // QB,),
        out_shape=[jax.ShapeDtypeStruct((1, SEQ, 128), BF), jax.ShapeDtypeStruct((8, SEQ), F32)],
        in_specs=[
            whole((3, SEQ, 128)), whole((SEQ, 1)), pl.BlockSpec((1, QB), lambda i: (0, i)),
            pl.BlockSpec((1, QB, 128), lambda i: (0, i, 0)),
        ],
        out_specs=[pl.BlockSpec((1, QB, 128), lambda i: (0, i, 0)), pl.BlockSpec((8, QB), lambda i: (0, i))],
        scratch_shapes=[pltpu.VMEM((128, SEQ), BF)],
        compiler_params=pltpu.CompilerParams(vmem_limit_bytes=VMEM_LIMIT),
    )(x, kpos, qpos, x)


def attend_back_kernel(x_ref, kpos_ref, qpos_ref, q_ref, do_ref, lse_ref, out_ref, kt, dk, dv):
    i = pl.program_id(0)

    @pl.when(i == 0)
    def _():
        kt[...] = x_ref[1].astype(F32).T.astype(BF)
        dk[...] = jnp.zeros_like(dk)
        dv[...] = jnp.zeros_like(dv)

    keys, vals = x_ref[1], x_ref[2]
    qpos = qpos_ref[...]
    query, do = q_ref[0], do_ref[0]
    parts = []
    for head in range(2):
        q_own, do_own = head_mask(query, head), head_mask(do, head)
        s = scores_of(keys, q_own * jnp.array(0.125, BF), kpos_ref, qpos)
        p = jnp.exp(s - lse_ref[head:head + 1])
        dp = dot(vals, do_own, NT)
        delta = jnp.sum(p * dp, 0, keepdims=True)
        ds = (p * (dp - delta) * 0.125).astype(BF)
        dk[...] += dot(ds, q_own)
        dv[...] += dot(p.astype(BF), do_own)
        parts.append(dot(kt[64 * head:64 * head + 64], ds))
    at = pl.ds(pl.multiple_of(i * QB, QB), QB)
    out_ref[0, at] = jnp.concatenate(parts, 0).T.astype(BF)

    @pl.when(i == SEQ // QB - 1)
    def _():
        out_ref[1] = dk[...].astype(BF)
        out_ref[2] = dv[...].astype(BF)


def attend_back_call(x, kpos, qpos, do, lse):
    return pl.pallas_call(
        attend_back_kernel,
        grid=(SEQ // QB,),
        out_shape=jax.ShapeDtypeStruct((3, SEQ, 128), BF),
        in_specs=[
            whole((3, SEQ, 128)), whole((SEQ, 1)), pl.BlockSpec((1, QB), lambda i: (0, i)),
            pl.BlockSpec((1, QB, 128), lambda i: (0, i, 0)), pl.BlockSpec((1, QB, 128), lambda i: (0, i, 0)),
            pl.BlockSpec((8, QB), lambda i: (0, i)),
        ],
        out_specs=whole((3, SEQ, 128)),
        scratch_shapes=[pltpu.VMEM((128, SEQ), BF), pltpu.VMEM((SEQ, 128), F32), pltpu.VMEM((SEQ, 128), F32)],
        compiler_params=pltpu.CompilerParams(vmem_limit_bytes=VMEM_LIMIT),
    )(x, kpos, qpos, x, do, lse)


def positions(block_order):
    index = jnp.arange(SEQ, dtype=jnp.int32)
    blocks = block_order.shape[0]
    length = SEQ // blocks
    table = jnp.arange(blocks, dtype=jnp.int32)
    chosen = jnp.sum(jnp.where((index // length)[:, None] == table[None, :], block_order[None, :], 0), axis=1)
    return chosen * length + index % length


def placed(chunk, gains, biases, fc_bias):
    wide_rows = lax.dynamic_update_slice(
        jnp.zeros((8, WIDTH), F32), jnp.concatenate([gains, biases], 0).astype(F32), (0, 12 * chunk))
    line_rows = lax.dynamic_update_slice(jnp.zeros((FF,), F32), fc_bias.astype(F32), (48 * chunk,))
    return wide_rows, line_rows.reshape(4, WIDTH)


def local(boundary, block_order, qkv_weight, out_weight, fc_weight, proj_weight, gains, biases, fc_bias):
    section = lax.axis_index("section")
    chunk = lax.axis_index("fsdp") * 16 + lax.axis_index("ctx")
    key_pos = positions(block_order)
    kpos, qpos = key_pos[:, None], key_pos[None, :]
    source = lax.broadcasted_iota(jnp.int32, (WIDTH, PADDED), 0)
    target = lax.broadcasted_iota(jnp.int32, (WIDTH, PADDED), 1)
    spread = ((target // 16 == source // 12) & (target % 16 == source % 12)).astype(BF)

    shards = (qkv_weight[0], out_weight[0], fc_weight[0], proj_weight[0]) + placed(chunk, gains[0], biases[0], fc_bias[0])

    def shaped(gathered):
        ga, gb, gc = gathered
        return ga.reshape(64, 64, WIDTH), gb.reshape(64, 64, WIDTH), gc.reshape(FF, WIDTH)

    def reduced(active, ident, grads):
        return scatter_all(active, ident, *(
            x.reshape(4, 4, 4, r, WIDTH) for x, r in zip(grads, ROWS_OF)))

    def forward(weights, u):
        ga, gb, gc = weights
        x = to_heads(qkv_call(u, ga, spread), 2)
        attended, lse = attend_call(x, kpos, qpos)
        o = from_heads(attended, UNITS, 3)
        y, r, f = mlp_call(o, u, ga, gb, gc, spread)
        return y, (u, x, lse, o, r, f)

    def backward(weights, saved, g):
        ga, gb, gc = weights
        u, x, lse, o, r, f = saved
        do, dr, *more = mlp_back_call(True, g, f, r, ga, gb, gc, spread)
        dx = from_heads(attend_back_call(x, kpos, qpos, to_heads(do, 4), lse), UNITS, 5)
        small, grad_b, grad_c = more
        gu, grad_a = qkv_back_call(True, dx, ga, u, dr, spread, o, small)
        return gu, (grad_a, grad_b, grad_c)

    held = boundary[0].reshape(ROWS, WIDTH)
    gathered = gather_all(0, 0, shards)
    first, _ = forward(shaped(gathered), held)
    gathered = gather_all(1, 6, shards, (*gathered, first))
    first, *gathered = lax.optimization_barrier((first, *gathered))
    weights = shaped(gathered)
    sent = lax.ppermute(first.astype(BF), "section", [(0, 1)])
    y, saved = forward(weights, jnp.where(section == 0, held, sent))
    back, grads = backward(weights, saved, held)
    returned = lax.ppermute(back.astype(BF), "section", [(1, 0)])
    returned, *grads = lax.optimization_barrier((returned, *grads))
    upper = reduced(1, 1, grads)
    returned, *upper = lax.optimization_barrier((returned, *upper))
    gu, grads = backward(weights, saved, jnp.where(section == 1, held, returned))
    lower = reduced(0, 7, grads)
    ra, rb, rc = (jnp.where(section == 0, low, up) for low, up in zip(lower, upper))
    ends = jnp.where(section == 0, gu, y).reshape(1, 2, 1, 64, WIDTH)
    qkv_grad = jnp.concatenate([ra[0:12], ra[16:28], ra[32:44]], 1)
    fc_grad = jnp.concatenate([rb[16 * k:16 * k + 12] for k in range(4)], 1)
    small = jnp.stack([ra[61], ra[13], ra[62], ra[12], ra[44], ra[60], ra[14], ra[15]])
    small = lax.dynamic_slice(small, (0, 12 * chunk), (8, 12))
    fc_rows = jnp.concatenate([rb[16 * k + 12] for k in range(4)])
    fc_small = lax.dynamic_slice(fc_rows, (48 * chunk,), (48,))
    return (
        ends, qkv_grad[None], ra[48:60][None], fc_grad[None], rc[None],
        small[0:2][None], small[2:8][None], fc_small[None],
    )


def solution(mesh):
    rows = P("section", ("fsdp", "ctx"), None)
    lanes = P("section", None, ("fsdp", "ctx"))
    ends = P("section", None, "fsdp", "ctx", None)
    flat_rows = P("section", ("fsdp", "ctx"))
    return jax.shard_map(
        local, mesh=mesh,
        in_specs=(ends, P(), rows, rows, rows, rows, lanes, lanes, flat_rows),
        out_specs=(ends, rows, rows, rows, rows, lanes, lanes, flat_rows),
        check_vma=False)
```

```python
import functools
import jax
import jax.numpy as jnp
from jax import lax
from jax.experimental import pallas as pl
from jax.experimental.pallas import tpu as pltpu
from jax.sharding import PartitionSpec as P

MESH = pl.DeviceIdType.MESH
ORDERS = ((0, 1, 2), (1, 2, 0), (2, 0, 1))
ROWS_OF = (64, 64, 48)


def coordinates():
    ctx = lax.axis_index("ctx")
    return (lax.axis_index("fsdp"), ctx // 4, lax.rem(ctx, 4))


def device_at(section, spot):
    return (section, spot[0], spot[1] * 4 + spot[2])


def shifted(spot, axis, by):
    moved = list(spot)
    moved[axis] = lax.rem(spot[axis] + by, 4)
    return tuple(moved)


def cut_of(rows, half):
    cut = rows // 2 // 16 * 16
    return pl.ds(0, cut) if half == 0 else pl.ds(cut, rows - cut)


def greet_neighbours(section, spot):
    barrier = pltpu.get_barrier_semaphore()
    for axis in range(3):
        for by in (1, 3):
            pl.semaphore_signal(barrier, inc=1, device_id=device_at(section, shifted(spot, axis, by)), device_id_type=MESH)
    pl.semaphore_wait(barrier, 6)


def gather_kernel(active, qkv_ref, out_ref, fc_ref, proj_ref, wide_ref, line_ref, *refs):
    @pl.when(lax.axis_index("section") == active)
    def _():
        gather_body(qkv_ref, out_ref, fc_ref, proj_ref, wide_ref, line_ref, *refs[-9:])


def gather_body(qkv_ref, out_ref, fc_ref, proj_ref, wide_ref, line_ref, ga, gb, gc,
                a_ref, b_ref, stage_ref, local_sem, send_sem, recv_sem):
    section = lax.axis_index("section")
    spot = coordinates()
    ins, outs = (a_ref, b_ref, proj_ref), (ga, gb, gc)

    none = jnp.zeros((1, 768), jnp.float32)

    def pack(into, piece, weight, rows):
        stage_ref[0:12] = weight.astype(jnp.float32)
        stage_ref[12:16] = jnp.concatenate([none if row is None else row for row in rows], 0)
        into[16 * piece:16 * piece + 16] = stage_ref[...].astype(into.dtype)

    row = [wide_ref[i:i + 1] for i in range(8)]
    pack(a_ref, 0, qkv_ref[:, 0:768], [row[3], row[0], row[2], None])
    pack(a_ref, 1, qkv_ref[:, 768:1536], [None] * 4)
    pack(a_ref, 2, qkv_ref[:, 1536:2304], [row[4], None, None, None])
    pack(a_ref, 3, out_ref[...], [row[5], row[1], row[6], row[7]])
    for k in range(4):
        pack(b_ref, k, fc_ref[:, 768 * k:768 * k + 768], [line_ref[k:k + 1], None, None, None])

    greet_neighbours(section, spot)
    own = []
    for part in range(3):
        copy = pltpu.make_async_copy(ins[part], outs[part].at[spot], local_sem.at[part])
        copy.start()
        own.append(copy)

    pending = []

    def at(part, first, second, third, rows=None):
        index = [None, None, None]
        for axis, value in zip(ORDERS[part], (first, second, third)):
            index[axis] = value
        return outs[part].at[tuple(index) if rows is None else tuple(index) + (rows,)]

    def here(part):
        return tuple(spot[axis] for axis in ORDERS[part])

    def near(value, by):
        return lax.rem(value + by, 4)

    full = pl.ds(0, 4)

    def halves(half):
        return pl.ds(2 * half, 2)

    def remote(part, axis, slot, way, src, dst):
        by = 1 if way == 0 else 3
        return pltpu.make_async_remote_copy(
            src_ref=src, dst_ref=dst, send_sem=send_sem.at[part, slot, way], recv_sem=recv_sem.at[part, slot, way],
            device_id=device_at(section, shifted(spot, ORDERS[part][axis], by)), device_id_type=MESH)

    def send(part, axis, slot, way, src, dst=None):
        copy = remote(part, axis, slot, way, src, src if dst is None else dst)
        copy.start()
        pending.append(copy)

    def came(part, axis, slot, way, ref):
        remote(part, axis, slot, way, ref, ref).wait_recv()

    BACK = (3, 1)

    def third_item(part, item, by):
        p1, p2, p3 = here(part)
        for way in (0, 1):
            send(part, 2, 4 + 2 * item, way, at(part, full, near(p2, by), p3))

    def third_pass(part, item, by):
        p1, p2, p3 = here(part)
        for way in (0, 1):
            came(part, 2, 4 + 2 * item, way, at(part, full, near(p2, by), near(p3, BACK[way])))
            send(part, 2, 5 + 2 * item, way, at(part, halves(way), near(p2, by), near(p3, BACK[way])))

    for part in range(3):
        p1, p2, p3 = here(part)
        for way in (0, 1):
            send(part, 0, 0, way, ins[part], at(part, p1, p2, p3))
    for part in range(3):
        p1, p2, p3 = here(part)
        for way in (0, 1):
            v = near(p1, BACK[way])
            came(part, 0, 0, way, at(part, v, p2, p3))
            send(part, 0, 1, way, at(part, v, p2, p3, cut_of(ROWS_OF[part], way)))
    for part in range(3):
        p1, p2, p3 = here(part)
        for way in (0, 1):
            came(part, 0, 1, way, at(part, near(p1, 2), p2, p3, cut_of(ROWS_OF[part], way)))
        own[part].wait()
        for way in (0, 1):
            send(part, 1, 2, way, at(part, full, p2, p3))
    for part in range(3):
        third_item(part, 0, 0)
    for part in range(3):
        p1, p2, p3 = here(part)
        for way in (0, 1):
            v = near(p2, BACK[way])
            came(part, 1, 2, way, at(part, full, v, p3))
            send(part, 1, 3, way, at(part, halves(way), v, p3))
    for part in range(3):
        third_item(part, 1, 3)
        third_item(part, 2, 1)
    for part in range(3):
        p1, p2, p3 = here(part)
        for way in (0, 1):
            came(part, 1, 3, way, at(part, halves(way), near(p2, 2), p3))
        third_item(part, 3, 2)
    for item, by in ((0, 0), (1, 3), (2, 1), (3, 2)):
        for part in range(3):
            third_pass(part, item, by)
    for item, by in ((0, 0), (1, 3), (2, 1), (3, 2)):
        for part in range(3):
            p1, p2, p3 = here(part)
            for way in (0, 1):
                came(part, 2, 5 + 2 * item, way, at(part, halves(way), near(p2, by), near(p3, 2)))
    for copy in pending:
        copy.wait_send()


def gather_all(active, ident, shards, held=()):
    vmem = pl.BlockSpec(memory_space=pltpu.VMEM)
    anywhere = pl.BlockSpec(memory_space=pl.ANY)
    return pl.pallas_call(
        functools.partial(gather_kernel, active),
        out_shape=[jax.ShapeDtypeStruct((4, 4, 4, r, 768), jnp.bfloat16) for r in ROWS_OF],
        in_specs=[vmem] * 6 + [anywhere] * len(held),
        out_specs=[anywhere] * 3,
        scratch_shapes=[
            pltpu.VMEM((64, 768), jnp.bfloat16),
            pltpu.VMEM((64, 768), jnp.bfloat16),
            pltpu.VMEM((16, 768), jnp.float32),
            pltpu.SemaphoreType.DMA((3,)),
            pltpu.SemaphoreType.DMA((3, 12, 2)),
            pltpu.SemaphoreType.DMA((3, 12, 2)),
        ],
        input_output_aliases={6: 0, 7: 1, 8: 2} if held else {},
        compiler_params=pltpu.CompilerParams(collective_id=ident, has_side_effects=True),
    )(*shards, *held)


def wide(ref, index):
    return ref[index].astype(jnp.float32)


def scatter_kernel(active, *refs):
    @pl.when(lax.axis_index("section") == active)
    def _():
        scatter_body(*refs)


def scatter_body(*refs):
    ins, outs = refs[:3], refs[3:6]
    box0, box1, box2 = refs[6:9], refs[9:12], refs[12:15]
    own, mid, work1, work2 = refs[15:18], refs[18:21], refs[21:24], refs[24:27]
    local_sem, send_sem, recv_sem = refs[27:30]
    section = lax.axis_index("section")
    spot = coordinates()
    greet_neighbours(section, spot)

    def here(part):
        return tuple(spot[axis] for axis in ORDERS[part])

    def near(value, by):
        return lax.rem(value + by, 4)

    def at(part, first, second, third=pl.ds(0, 4)):
        index = [None, None, None]
        for axis, value in zip(ORDERS[part], (first, second, third)):
            index[axis] = value
        return ins[part].at[tuple(index)]

    def halves(half):
        return pl.ds(2 * half, 2)

    def remote(part, axis, slot, way, src, dst):
        by = 1 if way == 0 else 3
        return pltpu.make_async_remote_copy(
            src_ref=src, dst_ref=dst, send_sem=send_sem.at[part, slot, way], recv_sem=recv_sem.at[part, slot, way],
            device_id=device_at(section, shifted(spot, ORDERS[part][axis], by)), device_id_type=MESH)

    pending = []

    def send(part, axis, slot, way, src, dst):
        copy = remote(part, axis, slot, way, src, dst)
        copy.start()
        pending.append(copy)

    def came(part, axis, slot, way, ref):
        remote(part, axis, slot, way, ref, ref).wait_recv()

    ITEMS = (2, 1, 3, 0)
    loads = {}

    def first_send(part, item):
        p1, p2, p3 = here(part)
        w = near(p2, ITEMS[item])
        for way in (0, 1):
            send(part, 0, 3 * item, way, at(part, near(p1, 2), w, halves(way)), box0[part].at[item, 0, halves(way)])
        for way in (0, 1):
            copy = pltpu.make_async_copy(
                at(part, near(p1, 1 + 2 * way), w, halves(way)), mid[part].at[item, halves(way)], local_sem.at[part, item, way])
            copy.start()
            loads[part, item, way] = copy
        copy = pltpu.make_async_copy(at(part, p1, w), own[part].at[item], local_sem.at[part, item, 2])
        copy.start()
        loads[part, item, 2] = copy
        for way in (0, 1):
            send(part, 0, 3 * item + 1, way, at(part, near(p1, 1 + 2 * way), w, halves(1 - way)),
                 box0[part].at[item, 1 + way, halves(1 - way)])

    def loop(count, body):
        def step(i, carry):
            body(i)
            return carry
        lax.fori_loop(0, count, step, 0)

    def first_middle(part, item):
        for way in (0, 1):
            got = box0[part].at[item, 0, halves(way)]
            came(part, 0, 3 * item, way, got)
            loads[part, item, way].wait()

            def body(i):
                f = box0[part]
                f[item, 0, 2 * way + i] = (wide(f, (item, 0, 2 * way + i)) + wide(mid[part], (item, 2 * way + i))).astype(f.dtype)

            loop(2, body)
            send(part, 0, 3 * item + 2, way, got, box0[part].at[item, 1 + way, halves(way)])

    def first_finish(part, item):
        box = box0[part]
        for way in (0, 1):
            came(part, 0, 3 * item + 1, way, box.at[item, 1 + way, halves(1 - way)])
            came(part, 0, 3 * item + 2, way, box.at[item, 1 + way, halves(way)])
        loads[part, item, 2].wait()

        def body(i):
            work1[part][item, i] = (
                wide(own[part], (item, i)) + wide(box, (item, 1, i)) + wide(box, (item, 2, i))).astype(box.dtype)

        loop(4, body)

    def second_far(part):
        for way in (0, 1):
            send(part, 1, 12, way, work1[part].at[0, halves(way)], box1[part].at[0, halves(way)])

    def second_raw(part):
        for way in (0, 1):
            send(part, 1, 13, way, work1[part].at[1 + way, halves(1 - way)], box1[part].at[1 + way, halves(1 - way)])

    def second_middle(part):
        for way in (0, 1):
            got = box1[part].at[0, halves(way)]
            came(part, 1, 12, way, got)

            def body(i):
                f = box1[part]
                f[0, 2 * way + i] = (wide(f, (0, 2 * way + i)) + wide(work1[part], (1 + way, 2 * way + i))).astype(f.dtype)

            loop(2, body)
            send(part, 1, 14, way, got, box1[part].at[1 + way, halves(way)])

    def second_finish(part):
        box = box1[part]
        for way in (0, 1):
            came(part, 1, 13, way, box.at[1 + way, halves(1 - way)])
            came(part, 1, 14, way, box.at[1 + way, halves(way)])

        def body(i):
            work2[part][i] = (wide(work1[part], (3, i)) + wide(box, (1, i)) + wide(box, (2, i))).astype(box.dtype)

        loop(4, body)

    def third_send(part):
        p1, p2, p3 = here(part)
        rows = ROWS_OF[part]
        for way in (0, 1):
            cut = cut_of(rows, way)
            send(part, 2, 15, way, work2[part].at[near(p3, 2), cut], box2[part].at[0, cut])
        for way in (0, 1):
            cut = cut_of(rows, 1 - way)
            send(part, 2, 16, way, work2[part].at[near(p3, 1 + 2 * way), cut], box2[part].at[1 + way, cut])

    def third_middle(part):
        p1, p2, p3 = here(part)
        rows = ROWS_OF[part]
        box = box2[part]
        for way in (0, 1):
            cut = cut_of(rows, way)
            came(part, 2, 15, way, box.at[0, cut])
            box[0, cut] = (wide(box, (0, cut)) + wide(work2[part], (near(p3, 1 + 2 * way), cut))).astype(box.dtype)
            send(part, 2, 17, way, box.at[0, cut], box.at[1 + way, cut])

    def third_finish(part):
        p1, p2, p3 = here(part)
        rows = ROWS_OF[part]
        box = box2[part]
        for way in (0, 1):
            came(part, 2, 16, way, box.at[1 + way, cut_of(rows, 1 - way)])
            came(part, 2, 17, way, box.at[1 + way, cut_of(rows, way)])
        outs[part][...] = wide(work2[part], p3) + wide(box, 1) + wide(box, 2)

    parts = range(3)
    for item in range(4):
        for part in parts:
            first_send(part, item)
    for item in range(4):
        for part in parts:
            first_middle(part, item)
    for part in parts:
        first_finish(part, 0)
        second_far(part)
    for part in parts:
        first_finish(part, 1)
        first_finish(part, 2)
        second_raw(part)
    for part in parts:
        second_middle(part)
    for part in parts:
        first_finish(part, 3)
    for part in parts:
        second_finish(part)
        third_send(part)
    for part in parts:
        third_middle(part)
    for part in parts:
        third_finish(part)
    for copy in pending:
        copy.wait_send()


def scatter_all(active, ident, a, b, c):
    scratch = []
    for shape in ((4, 3, 4), (3, 4), (3,), (4, 4), (4, 4), (4, 4), (4,)):
        scratch += [pltpu.VMEM(shape + (r, 768), jnp.bfloat16) for r in ROWS_OF]
    return pl.pallas_call(
        functools.partial(scatter_kernel, active),
        out_shape=[jax.ShapeDtypeStruct((r, 768), jnp.float32) for r in ROWS_OF],
        in_specs=[pl.BlockSpec(memory_space=pl.ANY)] * 3,
        out_specs=[pl.BlockSpec(memory_space=pltpu.VMEM)] * 3,
        scratch_shapes=scratch + [
            pltpu.SemaphoreType.DMA((3, 4, 3)),
            pltpu.SemaphoreType.DMA((3, 18, 2)),
            pltpu.SemaphoreType.DMA((3, 18, 2)),
        ],
        compiler_params=pltpu.CompilerParams(collective_id=ident, has_side_effects=True, vmem_limit_bytes=60 * 2**20),
    )(a, b, c)


EPS = 1e-05
ROOT = 0.7978845608028654
CUBIC = 0.044715
UNITS = 12
WIDTH = 768
PADDED = 1024
FF = 3072
ROWS = 128
HD = 64
BF = jnp.bfloat16
F32 = jnp.float32


def dot(left, right, over=((1,), (0,))):
    return lax.dot_general(left, right, (over, ((), ())), preferred_element_type=F32)


NT = ((1,), (1,))
TN = ((0,), (0,))


def ones_lane():
    return (lax.rem(lax.broadcasted_iota(jnp.int32, (1, PADDED), 1), 16) == 12).astype(F32)


def padded(rows, spread):
    return (dot(rows, spread) + ones_lane()).astype(BF)


def unpadded(rows, spread):
    high = rows.astype(BF)
    low = (rows - high.astype(F32)).astype(BF)
    return dot(high, spread, NT) + dot(low, spread, NT)


def extras(weight):
    lane = lax.rem(lax.broadcasted_iota(jnp.int32, (16, PADDED), 1), 16)
    row = lax.broadcasted_iota(jnp.int32, (16, PADDED), 0)
    return dot(((lane == row + 13) & (row < 3)).astype(F32).astype(BF), weight)


def normal(values):
    centre = values - jnp.mean(values, -1, keepdims=True)
    scale = lax.rsqrt(jnp.mean(centre * centre, -1, keepdims=True) + EPS)
    return centre * scale, scale


def norm_back(grad, n, scale):
    return scale * (grad - jnp.mean(grad, -1, keepdims=True) - n * jnp.mean(grad * n, -1, keepdims=True))


def flat(block):
    return block.reshape(PADDED, WIDTH)


def joined(ref):
    return jnp.concatenate(
        [jnp.concatenate([ref[m * 6 + h, 0] for h in range(6)], axis=1) for m in range(2)], axis=0)


def split_into(ref, rows):
    for m in range(2):
        for h in range(6):
            ref[m * 6 + h, 0] = rows[m * 64:(m + 1) * 64, h * 128:(h + 1) * 128]


def qkv_kernel(u_ref, w_ref, e_ref, x_ref, apad):
    weight = flat(w_ref[...])

    @pl.when(pl.program_id(0) == 0)
    def _():
        more = extras(weight)
        n, scale = normal(u_ref[...].astype(F32))
        apad[...] = padded((n * more[0:1] + more[1:2]).astype(BF), e_ref[...])

    split_into(x_ref, dot(apad[...], weight).astype(BF))


def whole(shape):
    return pl.BlockSpec(shape, lambda *i: (0,) * len(shape))


VMEM_LIMIT = 56 * 2**20


def qkv_call(u, ga, spread):
    return pl.pallas_call(
        qkv_kernel,
        grid=(3,),
        out_shape=jax.ShapeDtypeStruct((UNITS, 3, 64, 128), BF),
        in_specs=[whole((ROWS, WIDTH)), pl.BlockSpec((64, 16, WIDTH), lambda p: (0, p, 0)), whole((WIDTH, PADDED))],
        out_specs=pl.BlockSpec((UNITS, 1, 64, 128), lambda p: (0, p, 0, 0)),
        scratch_shapes=[pltpu.VMEM((ROWS, PADDED), BF)],
        compiler_params=pltpu.CompilerParams(vmem_limit_bytes=VMEM_LIMIT),
    )(u, ga, spread)


def gelu_parts(f):
    t = jnp.tanh(ROOT * (f + CUBIC * f * f * f))
    return t, 0.5 * f * (1.0 + t)


def mlp_kernel(o_ref, u_ref, wo_ref, wf_ref, wp_ref, e_ref, y_ref, r_ref, f_ref, bpad):
    @pl.when(pl.program_id(0) == 0)
    def _():
        wo = flat(wo_ref[...])
        more = extras(wo)
        r = u_ref[...].astype(F32) + dot(padded(joined(o_ref), e_ref[...]), wo)
        r_ref[...] = r
        n, scale = normal(r)
        bpad[...] = padded((n * more[0:1] + more[1:2]).astype(BF), e_ref[...])
        y_ref[...] = r + more[2:3]

    f = dot(bpad[...], flat(wf_ref[...]))
    f_ref[...] = f
    y_ref[...] += dot(gelu_parts(f)[1].astype(BF), wp_ref[...])


def mlp_call(o, u, ga, gb, gc, spread):
    piece = lambda p: pl.BlockSpec((64, 16, WIDTH), p)
    return pl.pallas_call(
        mlp_kernel,
        grid=(4,),
        out_shape=[
            jax.ShapeDtypeStruct((ROWS, WIDTH), F32),
            jax.ShapeDtypeStruct((ROWS, WIDTH), F32),
            jax.ShapeDtypeStruct((ROWS, FF), F32),
        ],
        in_specs=[
            whole((UNITS, 1, 64, 128)), whole((ROWS, WIDTH)), piece(lambda k: (0, 3, 0)),
            piece(lambda k: (0, k, 0)), pl.BlockSpec((WIDTH, WIDTH), lambda k: (k, 0)), whole((WIDTH, PADDED)),
        ],
        out_specs=[whole((ROWS, WIDTH)), whole((ROWS, WIDTH)), pl.BlockSpec((ROWS, WIDTH), lambda k: (0, k))],
        scratch_shapes=[pltpu.VMEM((ROWS, PADDED), BF)],
        compiler_params=pltpu.CompilerParams(vmem_limit_bytes=VMEM_LIMIT),
    )(o, u, ga, gb, gc, spread)


def mlp_back_kernel(full, g_ref, f_ref, r_ref, wo_ref, wf_ref, wp_ref, e_ref, *refs):
    if full:
        do_ref, dr_ref, small_ref, db_ref, dc_ref, bpad, dbacc = refs
    else:
        do_ref, dr_ref, dbacc = refs
    k = pl.program_id(0)

    @pl.when(k == 0)
    def _():
        dbacc[...] = jnp.zeros_like(dbacc)
        if full:
            more = extras(flat(wo_ref[...]))
            n, scale = normal(r_ref[...])
            bpad[...] = padded((n * more[0:1] + more[1:2]).astype(BF), e_ref[...])

    dm = g_ref[...]
    f = f_ref[...]
    t, act = gelu_parts(f)
    slope = 0.5 * (1.0 + t) + 0.5 * f * (1.0 - t * t) * (ROOT * (1.0 + 3 * CUBIC * f * f))
    df = (dot(dm, wp_ref[...], NT) * slope).astype(BF)
    if full:
        dc_ref[...] = dot(act.astype(BF), dm, TN).astype(BF)
        db_ref[...] = dot(bpad[...], df, TN).astype(BF).reshape(64, 16, WIDTH)
    dbacc[...] += dot(df, flat(wf_ref[...]), NT)

    @pl.when(k == 3)
    def _():
        wo = flat(wo_ref[...])
        more = extras(wo)
        n, scale = normal(r_ref[...])
        db = unpadded(dbacc[...], e_ref[...])
        dr = dm.astype(F32) + norm_back(more[0:1] * db, n, scale)
        dr_ref[...] = dr
        do = dot(dr.astype(BF), wo, NT).astype(BF)
        split_into(do_ref, dot(do, e_ref[...], NT).astype(BF))
        if full:
            small_ref[0:1] = jnp.sum(db * n, 0, keepdims=True)
            small_ref[1:2] = jnp.sum(db, 0, keepdims=True)
            small_ref[2:3] = jnp.sum(dm.astype(F32), 0, keepdims=True)
            small_ref[3:8] = jnp.zeros((5, WIDTH), F32)


def mlp_back_call(full, g, f, r, ga, gb, gc, spread):
    piece = lambda p: pl.BlockSpec((64, 16, WIDTH), p)
    out_shape = [jax.ShapeDtypeStruct((UNITS, 1, 64, 128), BF), jax.ShapeDtypeStruct((ROWS, WIDTH), F32)]
    out_specs = [whole((UNITS, 1, 64, 128)), whole((ROWS, WIDTH))]
    scratch = [pltpu.VMEM((ROWS, PADDED), F32)]
    if full:
        out_shape += [
            jax.ShapeDtypeStruct((8, WIDTH), F32),
            jax.ShapeDtypeStruct((64, 64, WIDTH), BF),
            jax.ShapeDtypeStruct((FF, WIDTH), BF),
        ]
        out_specs += [whole((8, WIDTH)), piece(lambda k: (0, k, 0)), pl.BlockSpec((WIDTH, WIDTH), lambda k: (k, 0))]
        scratch = [pltpu.VMEM((ROWS, PADDED), BF)] + scratch
    return pl.pallas_call(
        functools.partial(mlp_back_kernel, full),
        grid=(4,),
        out_shape=out_shape,
        in_specs=[
            whole((ROWS, WIDTH)), pl.BlockSpec((ROWS, WIDTH), lambda k: (0, k)), whole((ROWS, WIDTH)),
            piece(lambda k: (0, 3, 0)), piece(lambda k: (0, k, 0)),
            pl.BlockSpec((WIDTH, WIDTH), lambda k: (k, 0)), whole((WIDTH, PADDED)),
        ],
        out_specs=out_specs,
        scratch_shapes=scratch,
        compiler_params=pltpu.CompilerParams(vmem_limit_bytes=VMEM_LIMIT),
    )(g, f, r, ga, gb, gc, spread)


def qkv_back_kernel(full, dx_ref, w_ref, u_ref, dr_ref, e_ref, *refs):
    if full:
        o_ref, small_ref, gu_ref, da_ref, gain, daacc, apad = refs
    else:
        gu_ref, gain, daacc = refs
    p = pl.program_id(0)

    @pl.when(p == 0)
    def _():
        more = extras(flat(w_ref[...]))
        gain[...] = jnp.broadcast_to(more[0:1], gain.shape)
        daacc[...] = jnp.zeros_like(daacc)
        if full:
            n, scale = normal(u_ref[...].astype(F32))
            apad[...] = padded((n * more[0:1] + more[1:2]).astype(BF), e_ref[...])

    def stored(grad, rows):
        grad = grad.reshape(64, 16, WIDTH)
        if rows is not None:
            at = lax.broadcasted_iota(jnp.int32, (16, WIDTH), 0)
            add = jnp.zeros((16, WIDTH), F32)
            for i, row in enumerate(rows):
                add = add + jnp.where(at == 13 + i, row, 0.0)
            grad = grad + add[None]
        da_ref[...] = grad.astype(BF)

    @pl.when(p < 3)
    def _():
        dx = joined(dx_ref)
        daacc[...] += dot(dx, flat(w_ref[...]), NT)
        if full:
            grad = dot(apad[...], dx, TN)

            @pl.when(p == 0)
            def _():
                stored(grad, [small_ref[i:i + 1] for i in range(3)])

            @pl.when(p > 0)
            def _():
                stored(grad, None)

    @pl.when(p == (3 if full else 2))
    def _():
        n, scale = normal(u_ref[...].astype(F32))
        da = unpadded(daacc[...], e_ref[...])
        gu_ref[...] = dr_ref[...] + norm_back(gain[0:1] * da, n, scale)
        if full:
            grad = dot(padded(joined(o_ref), e_ref[...]), dr_ref[...].astype(BF), TN)
            stored(grad, [jnp.sum(da * n, 0, keepdims=True), jnp.sum(da, 0, keepdims=True)])


def qkv_back_call(full, dx, ga, u, dr, spread, o=None, small=None):
    last = lambda p: jnp.minimum(p, 2)
    in_specs = [
        pl.BlockSpec((UNITS, 1, 64, 128), lambda p: (0, last(p), 0, 0)),
        pl.BlockSpec((64, 16, WIDTH), lambda p: (0, last(p), 0)),
        whole((ROWS, WIDTH)), whole((ROWS, WIDTH)), whole((WIDTH, PADDED)),
    ]
    args = [dx, ga, u, dr, spread]
    out_shape = [jax.ShapeDtypeStruct((ROWS, WIDTH), F32)]
    out_specs = [whole((ROWS, WIDTH))]
    scratch = [pltpu.VMEM((8, WIDTH), F32), pltpu.VMEM((ROWS, PADDED), F32)]
    if full:
        in_specs += [whole((UNITS, 1, 64, 128)), whole((8, WIDTH))]
        args += [o, small]
        out_shape += [jax.ShapeDtypeStruct((64, 64, WIDTH), BF)]
        out_specs += [pl.BlockSpec((64, 16, WIDTH), lambda p: (0, p, 0))]
        scratch += [pltpu.VMEM((ROWS, PADDED), BF)]
    return pl.pallas_call(
        functools.partial(qkv_back_kernel, full),
        grid=(4 if full else 3,),
        out_shape=out_shape, in_specs=in_specs, out_specs=out_specs, scratch_shapes=scratch,
        compiler_params=pltpu.CompilerParams(vmem_limit_bytes=VMEM_LIMIT),
    )(*args)


SEQ = 1024
QB = 256


def head_mask(rows, head):
    lane = lax.broadcasted_iota(jnp.int32, rows.shape, 1)
    return jnp.where((lane >= 64 * head) & (lane < 64 * head + 64), rows, jnp.zeros_like(rows))


def rows_at(index, size):
    return pl.ds(pl.multiple_of(index * size, size), size)


class Exchange:
    def __init__(self, out_sems, back_sems, local_sem):
        self.place = (lax.axis_index("section"), lax.axis_index("fsdp"))
        self.me = lax.axis_index("ctx")
        self.out_sems, self.back_sems, self.local_sem = out_sems, back_sems, local_sem

    def device(self, ctx):
        return self.place + (ctx,)

    def greet(self, extra=()):
        barrier = pltpu.get_barrier_semaphore()
        for unit in range(16):
            @pl.when((self.me != unit) & ((self.me < UNITS) | (unit < UNITS)))
            def _():
                pl.semaphore_signal(barrier, inc=1, device_id=self.device(unit), device_id_type=MESH)
        for device in extra:
            pl.semaphore_signal(barrier, inc=1, device_id=device, device_id_type=MESH)
        more = len(extra)

        @pl.when(self.me < UNITS)
        def _():
            pl.semaphore_wait(barrier, 15 + more)

        @pl.when(self.me >= UNITS)
        def _():
            pl.semaphore_wait(barrier, UNITS + more)

    def outward(self, unit, sender, src, dst):
        send, recv = self.out_sems
        return pltpu.make_async_remote_copy(
            src_ref=src.at[unit], dst_ref=dst.at[:, rows_at(sender, 64)], send_sem=send.at[unit], recv_sem=recv.at[sender],
            device_id=self.device(unit), device_id_type=MESH)

    def spread_out(self, src, dst):
        for unit in range(UNITS):
            @pl.when(self.me != unit)
            def _():
                self.outward(unit, self.me, src, dst).start()

        @pl.when(self.me < UNITS)
        def _():
            pltpu.make_async_copy(src.at[self.me], dst.at[:, rows_at(self.me, 64)], self.local_sem.at[0]).start()

    def spread_in(self, src, dst):
        pltpu.make_async_copy(src.at[self.me], dst.at[:, rows_at(self.me, 64)], self.local_sem.at[0]).wait()
        for sender in range(16):
            @pl.when(self.me != sender)
            def _():
                self.outward(0, sender, src, dst).wait_recv()

    def spread_done(self, src, dst):
        for unit in range(UNITS):
            @pl.when(self.me != unit)
            def _():
                self.outward(unit, self.me, src, dst).wait_send()

    def inward(self, kind, unit, target, src, dst):
        send, recv = self.back_sems
        return pltpu.make_async_remote_copy(
            src_ref=src.at[:, rows_at(target, 64)], dst_ref=dst.at[unit], send_sem=send.at[kind, target],
            recv_sem=recv.at[kind, unit], device_id=self.device(target), device_id_type=MESH)

    def own_back(self, kind, src, dst):
        return pltpu.make_async_copy(src.at[:, rows_at(self.me, 64)], dst.at[self.me], self.local_sem.at[1 + kind])

    def return_to(self, kind, target, src, dst):
        @pl.when(self.me != target)
        def _():
            self.inward(kind, self.me, target, src, dst).start()

        @pl.when(self.me == target)
        def _():
            self.own_back(kind, src, dst).start()

    def return_in(self, kind, src, dst):
        for unit in range(UNITS):
            @pl.when(self.me != unit)
            def _():
                self.inward(kind, unit, 0, src, dst).wait_recv()

        @pl.when(self.me < UNITS)
        def _():
            self.own_back(kind, src, dst).wait()
            for target in range(16):
                @pl.when(self.me != target)
                def _():
                    self.inward(kind, self.me, target, src, dst).wait_send()


def loop(count, body):
    def step(i, carry):
        body(i)
        return carry
    lax.fori_loop(0, count, step, 0)


def attend_kernel(x_ref, kpos_ref, qpos_ref, y_ref, lse_ref, o_ref, att, vt, bias,
                  send_a, recv_a, send_b, recv_b, local_sem):
    ex = Exchange((send_a, recv_a), (send_b, recv_b), local_sem)
    ex.greet()
    ex.spread_out(x_ref, y_ref)

    @pl.when(ex.me < UNITS)
    def _():
        ex.spread_in(x_ref, y_ref)
        vt[...] = y_ref[2].astype(F32).T.astype(BF)

    def block(i):
        rows = rows_at(i, QB)
        bias[...] = jnp.where(kpos_ref[...] <= qpos_ref[:, rows], 0.0, -1e30)
        query = y_ref[0, rows] * jnp.array(0.125, BF)
        parts, stats = [], []
        for head in range(2):
            s = dot(y_ref[1], head_mask(query, head), NT) + bias[...]
            top = jnp.max(s, 0, keepdims=True)
            e = jnp.exp(s - top)
            total = jnp.sum(e, 0, keepdims=True)
            parts.append(dot(vt[64 * head:64 * head + 64], e.astype(BF)) * (1.0 / total))
            stats.append(top + jnp.log(total))
        att[0, rows] = jnp.concatenate(parts, 0).T.astype(BF)
        lse_ref[:, rows] = jnp.concatenate(stats + [jnp.zeros((6, QB), F32)], 0)
        for j in range(4):
            ex.return_to(0, 4 * i + j, att, o_ref)

    @pl.when(ex.me < UNITS)
    def _():
        loop(SEQ // QB, block)

    ex.return_in(0, att, o_ref)
    ex.spread_done(x_ref, y_ref)


def exchange_sems(kinds):
    return [
        pltpu.SemaphoreType.DMA((UNITS,)), pltpu.SemaphoreType.DMA((16,)),
        pltpu.SemaphoreType.DMA((kinds, 16)), pltpu.SemaphoreType.DMA((kinds, UNITS)),
        pltpu.SemaphoreType.DMA((1 + kinds,)),
    ]


VM = pl.BlockSpec(memory_space=pltpu.VMEM)
HBM = pl.BlockSpec(memory_space=pl.ANY)


def attend_call(x, kpos, qpos):
    return pl.pallas_call(
        attend_kernel,
        out_shape=[
            jax.ShapeDtypeStruct((3, SEQ, 128), BF), jax.ShapeDtypeStruct((8, SEQ), F32),
            jax.ShapeDtypeStruct((UNITS, 1, 64, 128), BF),
        ],
        in_specs=[VM] * 3,
        out_specs=[VM] * 3,
        scratch_shapes=[
            pltpu.VMEM((1, SEQ, 128), BF), pltpu.VMEM((128, SEQ), BF), pltpu.VMEM((SEQ, QB), F32),
        ] + exchange_sems(1),
        compiler_params=pltpu.CompilerParams(collective_id=2, has_side_effects=True, vmem_limit_bytes=VMEM_LIMIT),
    )(x, kpos, qpos)


def attend_back_kernel(do_ref, x_ref, lse_ref, kpos_ref, qpos_ref, dx_ref, dob, dq, dkv, kt, dk, dv, bias,
                       send_a, recv_a, send_b, recv_b, local_sem):
    ex = Exchange((send_a, recv_a), (send_b, recv_b), local_sem)
    dx_q, dx_kv = dx_ref.at[:, pl.ds(0, 1)], dx_ref.at[:, pl.ds(1, 2)]
    ex.greet()
    ex.spread_out(do_ref, dob)

    @pl.when(ex.me < UNITS)
    def _():
        kt[...] = x_ref[1].astype(F32).T.astype(BF)
        dk[...] = jnp.zeros_like(dk)
        dv[...] = jnp.zeros_like(dv)
        ex.spread_in(do_ref, dob)

    def block(i):
        rows = rows_at(i, QB)
        bias[...] = jnp.where(kpos_ref[...] <= qpos_ref[:, rows], 0.0, -1e30)
        query, do = x_ref[0, rows], dob[0, rows]
        parts = []
        for head in range(2):
            q_own, do_own = head_mask(query, head), head_mask(do, head)
            s = dot(x_ref[1], q_own * jnp.array(0.125, BF), NT) + bias[...]
            p = jnp.exp(s - lse_ref[head:head + 1, rows])
            dv[...] += dot(p.astype(BF), do_own)
            dp = dot(x_ref[2], do_own, NT)
            delta = jnp.sum(p * dp, 0, keepdims=True)
            ds = (p * (dp - delta) * 0.125).astype(BF)
            dk[...] += dot(ds, q_own)
            parts.append(dot(kt[64 * head:64 * head + 64], ds))
        dq[0, rows] = jnp.concatenate(parts, 0).T.astype(BF)
        for j in range(4):
            ex.return_to(0, 4 * i + j, dq, dx_q)

    @pl.when(ex.me < UNITS)
    def _():
        loop(SEQ // QB, block)
        dkv[0] = dk[...].astype(BF)
        dkv[1] = dv[...].astype(BF)
        for target in range(16):
            ex.return_to(1, target, dkv, dx_kv)

    ex.return_in(0, dq, dx_q)
    ex.return_in(1, dkv, dx_kv)
    ex.spread_done(do_ref, dob)


def attend_back_call(do, x, lse, kpos, qpos):
    return pl.pallas_call(
        attend_back_kernel,
        out_shape=jax.ShapeDtypeStruct((UNITS, 3, 64, 128), BF),
        in_specs=[VM] * 5,
        out_specs=VM,
        scratch_shapes=[
            pltpu.VMEM((1, SEQ, 128), BF), pltpu.VMEM((1, SEQ, 128), BF), pltpu.VMEM((2, SEQ, 128), BF),
            pltpu.VMEM((128, SEQ), BF), pltpu.VMEM((SEQ, 128), F32), pltpu.VMEM((SEQ, 128), F32),
            pltpu.VMEM((SEQ, QB), F32),
        ] + exchange_sems(2),
        compiler_params=pltpu.CompilerParams(collective_id=3, has_side_effects=True, vmem_limit_bytes=VMEM_LIMIT),
    )(do, x, lse, kpos, qpos)


def positions(block_order):
    index = jnp.arange(SEQ, dtype=jnp.int32)
    blocks = block_order.shape[0]
    length = SEQ // blocks
    table = jnp.arange(blocks, dtype=jnp.int32)
    chosen = jnp.sum(jnp.where((index // length)[:, None] == table[None, :], block_order[None, :], 0), axis=1)
    return chosen * length + index % length


def placed(chunk, gains, biases, fc_bias):
    wide_rows = lax.dynamic_update_slice(
        jnp.zeros((8, WIDTH), F32), jnp.concatenate([gains, biases], 0).astype(F32), (0, 12 * chunk))
    line_rows = lax.dynamic_update_slice(jnp.zeros((FF,), F32), fc_bias.astype(F32), (48 * chunk,))
    return wide_rows, line_rows.reshape(4, WIDTH)


def local(boundary, block_order, qkv_weight, out_weight, fc_weight, proj_weight, gains, biases, fc_bias):
    section = lax.axis_index("section")
    chunk = lax.axis_index("fsdp") * 16 + lax.axis_index("ctx")
    key_pos = positions(block_order)
    kpos, qpos = key_pos[:, None], key_pos[None, :]
    source = lax.broadcasted_iota(jnp.int32, (WIDTH, PADDED), 0)
    target = lax.broadcasted_iota(jnp.int32, (WIDTH, PADDED), 1)
    spread = ((target // 16 == source // 12) & (target % 16 == source % 12)).astype(BF)

    shards = (qkv_weight[0], out_weight[0], fc_weight[0], proj_weight[0]) + placed(chunk, gains[0], biases[0], fc_bias[0])

    def shaped(gathered):
        ga, gb, gc = gathered
        return ga.reshape(64, 64, WIDTH), gb.reshape(64, 64, WIDTH), gc.reshape(FF, WIDTH)

    def reduced(active, ident, grads):
        return scatter_all(active, ident, *(
            x.reshape(4, 4, 4, r, WIDTH) for x, r in zip(grads, ROWS_OF)))

    def forward(weights, u):
        ga, gb, gc = weights
        x, lse, o = attend_call(qkv_call(u, ga, spread), kpos, qpos)
        y, r, f = mlp_call(o, u, ga, gb, gc, spread)
        return y, (u, x, lse, o, r, f)

    def backward(weights, saved, g):
        ga, gb, gc = weights
        u, x, lse, o, r, f = saved
        do, dr, *more = mlp_back_call(True, g, f, r, ga, gb, gc, spread)
        dx = attend_back_call(do, x, lse, kpos, qpos)
        small, grad_b, grad_c = more
        gu, grad_a = qkv_back_call(True, dx, ga, u, dr, spread, o, small)
        return gu, (grad_a, grad_b, grad_c)

    held = boundary[0].reshape(ROWS, WIDTH)
    gathered = gather_all(0, 0, shards)
    first, _ = forward(shaped(gathered), held)
    gathered = gather_all(1, 6, shards, (*gathered, first))
    first, *gathered = lax.optimization_barrier((first, *gathered))
    weights = shaped(gathered)
    sent = lax.ppermute(first.astype(BF), "section", [(0, 1)])
    y, saved = forward(weights, jnp.where(section == 0, held, sent))
    back, grads = backward(weights, saved, held)
    returned = lax.ppermute(back.astype(BF), "section", [(1, 0)])
    returned, *grads = lax.optimization_barrier((returned, *grads))
    upper = reduced(1, 1, grads)
    returned, *upper = lax.optimization_barrier((returned, *upper))
    gu, grads = backward(weights, saved, jnp.where(section == 1, held, returned))
    lower = reduced(0, 7, grads)
    ra, rb, rc = (jnp.where(section == 0, low, up) for low, up in zip(lower, upper))
    ends = jnp.where(section == 0, gu, y).reshape(1, 2, 1, 64, WIDTH)
    qkv_grad = jnp.concatenate([ra[0:12], ra[16:28], ra[32:44]], 1)
    fc_grad = jnp.concatenate([rb[16 * k:16 * k + 12] for k in range(4)], 1)
    small = jnp.stack([ra[61], ra[13], ra[62], ra[12], ra[44], ra[60], ra[14], ra[15]])
    small = lax.dynamic_slice(small, (0, 12 * chunk), (8, 12))
    fc_rows = jnp.concatenate([rb[16 * k + 12] for k in range(4)])
    fc_small = lax.dynamic_slice(fc_rows, (48 * chunk,), (48,))
    return (
        ends, qkv_grad[None], ra[48:60][None], fc_grad[None], rc[None],
        small[0:2][None], small[2:8][None], fc_small[None],
    )


def solution(mesh):
    rows = P("section", ("fsdp", "ctx"), None)
    lanes = P("section", None, ("fsdp", "ctx"))
    ends = P("section", None, "fsdp", "ctx", None)
    flat_rows = P("section", ("fsdp", "ctx"))
    return jax.shard_map(
        local, mesh=mesh,
        in_specs=(ends, P(), rows, rows, rows, rows, lanes, lanes, flat_rows),
        out_specs=(ends, rows, rows, rows, rows, lanes, lanes, flat_rows),
        check_vma=False)
```

```python
import functools
import jax
import jax.numpy as jnp
from jax import lax
from jax.experimental import pallas as pl
from jax.experimental.pallas import tpu as pltpu
from jax.sharding import PartitionSpec as P

MESH = pl.DeviceIdType.MESH
ORDERS = ((0, 1, 2), (1, 2, 0), (2, 0, 1))
ROWS_OF = (64, 64, 48)


def coordinates():
    ctx = lax.axis_index("ctx")
    return (lax.axis_index("fsdp"), ctx // 4, lax.rem(ctx, 4))


def device_at(section, spot):
    return (section, spot[0], spot[1] * 4 + spot[2])


def shifted(spot, axis, by):
    moved = list(spot)
    moved[axis] = lax.rem(spot[axis] + by, 4)
    return tuple(moved)


def cut_of(rows, half):
    cut = rows // 2 // 16 * 16
    return pl.ds(0, cut) if half == 0 else pl.ds(cut, rows - cut)


def greet_neighbours(section, spot, partner=False):
    barrier = pltpu.get_barrier_semaphore()
    for axis in range(3):
        for by in (1, 3):
            pl.semaphore_signal(barrier, inc=1, device_id=device_at(section, shifted(spot, axis, by)), device_id_type=MESH)
    if partner:
        pl.semaphore_signal(barrier, inc=1, device_id=device_at(1 - section, spot), device_id_type=MESH)
    pl.semaphore_wait(barrier, 7 if partner else 6)


def gather_kernel(active, qkv_ref, out_ref, fc_ref, proj_ref, wide_ref, line_ref, *refs):
    @pl.when(lax.axis_index("section") == active)
    def _():
        gather_body(active, qkv_ref, out_ref, fc_ref, proj_ref, wide_ref, line_ref, *refs[-10:])

    if active == 0:
        @pl.when(lax.axis_index("section") == 1)
        def _():
            barrier = pltpu.get_barrier_semaphore()
            pl.semaphore_signal(barrier, inc=1, device_id=device_at(0, coordinates()), device_id_type=MESH)
            pl.semaphore_wait(barrier, 1)
            pl.semaphore_wait(refs[-1], 1)


def gather_body(active, qkv_ref, out_ref, fc_ref, proj_ref, wide_ref, line_ref, ga, gb, gc,
                a_ref, b_ref, stage_ref, local_sem, send_sem, recv_sem, turn_sem):
    section = lax.axis_index("section")
    spot = coordinates()
    ins, outs = (a_ref, b_ref, proj_ref), (ga, gb, gc)

    none = jnp.zeros((1, 768), jnp.float32)

    def pack(into, piece, weight, rows):
        stage_ref[0:12] = weight.astype(jnp.float32)
        stage_ref[12:16] = jnp.concatenate([none if row is None else row for row in rows], 0)
        into[16 * piece:16 * piece + 16] = stage_ref[...].astype(into.dtype)

    row = [wide_ref[i:i + 1] for i in range(8)]
    pack(a_ref, 0, qkv_ref[:, 0:768], [row[3], row[0], row[2], None])
    pack(a_ref, 1, qkv_ref[:, 768:1536], [None] * 4)
    pack(a_ref, 2, qkv_ref[:, 1536:2304], [row[4], None, None, None])
    pack(a_ref, 3, out_ref[...], [row[5], row[1], row[6], row[7]])
    for k in range(4):
        pack(b_ref, k, fc_ref[:, 768 * k:768 * k + 768], [line_ref[k:k + 1], None, None, None])

    greet_neighbours(section, spot, active == 0)
    own = []
    for part in range(3):
        copy = pltpu.make_async_copy(ins[part], outs[part].at[spot], local_sem.at[part])
        copy.start()
        own.append(copy)

    pending = []

    def at(part, first, second, third, rows=None):
        index = [None, None, None]
        for axis, value in zip(ORDERS[part], (first, second, third)):
            index[axis] = value
        return outs[part].at[tuple(index) if rows is None else tuple(index) + (rows,)]

    def here(part):
        return tuple(spot[axis] for axis in ORDERS[part])

    def near(value, by):
        return lax.rem(value + by, 4)

    full = pl.ds(0, 4)

    def halves(half):
        return pl.ds(2 * half, 2)

    def remote(part, axis, slot, way, src, dst):
        by = 1 if way == 0 else 3
        return pltpu.make_async_remote_copy(
            src_ref=src, dst_ref=dst, send_sem=send_sem.at[part, slot, way], recv_sem=recv_sem.at[part, slot, way],
            device_id=device_at(section, shifted(spot, ORDERS[part][axis], by)), device_id_type=MESH)

    def send(part, axis, slot, way, src, dst=None):
        copy = remote(part, axis, slot, way, src, src if dst is None else dst)
        copy.start()
        pending.append(copy)

    def came(part, axis, slot, way, ref):
        remote(part, axis, slot, way, ref, ref).wait_recv()

    BACK = (3, 1)

    def third_item(part, item, by):
        p1, p2, p3 = here(part)
        for way in (0, 1):
            send(part, 2, 4 + 2 * item, way, at(part, full, near(p2, by), p3))

    def third_pass(part, item, by):
        p1, p2, p3 = here(part)
        for way in (0, 1):
            came(part, 2, 4 + 2 * item, way, at(part, full, near(p2, by), near(p3, BACK[way])))
            send(part, 2, 5 + 2 * item, way, at(part, halves(way), near(p2, by), near(p3, BACK[way])))

    for part in range(3):
        p1, p2, p3 = here(part)
        for way in (0, 1):
            send(part, 0, 0, way, ins[part], at(part, p1, p2, p3))
    for part in range(3):
        p1, p2, p3 = here(part)
        for way in (0, 1):
            v = near(p1, BACK[way])
            came(part, 0, 0, way, at(part, v, p2, p3))
            send(part, 0, 1, way, at(part, v, p2, p3, cut_of(ROWS_OF[part], way)))
    for part in range(3):
        p1, p2, p3 = here(part)
        for way in (0, 1):
            came(part, 0, 1, way, at(part, near(p1, 2), p2, p3, cut_of(ROWS_OF[part], way)))
        own[part].wait()
        for way in (0, 1):
            send(part, 1, 2, way, at(part, full, p2, p3))
    for part in range(3):
        third_item(part, 0, 0)
    for part in range(3):
        p1, p2, p3 = here(part)
        for way in (0, 1):
            v = near(p2, BACK[way])
            came(part, 1, 2, way, at(part, full, v, p3))
            send(part, 1, 3, way, at(part, halves(way), v, p3))
    for part in range(3):
        third_item(part, 1, 3)
        third_item(part, 2, 1)
    for part in range(3):
        p1, p2, p3 = here(part)
        for way in (0, 1):
            came(part, 1, 3, way, at(part, halves(way), near(p2, 2), p3))
        third_item(part, 3, 2)
    if active == 0:
        pl.semaphore_signal(turn_sem, inc=1, device_id=device_at(1, spot), device_id_type=MESH)
    for item, by in ((0, 0), (1, 3), (2, 1), (3, 2)):
        for part in range(3):
            third_pass(part, item, by)
    for item, by in ((0, 0), (1, 3), (2, 1), (3, 2)):
        for part in range(3):
            p1, p2, p3 = here(part)
            for way in (0, 1):
                came(part, 2, 5 + 2 * item, way, at(part, halves(way), near(p2, by), near(p3, 2)))
    for copy in pending:
        copy.wait_send()


def gather_all(active, ident, shards, held=()):
    vmem = pl.BlockSpec(memory_space=pltpu.VMEM)
    anywhere = pl.BlockSpec(memory_space=pl.ANY)
    return pl.pallas_call(
        functools.partial(gather_kernel, active),
        out_shape=[jax.ShapeDtypeStruct((4, 4, 4, r, 768), jnp.bfloat16) for r in ROWS_OF],
        in_specs=[vmem] * 6 + [anywhere] * len(held),
        out_specs=[anywhere] * 3,
        scratch_shapes=[
            pltpu.VMEM((64, 768), jnp.bfloat16),
            pltpu.VMEM((64, 768), jnp.bfloat16),
            pltpu.VMEM((16, 768), jnp.float32),
            pltpu.SemaphoreType.DMA((3,)),
            pltpu.SemaphoreType.DMA((3, 12, 2)),
            pltpu.SemaphoreType.DMA((3, 12, 2)),
            pltpu.SemaphoreType.REGULAR,
        ],
        input_output_aliases={6: 0, 7: 1, 8: 2} if held else {},
        compiler_params=pltpu.CompilerParams(collective_id=ident, has_side_effects=True),
    )(*shards, *held)


def wide(ref, index):
    return ref[index].astype(jnp.float32)


def scatter_kernel(active, *refs):
    @pl.when(lax.axis_index("section") == active)
    def _():
        scatter_body(*refs)


def scatter_body(*refs):
    ins, outs = refs[:3], refs[3:6]
    box0, box1, box2 = refs[6:9], refs[9:12], refs[12:15]
    own, mid, work1, work2 = refs[15:18], refs[18:21], refs[21:24], refs[24:27]
    local_sem, send_sem, recv_sem = refs[27:30]
    section = lax.axis_index("section")
    spot = coordinates()
    greet_neighbours(section, spot)

    def here(part):
        return tuple(spot[axis] for axis in ORDERS[part])

    def near(value, by):
        return lax.rem(value + by, 4)

    def at(part, first, second, third=pl.ds(0, 4)):
        index = [None, None, None]
        for axis, value in zip(ORDERS[part], (first, second, third)):
            index[axis] = value
        return ins[part].at[tuple(index)]

    def halves(half):
        return pl.ds(2 * half, 2)

    def remote(part, axis, slot, way, src, dst):
        by = 1 if way == 0 else 3
        return pltpu.make_async_remote_copy(
            src_ref=src, dst_ref=dst, send_sem=send_sem.at[part, slot, way], recv_sem=recv_sem.at[part, slot, way],
            device_id=device_at(section, shifted(spot, ORDERS[part][axis], by)), device_id_type=MESH)

    pending = []

    def send(part, axis, slot, way, src, dst):
        copy = remote(part, axis, slot, way, src, dst)
        copy.start()
        pending.append(copy)

    def came(part, axis, slot, way, ref):
        remote(part, axis, slot, way, ref, ref).wait_recv()

    ITEMS = (2, 1, 3, 0)
    loads = {}

    def first_send(part, item):
        p1, p2, p3 = here(part)
        w = near(p2, ITEMS[item])
        for way in (0, 1):
            send(part, 0, 3 * item, way, at(part, near(p1, 2), w, halves(way)), box0[part].at[item, 0, halves(way)])
        for way in (0, 1):
            copy = pltpu.make_async_copy(
                at(part, near(p1, 1 + 2 * way), w, halves(way)), mid[part].at[item, halves(way)], local_sem.at[part, item, way])
            copy.start()
            loads[part, item, way] = copy
        copy = pltpu.make_async_copy(at(part, p1, w), own[part].at[item], local_sem.at[part, item, 2])
        copy.start()
        loads[part, item, 2] = copy
        for way in (0, 1):
            send(part, 0, 3 * item + 1, way, at(part, near(p1, 1 + 2 * way), w, halves(1 - way)),
                 box0[part].at[item, 1 + way, halves(1 - way)])

    def loop(count, body):
        def step(i, carry):
            body(i)
            return carry
        lax.fori_loop(0, count, step, 0)

    def first_middle(part, item):
        for way in (0, 1):
            got = box0[part].at[item, 0, halves(way)]
            came(part, 0, 3 * item, way, got)
            loads[part, item, way].wait()

            def body(i):
                f = box0[part]
                f[item, 0, 2 * way + i] = (wide(f, (item, 0, 2 * way + i)) + wide(mid[part], (item, 2 * way + i))).astype(f.dtype)

            loop(2, body)
            send(part, 0, 3 * item + 2, way, got, box0[part].at[item, 1 + way, halves(way)])

    def first_finish(part, item):
        box = box0[part]
        for way in (0, 1):
            came(part, 0, 3 * item + 1, way, box.at[item, 1 + way, halves(1 - way)])
            came(part, 0, 3 * item + 2, way, box.at[item, 1 + way, halves(way)])
        loads[part, item, 2].wait()

        def body(i):
            work1[part][item, i] = (
                wide(own[part], (item, i)) + wide(box, (item, 1, i)) + wide(box, (item, 2, i))).astype(box.dtype)

        loop(4, body)

    def second_far(part):
        for way in (0, 1):
            send(part, 1, 12, way, work1[part].at[0, halves(way)], box1[part].at[0, halves(way)])

    def second_raw(part):
        for way in (0, 1):
            send(part, 1, 13, way, work1[part].at[1 + way, halves(1 - way)], box1[part].at[1 + way, halves(1 - way)])

    def second_middle(part):
        for way in (0, 1):
            got = box1[part].at[0, halves(way)]
            came(part, 1, 12, way, got)

            def body(i):
                f = box1[part]
                f[0, 2 * way + i] = (wide(f, (0, 2 * way + i)) + wide(work1[part], (1 + way, 2 * way + i))).astype(f.dtype)

            loop(2, body)
            send(part, 1, 14, way, got, box1[part].at[1 + way, halves(way)])

    def second_finish(part):
        box = box1[part]
        for way in (0, 1):
            came(part, 1, 13, way, box.at[1 + way, halves(1 - way)])
            came(part, 1, 14, way, box.at[1 + way, halves(way)])

        def body(i):
            work2[part][i] = (wide(work1[part], (3, i)) + wide(box, (1, i)) + wide(box, (2, i))).astype(box.dtype)

        loop(4, body)

    def third_send(part):
        p1, p2, p3 = here(part)
        rows = ROWS_OF[part]
        for way in (0, 1):
            cut = cut_of(rows, way)
            send(part, 2, 15, way, work2[part].at[near(p3, 2), cut], box2[part].at[0, cut])
        for way in (0, 1):
            cut = cut_of(rows, 1 - way)
            send(part, 2, 16, way, work2[part].at[near(p3, 1 + 2 * way), cut], box2[part].at[1 + way, cut])

    def third_middle(part):
        p1, p2, p3 = here(part)
        rows = ROWS_OF[part]
        box = box2[part]
        for way in (0, 1):
            cut = cut_of(rows, way)
            came(part, 2, 15, way, box.at[0, cut])
            box[0, cut] = (wide(box, (0, cut)) + wide(work2[part], (near(p3, 1 + 2 * way), cut))).astype(box.dtype)
            send(part, 2, 17, way, box.at[0, cut], box.at[1 + way, cut])

    def third_finish(part):
        p1, p2, p3 = here(part)
        rows = ROWS_OF[part]
        box = box2[part]
        for way in (0, 1):
            came(part, 2, 16, way, box.at[1 + way, cut_of(rows, 1 - way)])
            came(part, 2, 17, way, box.at[1 + way, cut_of(rows, way)])
        outs[part][...] = wide(work2[part], p3) + wide(box, 1) + wide(box, 2)

    parts = range(3)
    for item in range(4):
        for part in parts:
            first_send(part, item)
    for item in range(4):
        for part in parts:
            first_middle(part, item)
    for part in parts:
        first_finish(part, 0)
        second_far(part)
    for part in parts:
        first_finish(part, 1)
        first_finish(part, 2)
        second_raw(part)
    for part in parts:
        second_middle(part)
    for part in parts:
        first_finish(part, 3)
    for part in parts:
        second_finish(part)
        third_send(part)
    for part in parts:
        third_middle(part)
    for part in parts:
        third_finish(part)
    for copy in pending:
        copy.wait_send()


def scatter_all(active, ident, a, b, c):
    scratch = []
    for shape in ((4, 3, 4), (3, 4), (3,), (4, 4), (4, 4), (4, 4), (4,)):
        scratch += [pltpu.VMEM(shape + (r, 768), jnp.bfloat16) for r in ROWS_OF]
    return pl.pallas_call(
        functools.partial(scatter_kernel, active),
        out_shape=[jax.ShapeDtypeStruct((r, 768), jnp.float32) for r in ROWS_OF],
        in_specs=[pl.BlockSpec(memory_space=pl.ANY)] * 3,
        out_specs=[pl.BlockSpec(memory_space=pltpu.VMEM)] * 3,
        scratch_shapes=scratch + [
            pltpu.SemaphoreType.DMA((3, 4, 3)),
            pltpu.SemaphoreType.DMA((3, 18, 2)),
            pltpu.SemaphoreType.DMA((3, 18, 2)),
        ],
        compiler_params=pltpu.CompilerParams(collective_id=ident, has_side_effects=True, vmem_limit_bytes=60 * 2**20),
    )(a, b, c)


EPS = 1e-05
ROOT = 0.7978845608028654
CUBIC = 0.044715
UNITS = 12
WIDTH = 768
PADDED = 1024
FF = 3072
ROWS = 128
HD = 64
BF = jnp.bfloat16
F32 = jnp.float32


def dot(left, right, over=((1,), (0,))):
    return lax.dot_general(left, right, (over, ((), ())), preferred_element_type=F32)


NT = ((1,), (1,))
TN = ((0,), (0,))


def ones_lane():
    return (lax.rem(lax.broadcasted_iota(jnp.int32, (1, PADDED), 1), 16) == 12).astype(F32)


def padded(rows, spread):
    return (dot(rows, spread) + ones_lane()).astype(BF)


def unpadded(rows, spread):
    high = rows.astype(BF)
    low = (rows - high.astype(F32)).astype(BF)
    return dot(high, spread, NT) + dot(low, spread, NT)


def extras(weight):
    lane = lax.rem(lax.broadcasted_iota(jnp.int32, (16, PADDED), 1), 16)
    row = lax.broadcasted_iota(jnp.int32, (16, PADDED), 0)
    return dot(((lane == row + 13) & (row < 3)).astype(F32).astype(BF), weight)


def normal(values):
    centre = values - jnp.mean(values, -1, keepdims=True)
    scale = lax.rsqrt(jnp.mean(centre * centre, -1, keepdims=True) + EPS)
    return centre * scale, scale


def norm_back(grad, n, scale):
    return scale * (grad - jnp.mean(grad, -1, keepdims=True) - n * jnp.mean(grad * n, -1, keepdims=True))


def flat(block):
    return block.reshape(PADDED, WIDTH)


def joined(ref, kind=0):
    return jnp.concatenate(
        [jnp.concatenate([ref[m * 6 + h, kind] for h in range(6)], axis=1) for m in range(2)], axis=0)


def split_into(ref, rows, kind=0):
    for m in range(2):
        for h in range(6):
            ref[m * 6 + h, kind] = rows[m * 64:(m + 1) * 64, h * 128:(h + 1) * 128]


def whole(shape):
    return pl.BlockSpec(shape, lambda *i: (0,) * len(shape))


VMEM_LIMIT = 60 * 2**20


def gelu_parts(f):
    t = jnp.tanh(ROOT * (f + CUBIC * f * f * f))
    return t, 0.5 * f * (1.0 + t)


SEQ = 1024
QB = 256


def head_mask(rows, head):
    lane = lax.broadcasted_iota(jnp.int32, rows.shape, 1)
    return jnp.where((lane >= 64 * head) & (lane < 64 * head + 64), rows, jnp.zeros_like(rows))


def rows_at(index, size):
    return pl.ds(pl.multiple_of(index * size, size), size)


class Exchange:
    def __init__(self, out_sems, back_sems, local_sem):
        self.place = (lax.axis_index("section"), lax.axis_index("fsdp"))
        self.me = lax.axis_index("ctx")
        self.out_sems, self.back_sems, self.local_sem = out_sems, back_sems, local_sem

    def device(self, ctx):
        return self.place + (ctx,)

    def greet(self):
        barrier = pltpu.get_barrier_semaphore()
        for unit in range(16):
            @pl.when((self.me != unit) & ((self.me < UNITS) | (unit < UNITS)))
            def _():
                pl.semaphore_signal(barrier, inc=1, device_id=self.device(unit), device_id_type=MESH)

    def greeted(self):
        barrier = pltpu.get_barrier_semaphore()

        @pl.when(self.me < UNITS)
        def _():
            pl.semaphore_wait(barrier, 15)

        @pl.when(self.me >= UNITS)
        def _():
            pl.semaphore_wait(barrier, UNITS)

    def outward(self, kind, unit, sender, src, dst):
        send, recv = self.out_sems
        return pltpu.make_async_remote_copy(
            src_ref=src.at[unit, kind], dst_ref=dst.at[kind, rows_at(sender, 64)], send_sem=send.at[kind, unit],
            recv_sem=recv.at[kind, sender], device_id=self.device(unit), device_id_type=MESH)

    def own_out(self, kind, src, dst):
        return pltpu.make_async_copy(src.at[self.me, kind], dst.at[kind, rows_at(self.me, 64)], self.local_sem.at[kind])

    def spread_out(self, kind, src, dst):
        for unit in range(UNITS):
            @pl.when(self.me != unit)
            def _():
                self.outward(kind, unit, self.me, src, dst).start()

        @pl.when(self.me < UNITS)
        def _():
            self.own_out(kind, src, dst).start()

    def spread_in(self, kind, src, dst):
        self.own_out(kind, src, dst).wait()
        for sender in range(16):
            @pl.when(self.me != sender)
            def _():
                self.outward(kind, 0, sender, src, dst).wait_recv()

    def spread_done(self, kind, src, dst):
        for unit in range(UNITS):
            @pl.when(self.me != unit)
            def _():
                self.outward(kind, unit, self.me, src, dst).wait_send()

    def inward(self, kind, unit, target, src, dst):
        send, recv = self.back_sems
        return pltpu.make_async_remote_copy(
            src_ref=src.at[kind, rows_at(target, 64)], dst_ref=dst.at[unit, kind], send_sem=send.at[kind, target],
            recv_sem=recv.at[kind, unit], device_id=self.device(target), device_id_type=MESH)

    def own_back(self, kind, src, dst):
        return pltpu.make_async_copy(
            src.at[kind, rows_at(self.me, 64)], dst.at[self.me, kind], self.local_sem.at[3 + kind])

    def return_to(self, kind, target, src, dst):
        @pl.when(self.me != target)
        def _():
            self.inward(kind, self.me, target, src, dst).start()

        @pl.when(self.me == target)
        def _():
            self.own_back(kind, src, dst).start()

    def return_in(self, kind, src, dst):
        for unit in range(UNITS):
            @pl.when(self.me != unit)
            def _():
                self.inward(kind, unit, 0, src, dst).wait_recv()

        @pl.when(self.me < UNITS)
        def _():
            self.own_back(kind, src, dst).wait()

    def return_done(self, kind, src, dst):
        @pl.when(self.me < UNITS)
        def _():
            for target in range(16):
                @pl.when(self.me != target)
                def _():
                    self.inward(kind, self.me, target, src, dst).wait_send()


def exchange_sems(out, back):
    return [
        pltpu.SemaphoreType.DMA((out, UNITS)), pltpu.SemaphoreType.DMA((out, 16)),
        pltpu.SemaphoreType.DMA((back, 16)), pltpu.SemaphoreType.DMA((back, UNITS)),
        pltpu.SemaphoreType.DMA((6,)),
    ]


def loop(count, body):
    def step(i, carry):
        body(i)
        return carry
    lax.fori_loop(0, count, step, 0)


def masked(bias, kpos_ref, qpos_ref, rows):
    bias[...] = jnp.where(kpos_ref[...] <= qpos_ref[:, rows], 0.0, -1e30)


def attend(ex, x_ref, kpos_ref, qpos_ref, lse_ref, o_ref, att, vt, bias):
    def block(i):
        rows = rows_at(i, QB)
        masked(bias, kpos_ref, qpos_ref, rows)
        query = x_ref[0, rows] * jnp.array(0.125, BF)
        parts, stats = [], []
        for head in range(2):
            s = dot(x_ref[1], head_mask(query, head), NT) + bias[...]
            top = jnp.max(s, 0, keepdims=True)
            e = jnp.exp(s - top)
            total = jnp.sum(e, 0, keepdims=True)
            parts.append(dot(vt[64 * head:64 * head + 64], e.astype(BF)) * (1.0 / total))
            stats.append(top + jnp.log(total))
        att[0, rows] = jnp.concatenate(parts, 0).T.astype(BF)
        lse_ref[:, rows] = jnp.concatenate(stats + [jnp.zeros((6, QB), F32)], 0)
        for j in range(4):
            ex.return_to(0, 4 * i + j, att, o_ref)

    loop(SEQ // QB, block)


def attend_back(ex, do_ref, x_ref, kpos_ref, qpos_ref, lse_ref, dx_ref, dqkv, kt, dk, dv, bias):
    def block(i):
        rows = rows_at(i, QB)
        masked(bias, kpos_ref, qpos_ref, rows)
        query, do = x_ref[0, rows], do_ref[0, rows]
        parts = []
        for head in range(2):
            q_own, do_own = head_mask(query, head), head_mask(do, head)
            s = dot(x_ref[1], q_own * jnp.array(0.125, BF), NT) + bias[...]
            p = jnp.exp(s - lse_ref[head:head + 1, rows])
            dv[...] += dot(p.astype(BF), do_own)
            dp = dot(x_ref[2], do_own, NT)
            delta = jnp.sum(p * dp, 0, keepdims=True)
            ds = (p * (dp - delta) * 0.125).astype(BF)
            dk[...] += dot(ds, q_own)
            parts.append(dot(kt[64 * head:64 * head + 64], ds))
        dqkv[0, rows] = jnp.concatenate(parts, 0).T.astype(BF)
        for j in range(4):
            ex.return_to(0, 4 * i + j, dqkv, dx_ref)

    loop(SEQ // QB, block)
    for kind, total in ((1, dk), (2, dv)):
        dqkv[kind] = total[...].astype(BF)
        for target in range(16):
            ex.return_to(kind, target, dqkv, dx_ref)


def forward_kernel(active, u_ref, w_ref, wf_ref, wp_ref, e_ref, kpos_ref, qpos_ref,
                   x_ref, lse_ref, o_ref, y_ref, r_ref, f_ref,
                   qkv, landed, heads, apad, bpad, att, vt, bias, *sems):
    step = pl.program_id(0)
    ex = Exchange(sems[0:2], sems[2:4], sems[4])
    mine = lax.axis_index("section") == active

    @pl.when((step == 0) & mine)
    def _():
        ex.greet()

    @pl.when(step == 0)
    def _():
        more = extras(flat(w_ref[...]))
        n, scale = normal(u_ref[...].astype(F32))
        apad[...] = padded((n * more[0:1] + more[1:2]).astype(BF), e_ref[...])

    for kind in range(3):
        @pl.when(step == kind)
        def _():
            split_into(qkv, dot(apad[...], flat(w_ref[...])).astype(BF), kind)

            @pl.when(mine)
            def _():
                if kind == 0:
                    ex.greeted()
                ex.spread_out(kind, qkv, landed)

    @pl.when((step == 2) & mine)
    def _():
        @pl.when(ex.me < UNITS)
        def _():
            for kind in range(3):
                ex.spread_in(kind, qkv, landed)
            vt[...] = landed[2].astype(F32).T.astype(BF)
            attend(ex, landed, kpos_ref, qpos_ref, lse_ref, heads, att, vt, bias)

        ex.return_in(0, att, heads)
        for kind in range(3):
            ex.spread_done(kind, qkv, landed)
        ex.return_done(0, att, heads)
        x_ref[...] = landed[...]
        o_ref[...] = heads[...]

    @pl.when(step == 3)
    def _():
        wo = flat(w_ref[...])
        more = extras(wo)
        r = u_ref[...].astype(F32) + dot(padded(joined(heads), e_ref[...]), wo)
        r_ref[...] = r
        n, scale = normal(r)
        bpad[...] = padded((n * more[0:1] + more[1:2]).astype(BF), e_ref[...])
        y_ref[...] = r + more[2:3]

    @pl.when(step >= 3)
    def _():
        f = dot(bpad[...], flat(wf_ref[...]))
        f_ref[...] = f
        y_ref[...] += dot(gelu_parts(f)[1].astype(BF), wp_ref[...])


def piece(index):
    return pl.BlockSpec((64, 16, WIDTH), index)


def forward_call(active, ident, u, weights, spread, kpos, qpos):
    ga, gb, gc = weights
    later = lambda s: jnp.maximum(s - 3, 0)
    return pl.pallas_call(
        functools.partial(forward_kernel, active),
        grid=(7,),
        out_shape=[
            jax.ShapeDtypeStruct((3, SEQ, 128), BF), jax.ShapeDtypeStruct((8, SEQ), F32),
            jax.ShapeDtypeStruct((UNITS, 1, 64, 128), BF), jax.ShapeDtypeStruct((ROWS, WIDTH), F32),
            jax.ShapeDtypeStruct((ROWS, WIDTH), F32), jax.ShapeDtypeStruct((ROWS, FF), F32),
        ],
        in_specs=[
            whole((ROWS, WIDTH)), piece(lambda s: (0, jnp.minimum(s, 3), 0)), piece(lambda s: (0, later(s), 0)),
            pl.BlockSpec((WIDTH, WIDTH), lambda s: (later(s), 0)), whole((WIDTH, PADDED)),
            whole((SEQ, 1)), whole((1, SEQ)),
        ],
        out_specs=[
            whole((3, SEQ, 128)), whole((8, SEQ)), whole((UNITS, 1, 64, 128)), whole((ROWS, WIDTH)),
            whole((ROWS, WIDTH)), pl.BlockSpec((ROWS, WIDTH), lambda s: (0, later(s))),
        ],
        scratch_shapes=[
            pltpu.VMEM((UNITS, 3, 64, 128), BF), pltpu.VMEM((3, SEQ, 128), BF), pltpu.VMEM((UNITS, 1, 64, 128), BF),
            pltpu.VMEM((ROWS, PADDED), BF), pltpu.VMEM((ROWS, PADDED), BF), pltpu.VMEM((1, SEQ, 128), BF),
            pltpu.VMEM((128, SEQ), BF), pltpu.VMEM((SEQ, QB), F32),
        ] + exchange_sems(3, 1),
        compiler_params=pltpu.CompilerParams(collective_id=ident, has_side_effects=True, vmem_limit_bytes=VMEM_LIMIT),
    )(u, ga, gb, gc, spread, kpos, qpos)


def backward_kernel(active, g_ref, f_ref, r_ref, u_ref, o_ref, x_ref, lse_ref, kpos_ref, qpos_ref, e_ref,
                    w_ref, wf_ref, wp_ref, gu_ref, da_ref, db_ref, dc_ref,
                    pad, acc, dr, small, gain, sent, landed, dqkv, dx, kt, dk, dv, bias, *sems):
    step = pl.program_id(0)
    ex = Exchange(sems[0:2], sems[2:4], sems[4])
    mine = lax.axis_index("section") == active

    @pl.when((step == 0) & mine)
    def _():
        ex.greet()

    @pl.when(step == 0)
    def _():
        acc[...] = jnp.zeros_like(acc)
        more = extras(flat(w_ref[...]))
        n, scale = normal(r_ref[...])
        pad[...] = padded((n * more[0:1] + more[1:2]).astype(BF), e_ref[...])

    @pl.when(step < 4)
    def _():
        dm = g_ref[...]
        f = f_ref[...]
        t, act = gelu_parts(f)
        slope = 0.5 * (1.0 + t) + 0.5 * f * (1.0 - t * t) * (ROOT * (1.0 + 3 * CUBIC * f * f))
        df = (dot(dm, wp_ref[...], NT) * slope).astype(BF)
        dc_ref[...] = dot(act.astype(BF), dm, TN).astype(BF)
        db_ref[...] = dot(pad[...], df, TN).astype(BF).reshape(64, 16, WIDTH)
        acc[...] += dot(df, flat(wf_ref[...]), NT)

    @pl.when(step == 3)
    def _():
        dm = g_ref[...].astype(F32)
        wo = flat(w_ref[...])
        more = extras(wo)
        n, scale = normal(r_ref[...])
        db = unpadded(acc[...], e_ref[...])
        dr[...] = dm + norm_back(more[0:1] * db, n, scale)
        do = dot(dr[...].astype(BF), wo, NT).astype(BF)
        split_into(sent, dot(do, e_ref[...], NT).astype(BF))
        small[0:1] = jnp.sum(db * n, 0, keepdims=True)
        small[1:2] = jnp.sum(db, 0, keepdims=True)
        small[2:3] = jnp.sum(dm, 0, keepdims=True)

    @pl.when((step == 3) & mine)
    def _():
        ex.greeted()
        ex.spread_out(0, sent, landed)

        @pl.when(ex.me < UNITS)
        def _():
            kt[...] = x_ref[1].astype(F32).T.astype(BF)
            dk[...] = jnp.zeros_like(dk)
            dv[...] = jnp.zeros_like(dv)
            ex.spread_in(0, sent, landed)
            attend_back(ex, landed, x_ref, kpos_ref, qpos_ref, lse_ref, dx, dqkv, kt, dk, dv, bias)

        for kind in range(3):
            ex.return_in(kind, dqkv, dx)
        ex.spread_done(0, sent, landed)
        for kind in range(3):
            ex.return_done(kind, dqkv, dx)

    def stored(grad, rows):
        grad = grad.reshape(64, 16, WIDTH)
        if rows is not None:
            at = lax.broadcasted_iota(jnp.int32, (16, WIDTH), 0)
            add = jnp.zeros((16, WIDTH), F32)
            for i, row in enumerate(rows):
                add = add + jnp.where(at == 13 + i, row, 0.0)
            grad = grad + add[None]
        da_ref[...] = grad.astype(BF)

    @pl.when(step == 4)
    def _():
        more = extras(flat(w_ref[...]))
        gain[...] = jnp.broadcast_to(more[0:1], gain.shape)
        n, scale = normal(u_ref[...].astype(F32))
        pad[...] = padded((n * more[0:1] + more[1:2]).astype(BF), e_ref[...])

    for kind in range(3):
        @pl.when(step == 4 + kind)
        def _():
            grad = joined(dx, kind)
            back = dot(grad, flat(w_ref[...]), NT)
            if kind == 0:
                acc[...] = back
            else:
                acc[...] += back
            stored(dot(pad[...], grad, TN), [small[i:i + 1] for i in range(3)] if kind == 0 else None)

    @pl.when(step == 7)
    def _():
        n, scale = normal(u_ref[...].astype(F32))
        da = unpadded(acc[...], e_ref[...])
        gu_ref[...] = dr[...] + norm_back(gain[0:1] * da, n, scale)
        grad = dot(padded(joined(o_ref), e_ref[...]), dr[...].astype(BF), TN)
        stored(grad, [jnp.sum(da * n, 0, keepdims=True), jnp.sum(da, 0, keepdims=True)])


def backward_call(active, ident, saved, g, weights, spread, kpos, qpos):
    u, x, lse, o, r, f = saved
    ga, gb, gc = weights
    early = lambda s: jnp.minimum(s, 3)
    late = lambda s: jnp.maximum(s - 4, 0)
    return pl.pallas_call(
        functools.partial(backward_kernel, active),
        grid=(8,),
        out_shape=[
            jax.ShapeDtypeStruct((ROWS, WIDTH), F32), jax.ShapeDtypeStruct((64, 64, WIDTH), BF),
            jax.ShapeDtypeStruct((64, 64, WIDTH), BF), jax.ShapeDtypeStruct((FF, WIDTH), BF),
        ],
        in_specs=[
            whole((ROWS, WIDTH)), pl.BlockSpec((ROWS, WIDTH), lambda s: (0, early(s))), whole((ROWS, WIDTH)),
            whole((ROWS, WIDTH)), whole((UNITS, 1, 64, 128)), whole((3, SEQ, 128)), whole((8, SEQ)),
            whole((SEQ, 1)), whole((1, SEQ)), whole((WIDTH, PADDED)),
            piece(lambda s: (0, jnp.where(s < 4, 3, jnp.minimum(s - 4, 2)), 0)),
            piece(lambda s: (0, early(s), 0)), pl.BlockSpec((WIDTH, WIDTH), lambda s: (early(s), 0)),
        ],
        out_specs=[
            whole((ROWS, WIDTH)), piece(lambda s: (0, late(s), 0)), piece(lambda s: (0, early(s), 0)),
            pl.BlockSpec((WIDTH, WIDTH), lambda s: (early(s), 0)),
        ],
        scratch_shapes=[
            pltpu.VMEM((ROWS, PADDED), BF), pltpu.VMEM((ROWS, PADDED), F32), pltpu.VMEM((ROWS, WIDTH), F32),
            pltpu.VMEM((8, WIDTH), F32), pltpu.VMEM((8, WIDTH), F32),
            pltpu.VMEM((UNITS, 1, 64, 128), BF), pltpu.VMEM((1, SEQ, 128), BF), pltpu.VMEM((3, SEQ, 128), BF),
            pltpu.VMEM((UNITS, 3, 64, 128), BF), pltpu.VMEM((128, SEQ), BF), pltpu.VMEM((SEQ, 128), F32),
            pltpu.VMEM((SEQ, 128), F32), pltpu.VMEM((SEQ, QB), F32),
        ] + exchange_sems(1, 3),
        compiler_params=pltpu.CompilerParams(collective_id=ident, has_side_effects=True, vmem_limit_bytes=VMEM_LIMIT),
    )(g, f, r, u, o, x, lse, kpos, qpos, spread, ga, gb, gc)


def positions(block_order):
    index = jnp.arange(SEQ, dtype=jnp.int32)
    blocks = block_order.shape[0]
    length = SEQ // blocks
    table = jnp.arange(blocks, dtype=jnp.int32)
    chosen = jnp.sum(jnp.where((index // length)[:, None] == table[None, :], block_order[None, :], 0), axis=1)
    return chosen * length + index % length


def placed(chunk, gains, biases, fc_bias):
    wide_rows = lax.dynamic_update_slice(
        jnp.zeros((8, WIDTH), F32), jnp.concatenate([gains, biases], 0).astype(F32), (0, 12 * chunk))
    line_rows = lax.dynamic_update_slice(jnp.zeros((FF,), F32), fc_bias.astype(F32), (48 * chunk,))
    return wide_rows, line_rows.reshape(4, WIDTH)


def local(boundary, block_order, qkv_weight, out_weight, fc_weight, proj_weight, gains, biases, fc_bias):
    section = lax.axis_index("section")
    chunk = lax.axis_index("fsdp") * 16 + lax.axis_index("ctx")
    key_pos = positions(block_order)
    kpos, qpos = key_pos[:, None], key_pos[None, :]
    source = lax.broadcasted_iota(jnp.int32, (WIDTH, PADDED), 0)
    target = lax.broadcasted_iota(jnp.int32, (WIDTH, PADDED), 1)
    spread = ((target // 16 == source // 12) & (target % 16 == source % 12)).astype(BF)

    shards = (qkv_weight[0], out_weight[0], fc_weight[0], proj_weight[0]) + placed(chunk, gains[0], biases[0], fc_bias[0])

    def shaped(gathered):
        ga, gb, gc = gathered
        return ga.reshape(64, 64, WIDTH), gb.reshape(64, 64, WIDTH), gc.reshape(FF, WIDTH)

    def reduced(active, ident, grads):
        return scatter_all(active, ident, *(
            x.reshape(4, 4, 4, r, WIDTH) for x, r in zip(grads, ROWS_OF)))

    def forward(active, ident, weights, u):
        x, lse, o, y, r, f = forward_call(active, ident, u, weights, spread, kpos, qpos)
        return y, (u, x, lse, o, r, f)

    held = boundary[0].reshape(ROWS, WIDTH)
    gathered = gather_all(0, 0, shards)
    first, saved_lower = forward(0, 2, shaped(gathered), held)
    gathered = gather_all(1, 6, shards, (*gathered, first))
    first, *gathered = lax.optimization_barrier((first, *gathered))
    weights = shaped(gathered)
    sent = lax.ppermute(first.astype(BF), "section", [(0, 1)])
    y, saved_upper = forward(1, 3, weights, sent)
    back, *grads = backward_call(1, 4, saved_upper, held, weights, spread, kpos, qpos)
    returned = lax.ppermute(back.astype(BF), "section", [(1, 0)])
    returned, *grads = lax.optimization_barrier((returned, *grads))
    upper = reduced(1, 1, grads)
    returned, *upper = lax.optimization_barrier((returned, *upper))
    gu, *grads = backward_call(0, 5, saved_lower, returned, weights, spread, kpos, qpos)
    lower = reduced(0, 7, grads)
    ra, rb, rc = (jnp.where(section == 0, low, up) for low, up in zip(lower, upper))
    ends = jnp.where(section == 0, gu, y).reshape(1, 2, 1, 64, WIDTH)
    qkv_grad = jnp.concatenate([ra[0:12], ra[16:28], ra[32:44]], 1)
    fc_grad = jnp.concatenate([rb[16 * k:16 * k + 12] for k in range(4)], 1)
    small = jnp.stack([ra[61], ra[13], ra[62], ra[12], ra[44], ra[60], ra[14], ra[15]])
    small = lax.dynamic_slice(small, (0, 12 * chunk), (8, 12))
    fc_rows = jnp.concatenate([rb[16 * k + 12] for k in range(4)])
    fc_small = lax.dynamic_slice(fc_rows, (48 * chunk,), (48,))
    return (
        ends, qkv_grad[None], ra[48:60][None], fc_grad[None], rc[None],
        small[0:2][None], small[2:8][None], fc_small[None],
    )


def solution(mesh):
    rows = P("section", ("fsdp", "ctx"), None)
    lanes = P("section", None, ("fsdp", "ctx"))
    ends = P("section", None, "fsdp", "ctx", None)
    flat_rows = P("section", ("fsdp", "ctx"))
    return jax.shard_map(
        local, mesh=mesh,
        in_specs=(ends, P(), rows, rows, rows, rows, lanes, lanes, flat_rows),
        out_specs=(ends, rows, rows, rows, rows, lanes, lanes, flat_rows),
        check_vma=False)
```

```python
import functools
import jax
import jax.numpy as jnp
from jax import lax
from jax.experimental import pallas as pl
from jax.experimental.pallas import tpu as pltpu
from jax.sharding import PartitionSpec as P

MESH = pl.DeviceIdType.MESH
ORDERS = ((0, 1, 2), (1, 2, 0), (2, 0, 1))
ROWS_OF = (64, 64, 48)


def coordinates():
    ctx = lax.axis_index("ctx")
    return (lax.axis_index("fsdp"), ctx // 4, lax.rem(ctx, 4))


def device_at(section, spot):
    return (section, spot[0], spot[1] * 4 + spot[2])


def shifted(spot, axis, by):
    moved = list(spot)
    moved[axis] = lax.rem(spot[axis] + by, 4)
    return tuple(moved)


def cut_of(rows, half):
    cut = rows // 2 // 16 * 16
    return pl.ds(0, cut) if half == 0 else pl.ds(cut, rows - cut)


def greet_neighbours(section, spot, partner=False):
    barrier = pltpu.get_barrier_semaphore()
    for axis in range(3):
        for by in (1, 3):
            pl.semaphore_signal(barrier, inc=1, device_id=device_at(section, shifted(spot, axis, by)), device_id_type=MESH)
    if partner:
        pl.semaphore_signal(barrier, inc=1, device_id=device_at(1 - section, spot), device_id_type=MESH)
    pl.semaphore_wait(barrier, 7 if partner else 6)


def spread_rows(ref):
    source = lax.broadcasted_iota(jnp.int32, ref.shape, 0)
    target = lax.broadcasted_iota(jnp.int32, ref.shape, 1)
    lane = lax.rem(target, 16)
    ref[...] = ((source == 12 * (target // 16) + lane) & (lane < 12)).astype(jnp.float32).astype(ref.dtype)


def gather_kernel(active, qkv_ref, out_ref, fc_ref, proj_ref, wide_ref, line_ref, *refs):
    spread_ref = None
    if active == 0:
        spread_ref = refs[3]
        refs = refs[:3] + refs[4:]
    else:
        refs = refs[-10:]

    @pl.when(lax.axis_index("section") == active)
    def _():
        gather_body(active, spread_ref, qkv_ref, out_ref, fc_ref, proj_ref, wide_ref, line_ref, *refs)

    if active == 0:
        @pl.when(lax.axis_index("section") == 1)
        def _():
            barrier = pltpu.get_barrier_semaphore()
            pl.semaphore_signal(barrier, inc=1, device_id=device_at(0, coordinates()), device_id_type=MESH)
            spread_rows(spread_ref)
            pl.semaphore_wait(barrier, 1)
            pl.semaphore_wait(refs[-1], 1)


def gather_body(active, spread_ref, qkv_ref, out_ref, fc_ref, proj_ref, wide_ref, line_ref, ga, gb, gc,
                a_ref, b_ref, stage_ref, local_sem, send_sem, recv_sem, turn_sem):
    section = lax.axis_index("section")
    spot = coordinates()
    ins, outs = (a_ref, b_ref, proj_ref), (ga, gb, gc)

    none = jnp.zeros((1, 768), jnp.float32)

    def pack(into, piece, weight, rows):
        stage_ref[0:12] = weight.astype(jnp.float32)
        stage_ref[12:16] = jnp.concatenate([none if row is None else row for row in rows], 0)
        into[16 * piece:16 * piece + 16] = stage_ref[...].astype(into.dtype)

    row = [wide_ref[i:i + 1] for i in range(8)]
    pack(a_ref, 0, qkv_ref[:, 0:768], [row[3], row[0], row[2], None])
    pack(a_ref, 1, qkv_ref[:, 768:1536], [None] * 4)
    pack(a_ref, 2, qkv_ref[:, 1536:2304], [row[4], None, None, None])
    pack(a_ref, 3, out_ref[...], [row[5], row[1], row[6], row[7]])
    for k in range(4):
        pack(b_ref, k, fc_ref[:, 768 * k:768 * k + 768], [line_ref[k:k + 1], None, None, None])

    greet_neighbours(section, spot, active == 0)
    own = []
    for part in range(3):
        copy = pltpu.make_async_copy(ins[part], outs[part].at[spot], local_sem.at[part])
        copy.start()
        own.append(copy)

    pending = []

    def at(part, first, second, third, rows=None):
        index = [None, None, None]
        for axis, value in zip(ORDERS[part], (first, second, third)):
            index[axis] = value
        return outs[part].at[tuple(index) if rows is None else tuple(index) + (rows,)]

    def here(part):
        return tuple(spot[axis] for axis in ORDERS[part])

    def near(value, by):
        return lax.rem(value + by, 4)

    full = pl.ds(0, 4)

    def halves(half):
        return pl.ds(2 * half, 2)

    def remote(part, axis, slot, way, src, dst):
        by = 1 if way == 0 else 3
        return pltpu.make_async_remote_copy(
            src_ref=src, dst_ref=dst, send_sem=send_sem.at[part, slot, way], recv_sem=recv_sem.at[part, slot, way],
            device_id=device_at(section, shifted(spot, ORDERS[part][axis], by)), device_id_type=MESH)

    def send(part, axis, slot, way, src, dst=None):
        copy = remote(part, axis, slot, way, src, src if dst is None else dst)
        copy.start()
        pending.append(copy)

    def came(part, axis, slot, way, ref):
        remote(part, axis, slot, way, ref, ref).wait_recv()

    BACK = (3, 1)

    def third_item(part, item, by):
        p1, p2, p3 = here(part)
        for way in (0, 1):
            send(part, 2, 4 + 2 * item, way, at(part, full, near(p2, by), p3))

    def third_pass(part, item, by):
        p1, p2, p3 = here(part)
        for way in (0, 1):
            came(part, 2, 4 + 2 * item, way, at(part, full, near(p2, by), near(p3, BACK[way])))
            send(part, 2, 5 + 2 * item, way, at(part, halves(way), near(p2, by), near(p3, BACK[way])))

    for part in range(3):
        p1, p2, p3 = here(part)
        for way in (0, 1):
            send(part, 0, 0, way, ins[part], at(part, p1, p2, p3))
    if active == 0:
        spread_rows(spread_ref)
    for part in range(3):
        p1, p2, p3 = here(part)
        for way in (0, 1):
            v = near(p1, BACK[way])
            came(part, 0, 0, way, at(part, v, p2, p3))
            send(part, 0, 1, way, at(part, v, p2, p3, cut_of(ROWS_OF[part], way)))
    for part in range(3):
        p1, p2, p3 = here(part)
        for way in (0, 1):
            came(part, 0, 1, way, at(part, near(p1, 2), p2, p3, cut_of(ROWS_OF[part], way)))
        own[part].wait()
        for way in (0, 1):
            send(part, 1, 2, way, at(part, full, p2, p3))
    for part in range(3):
        third_item(part, 0, 0)
    for part in range(3):
        p1, p2, p3 = here(part)
        for way in (0, 1):
            v = near(p2, BACK[way])
            came(part, 1, 2, way, at(part, full, v, p3))
            send(part, 1, 3, way, at(part, halves(way), v, p3))
    for part in range(3):
        third_item(part, 1, 3)
        third_item(part, 2, 1)
    if active == 0:
        pl.semaphore_signal(turn_sem, inc=1, device_id=device_at(1, spot), device_id_type=MESH)
    for part in range(3):
        p1, p2, p3 = here(part)
        for way in (0, 1):
            came(part, 1, 3, way, at(part, halves(way), near(p2, 2), p3))
        third_item(part, 3, 2)
    for item, by in ((0, 0), (1, 3), (2, 1), (3, 2)):
        for part in range(3):
            third_pass(part, item, by)
    for item, by in ((0, 0), (1, 3), (2, 1), (3, 2)):
        for part in range(3):
            p1, p2, p3 = here(part)
            for way in (0, 1):
                came(part, 2, 5 + 2 * item, way, at(part, halves(way), near(p2, by), near(p3, 2)))
    for copy in pending:
        copy.wait_send()


def gather_all(active, ident, shards, held=()):
    vmem = pl.BlockSpec(memory_space=pltpu.VMEM)
    anywhere = pl.BlockSpec(memory_space=pl.ANY)
    return pl.pallas_call(
        functools.partial(gather_kernel, active),
        out_shape=[jax.ShapeDtypeStruct((4, 4, 4, r, 768), jnp.bfloat16) for r in ROWS_OF] + (
            [jax.ShapeDtypeStruct((768, 1024), jnp.bfloat16)] if active == 0 else []),
        in_specs=[vmem] * 6 + [anywhere] * len(held),
        out_specs=[anywhere] * 3 + ([vmem] if active == 0 else []),
        scratch_shapes=[
            pltpu.VMEM((64, 768), jnp.bfloat16),
            pltpu.VMEM((64, 768), jnp.bfloat16),
            pltpu.VMEM((16, 768), jnp.float32),
            pltpu.SemaphoreType.DMA((3,)),
            pltpu.SemaphoreType.DMA((3, 12, 2)),
            pltpu.SemaphoreType.DMA((3, 12, 2)),
            pltpu.SemaphoreType.REGULAR,
        ],
        input_output_aliases={6: 0, 7: 1, 8: 2} if held else {},
        compiler_params=pltpu.CompilerParams(collective_id=ident, has_side_effects=True),
    )(*shards, *held)


def wide(ref, index):
    return ref[index].astype(jnp.float32)


def scatter_kernel(active, *refs):
    if active == 1:
        @pl.when(lax.axis_index("section") == 1)
        def _():
            scatter_body(*refs)
        return
    ins, upper, outs, sums, refs = refs[:3], refs[3:6], refs[6:12], refs[12:15], refs[15:]

    def final(a_ref, b_ref, c_ref):
        qkv, out, fc, proj, small, line = outs
        for i in range(3):
            qkv[:, 768 * i:768 * i + 768] = a_ref[16 * i:16 * i + 12]
        out[...] = a_ref[48:60]
        proj[...] = c_ref[...]
        for k in range(4):
            fc[:, 768 * k:768 * k + 768] = b_ref[16 * k:16 * k + 12]
            line[k:k + 1] = b_ref[16 * k + 12:16 * k + 13]
        for i, row in enumerate((61, 13, 62, 12, 44, 60, 14, 15)):
            small[i:i + 1] = a_ref[row:row + 1]

    @pl.when(lax.axis_index("section") == 0)
    def _():
        scatter_body(*ins, *sums, *refs)
        final(*sums)

    @pl.when(lax.axis_index("section") == 1)
    def _():
        final(*upper)


def scatter_body(*refs):
    ins, outs = refs[:3], refs[3:6]
    box0, box1, box2 = refs[6:9], refs[9:12], refs[12:15]
    own, mid, work1, work2 = refs[15:18], refs[18:21], refs[21:24], refs[24:27]
    local_sem, send_sem, recv_sem = refs[27:30]
    section = lax.axis_index("section")
    spot = coordinates()
    greet_neighbours(section, spot)

    def here(part):
        return tuple(spot[axis] for axis in ORDERS[part])

    def near(value, by):
        return lax.rem(value + by, 4)

    def at(part, first, second, third=pl.ds(0, 4)):
        index = [None, None, None]
        for axis, value in zip(ORDERS[part], (first, second, third)):
            index[axis] = value
        return ins[part].at[tuple(index)]

    def halves(half):
        return pl.ds(2 * half, 2)

    def remote(part, axis, slot, way, src, dst):
        by = 1 if way == 0 else 3
        return pltpu.make_async_remote_copy(
            src_ref=src, dst_ref=dst, send_sem=send_sem.at[part, slot, way], recv_sem=recv_sem.at[part, slot, way],
            device_id=device_at(section, shifted(spot, ORDERS[part][axis], by)), device_id_type=MESH)

    pending = []

    def send(part, axis, slot, way, src, dst):
        copy = remote(part, axis, slot, way, src, dst)
        copy.start()
        pending.append(copy)

    def came(part, axis, slot, way, ref):
        remote(part, axis, slot, way, ref, ref).wait_recv()

    ITEMS = (2, 1, 3, 0)
    loads = {}

    def first_send(part, item):
        p1, p2, p3 = here(part)
        w = near(p2, ITEMS[item])
        for way in (0, 1):
            send(part, 0, 3 * item, way, at(part, near(p1, 2), w, halves(way)), box0[part].at[item, 0, halves(way)])
        for way in (0, 1):
            copy = pltpu.make_async_copy(
                at(part, near(p1, 1 + 2 * way), w, halves(way)), mid[part].at[item, halves(way)], local_sem.at[part, item, way])
            copy.start()
            loads[part, item, way] = copy
        copy = pltpu.make_async_copy(at(part, p1, w), own[part].at[item], local_sem.at[part, item, 2])
        copy.start()
        loads[part, item, 2] = copy
        for way in (0, 1):
            send(part, 0, 3 * item + 1, way, at(part, near(p1, 1 + 2 * way), w, halves(1 - way)),
                 box0[part].at[item, 1 + way, halves(1 - way)])

    def loop(count, body):
        def step(i, carry):
            body(i)
            return carry
        lax.fori_loop(0, count, step, 0)

    def first_middle(part, item):
        for way in (0, 1):
            got = box0[part].at[item, 0, halves(way)]
            came(part, 0, 3 * item, way, got)
            loads[part, item, way].wait()

            def body(i):
                f = box0[part]
                f[item, 0, 2 * way + i] = (wide(f, (item, 0, 2 * way + i)) + wide(mid[part], (item, 2 * way + i))).astype(f.dtype)

            loop(2, body)
            send(part, 0, 3 * item + 2, way, got, box0[part].at[item, 1 + way, halves(way)])

    def first_finish(part, item):
        box = box0[part]
        for way in (0, 1):
            came(part, 0, 3 * item + 1, way, box.at[item, 1 + way, halves(1 - way)])
            came(part, 0, 3 * item + 2, way, box.at[item, 1 + way, halves(way)])
        loads[part, item, 2].wait()

        def body(i):
            work1[part][item, i] = (
                wide(own[part], (item, i)) + wide(box, (item, 1, i)) + wide(box, (item, 2, i))).astype(box.dtype)

        loop(4, body)

    def second_far(part):
        for way in (0, 1):
            send(part, 1, 12, way, work1[part].at[0, halves(way)], box1[part].at[0, halves(way)])

    def second_raw(part):
        for way in (0, 1):
            send(part, 1, 13, way, work1[part].at[1 + way, halves(1 - way)], box1[part].at[1 + way, halves(1 - way)])

    def second_middle(part):
        for way in (0, 1):
            got = box1[part].at[0, halves(way)]
            came(part, 1, 12, way, got)

            def body(i):
                f = box1[part]
                f[0, 2 * way + i] = (wide(f, (0, 2 * way + i)) + wide(work1[part], (1 + way, 2 * way + i))).astype(f.dtype)

            loop(2, body)
            send(part, 1, 14, way, got, box1[part].at[1 + way, halves(way)])

    def second_finish(part):
        box = box1[part]
        for way in (0, 1):
            came(part, 1, 13, way, box.at[1 + way, halves(1 - way)])
            came(part, 1, 14, way, box.at[1 + way, halves(way)])

        def body(i):
            work2[part][i] = (wide(work1[part], (3, i)) + wide(box, (1, i)) + wide(box, (2, i))).astype(box.dtype)

        loop(4, body)

    def third_send(part):
        p1, p2, p3 = here(part)
        rows = ROWS_OF[part]
        for way in (0, 1):
            cut = cut_of(rows, way)
            send(part, 2, 15, way, work2[part].at[near(p3, 2), cut], box2[part].at[0, cut])
        for way in (0, 1):
            cut = cut_of(rows, 1 - way)
            send(part, 2, 16, way, work2[part].at[near(p3, 1 + 2 * way), cut], box2[part].at[1 + way, cut])

    def third_middle(part):
        p1, p2, p3 = here(part)
        rows = ROWS_OF[part]
        box = box2[part]
        for way in (0, 1):
            cut = cut_of(rows, way)
            came(part, 2, 15, way, box.at[0, cut])
            box[0, cut] = (wide(box, (0, cut)) + wide(work2[part], (near(p3, 1 + 2 * way), cut))).astype(box.dtype)
            send(part, 2, 17, way, box.at[0, cut], box.at[1 + way, cut])

    def third_finish(part):
        p1, p2, p3 = here(part)
        rows = ROWS_OF[part]
        box = box2[part]
        for way in (0, 1):
            came(part, 2, 16, way, box.at[1 + way, cut_of(rows, 1 - way)])
            came(part, 2, 17, way, box.at[1 + way, cut_of(rows, way)])
        outs[part][...] = wide(work2[part], p3) + wide(box, 1) + wide(box, 2)

    parts = range(3)
    for item in range(4):
        for part in parts:
            first_send(part, item)
    for item in range(4):
        for part in parts:
            first_middle(part, item)
    for part in parts:
        first_finish(part, 0)
        second_far(part)
    for part in parts:
        first_finish(part, 1)
        first_finish(part, 2)
        second_raw(part)
    for part in parts:
        second_middle(part)
    for part in parts:
        first_finish(part, 3)
    for part in parts:
        second_finish(part)
        third_send(part)
    for part in parts:
        third_middle(part)
    for part in parts:
        third_finish(part)
    for copy in pending:
        copy.wait_send()


def scatter_all(active, ident, grads, upper=()):
    scratch = []
    for shape in ((4, 3, 4), (3, 4), (3,), (4, 4), (4, 4), (4, 4), (4,)):
        scratch += [pltpu.VMEM(shape + (r, 768), jnp.bfloat16) for r in ROWS_OF]
    shapes = [(r, 768) for r in ROWS_OF]
    if upper:
        scratch = [pltpu.VMEM(shape, jnp.float32) for shape in shapes] + scratch
        shapes = [(12, 2304), (12, 768), (12, 3072), (48, 768), (8, 768), (4, 768)]
    vmem = pl.BlockSpec(memory_space=pltpu.VMEM)
    return pl.pallas_call(
        functools.partial(scatter_kernel, active),
        out_shape=[jax.ShapeDtypeStruct(shape, jnp.float32) for shape in shapes],
        in_specs=[pl.BlockSpec(memory_space=pl.ANY)] * 3 + [vmem] * len(upper),
        out_specs=[vmem] * len(shapes),
        scratch_shapes=scratch + [
            pltpu.SemaphoreType.DMA((3, 4, 3)),
            pltpu.SemaphoreType.DMA((3, 18, 2)),
            pltpu.SemaphoreType.DMA((3, 18, 2)),
        ],
        compiler_params=pltpu.CompilerParams(collective_id=ident, has_side_effects=True, vmem_limit_bytes=60 * 2**20),
    )(*grads, *upper)


EPS = 1e-05
ROOT = 0.7978845608028654
CUBIC = 0.044715
UNITS = 12
WIDTH = 768
PADDED = 1024
FF = 3072
ROWS = 128
HD = 64
BF = jnp.bfloat16
F32 = jnp.float32


def dot(left, right, over=((1,), (0,))):
    return lax.dot_general(left, right, (over, ((), ())), preferred_element_type=F32)


NT = ((1,), (1,))
TN = ((0,), (0,))


def ones_lane():
    return (lax.rem(lax.broadcasted_iota(jnp.int32, (1, PADDED), 1), 16) == 12).astype(F32)


def padded(rows, spread):
    return (dot(rows, spread) + ones_lane()).astype(BF)


def unpadded(rows, spread):
    high = rows.astype(BF)
    low = (rows - high.astype(F32)).astype(BF)
    return dot(high, spread, NT) + dot(low, spread, NT)


def extras(weight):
    lane = lax.rem(lax.broadcasted_iota(jnp.int32, (16, PADDED), 1), 16)
    row = lax.broadcasted_iota(jnp.int32, (16, PADDED), 0)
    return dot(((lane == row + 13) & (row < 3)).astype(F32).astype(BF), weight)


def normal(values):
    centre = values - jnp.mean(values, -1, keepdims=True)
    scale = lax.rsqrt(jnp.mean(centre * centre, -1, keepdims=True) + EPS)
    return centre * scale, scale


def norm_back(grad, n, scale):
    return scale * (grad - jnp.mean(grad, -1, keepdims=True) - n * jnp.mean(grad * n, -1, keepdims=True))


def flat(block):
    return block.reshape(PADDED, WIDTH)


def joined(ref, kind=0):
    return jnp.concatenate(
        [jnp.concatenate([ref[m * 6 + h, kind] for h in range(6)], axis=1) for m in range(2)], axis=0)


def split_into(ref, rows, kind=0):
    for m in range(2):
        for h in range(6):
            ref[m * 6 + h, kind] = rows[m * 64:(m + 1) * 64, h * 128:(h + 1) * 128]


def whole(shape):
    return pl.BlockSpec(shape, lambda *i: (0,) * len(shape))


VMEM_LIMIT = 60 * 2**20


def gelu_parts(f):
    t = jnp.tanh(ROOT * (f + CUBIC * f * f * f))
    return t, 0.5 * f * (1.0 + t)


SEQ = 1024
QB = 256


def head_mask(rows, head):
    lane = lax.broadcasted_iota(jnp.int32, rows.shape, 1)
    return jnp.where((lane >= 64 * head) & (lane < 64 * head + 64), rows, jnp.zeros_like(rows))


def rows_at(index, size):
    return pl.ds(pl.multiple_of(index * size, size), size)


class Exchange:
    def __init__(self, out_sems, back_sems, local_sem):
        self.place = (lax.axis_index("section"), lax.axis_index("fsdp"))
        self.me = lax.axis_index("ctx")
        self.out_sems, self.back_sems, self.local_sem = out_sems, back_sems, local_sem

    def device(self, ctx):
        return self.place + (ctx,)

    def greet(self):
        barrier = pltpu.get_barrier_semaphore()
        for unit in range(16):
            @pl.when((self.me != unit) & ((self.me < UNITS) | (unit < UNITS)))
            def _():
                pl.semaphore_signal(barrier, inc=1, device_id=self.device(unit), device_id_type=MESH)

    def greeted(self):
        barrier = pltpu.get_barrier_semaphore()

        @pl.when(self.me < UNITS)
        def _():
            pl.semaphore_wait(barrier, 15)

        @pl.when(self.me >= UNITS)
        def _():
            pl.semaphore_wait(barrier, UNITS)

    def outward(self, kind, unit, sender, src, dst):
        send, recv = self.out_sems
        return pltpu.make_async_remote_copy(
            src_ref=src.at[unit, kind], dst_ref=dst.at[kind, rows_at(sender, 64)], send_sem=send.at[kind, unit],
            recv_sem=recv.at[kind, sender], device_id=self.device(unit), device_id_type=MESH)

    def own_out(self, kind, src, dst):
        return pltpu.make_async_copy(src.at[self.me, kind], dst.at[kind, rows_at(self.me, 64)], self.local_sem.at[kind])

    def spread_out(self, kind, src, dst):
        for unit in range(UNITS):
            @pl.when(self.me != unit)
            def _():
                self.outward(kind, unit, self.me, src, dst).start()

        @pl.when(self.me < UNITS)
        def _():
            self.own_out(kind, src, dst).start()

    def spread_in(self, kind, src, dst):
        self.own_out(kind, src, dst).wait()
        for sender in range(16):
            @pl.when(self.me != sender)
            def _():
                self.outward(kind, 0, sender, src, dst).wait_recv()

    def spread_done(self, kind, src, dst):
        for unit in range(UNITS):
            @pl.when(self.me != unit)
            def _():
                self.outward(kind, unit, self.me, src, dst).wait_send()

    def inward(self, kind, unit, target, src, dst):
        send, recv = self.back_sems
        return pltpu.make_async_remote_copy(
            src_ref=src.at[kind, rows_at(target, 64)], dst_ref=dst.at[unit, kind], send_sem=send.at[kind, target],
            recv_sem=recv.at[kind, unit], device_id=self.device(target), device_id_type=MESH)

    def own_back(self, kind, src, dst):
        return pltpu.make_async_copy(
            src.at[kind, rows_at(self.me, 64)], dst.at[self.me, kind], self.local_sem.at[3 + kind])

    def return_to(self, kind, target, src, dst):
        @pl.when(self.me != target)
        def _():
            self.inward(kind, self.me, target, src, dst).start()

        @pl.when(self.me == target)
        def _():
            self.own_back(kind, src, dst).start()

    def return_in(self, kind, src, dst):
        for unit in range(UNITS):
            @pl.when(self.me != unit)
            def _():
                self.inward(kind, unit, 0, src, dst).wait_recv()

        @pl.when(self.me < UNITS)
        def _():
            self.own_back(kind, src, dst).wait()

    def return_done(self, kind, src, dst):
        @pl.when(self.me < UNITS)
        def _():
            for target in range(16):
                @pl.when(self.me != target)
                def _():
                    self.inward(kind, self.me, target, src, dst).wait_send()


def exchange_sems(out, back):
    return [
        pltpu.SemaphoreType.DMA((out, UNITS)), pltpu.SemaphoreType.DMA((out, 16)),
        pltpu.SemaphoreType.DMA((back, 16)), pltpu.SemaphoreType.DMA((back, UNITS)),
        pltpu.SemaphoreType.DMA((6,)),
    ]


def loop(count, body):
    def step(i, carry):
        body(i)
        return carry
    lax.fori_loop(0, count, step, 0)


def permuted(matrix, src, dst):
    count = src.shape[0]
    rows = jnp.concatenate([src[kind] for kind in range(count)], 1)
    moved = dot(matrix[...], rows).astype(BF)
    for kind in range(count):
        dst[kind] = moved[:, 128 * kind:128 * kind + 128]


def permutations(kpos_ref, qpos_ref, to_sorted, to_stored):
    to_sorted[...] = (lax.broadcasted_iota(jnp.int32, (SEQ, SEQ), 0) == qpos_ref[...]).astype(F32).astype(BF)
    to_stored[...] = (lax.broadcasted_iota(jnp.int32, (SEQ, SEQ), 1) == kpos_ref[...]).astype(F32).astype(BF)


def triangle(bias):
    row = lax.broadcasted_iota(jnp.int32, bias.shape, 0) - (SEQ - QB)
    column = lax.rem(lax.broadcasted_iota(jnp.int32, bias.shape, 1), QB)
    bias[...] = jnp.where(row <= column, 0.0, -1e30)


def both_heads(rows):
    return jnp.concatenate([head_mask(rows, 0), head_mask(rows, 1)], 0)


def attend(x_ref, lse_ref, out, vt, bias):
    for i in range(SEQ // QB):
        rows = pl.ds(i * QB, QB)
        size = (i + 1) * QB
        query = both_heads(x_ref[0, rows] * jnp.array(0.125, BF))
        s = dot(x_ref[1, 0:size], query, NT) + bias[SEQ - size:SEQ]
        top = jnp.max(s, 0, keepdims=True)
        e = jnp.exp(s - top)
        total = jnp.sum(e, 0, keepdims=True)
        e = e.astype(BF)
        share = 1.0 / total
        parts = [
            dot(vt[64 * h:64 * h + 64, 0:size], e[:, QB * h:QB * h + QB]) * share[:, QB * h:QB * h + QB] for h in range(2)]
        out[0, rows] = jnp.concatenate(parts, 0).T.astype(BF)
        stat = top + jnp.log(total)
        lse_ref[:, rows] = jnp.concatenate([stat[:, 0:QB], stat[:, QB:], jnp.zeros((6, QB), F32)], 0)


def attend_back(do_ref, x_ref, lse_ref, out, kt, dk, dv, bias):
    for i in range(SEQ // QB):
        rows = pl.ds(i * QB, QB)
        size = (i + 1) * QB
        query, do = both_heads(x_ref[0, rows]), both_heads(do_ref[0, rows])
        lse = jnp.concatenate([lse_ref[0:1, rows], lse_ref[1:2, rows]], 1)
        s = dot(x_ref[1, 0:size], query * jnp.array(0.125, BF), NT) + bias[SEQ - size:SEQ]
        p = jnp.exp(s - lse)
        dv[0:size] += dot(p.astype(BF), do)
        dp = dot(x_ref[2, 0:size], do, NT)
        delta = jnp.sum(p * dp, 0, keepdims=True)
        ds = (p * (dp - delta) * 0.125).astype(BF)
        dk[0:size] += dot(ds, query)
        parts = [dot(kt[64 * h:64 * h + 64, 0:size], ds[:, QB * h:QB * h + QB]) for h in range(2)]
        out[0, rows] = jnp.concatenate(parts, 0).T.astype(BF)
    out[1] = dk[...].astype(BF)
    out[2] = dv[...].astype(BF)


def forward_kernel(active, u_ref, w_ref, wf_ref, wp_ref, e_ref, kpos_ref, qpos_ref,
                   x_ref, lse_ref, o_ref, y_ref, r_ref, f_ref, low_ref,
                   qkv, landed, heads, apad, bpad, to_sorted, to_stored, sorted_out, att, vt, bias, *sems):
    step = pl.program_id(0)
    ex = Exchange(sems[0:2], sems[2:4], sems[4])
    mine = lax.axis_index("section") == active

    @pl.when((step == 0) & mine)
    def _():
        ex.greet()

    @pl.when(step == 0)
    def _():
        more = extras(flat(w_ref[...]))
        n, scale = normal(u_ref[...].astype(F32))
        apad[...] = padded((n * more[0:1] + more[1:2]).astype(BF), e_ref[...])
        triangle(bias)
        permutations(kpos_ref, qpos_ref, to_sorted, to_stored)

    for kind in range(3):
        @pl.when(step == kind)
        def _():
            split_into(qkv, dot(apad[...], flat(w_ref[...])).astype(BF), kind)

            @pl.when(mine)
            def _():
                if kind == 0:
                    ex.greeted()
                ex.spread_out(kind, qkv, landed)

    @pl.when((step == 2) & mine)
    def _():
        @pl.when(ex.me < UNITS)
        def _():
            for kind in range(3):
                ex.spread_in(kind, qkv, landed)
            permuted(to_sorted, landed, x_ref)
            vt[...] = x_ref[2].astype(F32).T.astype(BF)
            attend(x_ref, lse_ref, sorted_out, vt, bias)
            permuted(to_stored, sorted_out, att)
            for target in range(16):
                ex.return_to(0, target, att, heads)

        ex.return_in(0, att, heads)
        for kind in range(3):
            ex.spread_done(kind, qkv, landed)
        ex.return_done(0, att, heads)
        o_ref[...] = heads[...]

    @pl.when(step == 3)
    def _():
        wo = flat(w_ref[...])
        more = extras(wo)
        r = u_ref[...].astype(F32) + dot(padded(joined(heads), e_ref[...]), wo)
        r_ref[...] = r
        n, scale = normal(r)
        bpad[...] = padded((n * more[0:1] + more[1:2]).astype(BF), e_ref[...])
        y_ref[...] = r + more[2:3]

    @pl.when(step >= 3)
    def _():
        f = dot(bpad[...], flat(wf_ref[...]))
        f_ref[...] = f
        y_ref[...] += dot(gelu_parts(f)[1].astype(BF), wp_ref[...])

    @pl.when(step == 6)
    def _():
        low_ref[...] = y_ref[...].astype(BF)


def piece(index):
    return pl.BlockSpec((64, 16, WIDTH), index)


def forward_call(active, ident, u, weights, spread, kpos, qpos):
    ga, gb, gc = weights
    later = lambda s: jnp.maximum(s - 3, 0)
    return pl.pallas_call(
        functools.partial(forward_kernel, active),
        grid=(7,),
        out_shape=[
            jax.ShapeDtypeStruct((3, SEQ, 128), BF), jax.ShapeDtypeStruct((8, SEQ), F32),
            jax.ShapeDtypeStruct((UNITS, 1, 64, 128), BF), jax.ShapeDtypeStruct((ROWS, WIDTH), F32),
            jax.ShapeDtypeStruct((ROWS, WIDTH), F32), jax.ShapeDtypeStruct((ROWS, FF), F32),
            jax.ShapeDtypeStruct((ROWS, WIDTH), BF),
        ],
        in_specs=[
            whole((ROWS, WIDTH)), piece(lambda s: (0, jnp.minimum(s, 3), 0)), piece(lambda s: (0, later(s), 0)),
            pl.BlockSpec((WIDTH, WIDTH), lambda s: (later(s), 0)), whole((WIDTH, PADDED)),
            whole((SEQ, 1)), whole((1, SEQ)),
        ],
        out_specs=[
            whole((3, SEQ, 128)), whole((8, SEQ)), whole((UNITS, 1, 64, 128)), whole((ROWS, WIDTH)),
            whole((ROWS, WIDTH)), pl.BlockSpec((ROWS, WIDTH), lambda s: (0, later(s))),
            whole((ROWS, WIDTH)),
        ],
        scratch_shapes=[
            pltpu.VMEM((UNITS, 3, 64, 128), BF), pltpu.VMEM((3, SEQ, 128), BF), pltpu.VMEM((UNITS, 1, 64, 128), BF),
            pltpu.VMEM((ROWS, PADDED), BF), pltpu.VMEM((ROWS, PADDED), BF),
            pltpu.VMEM((SEQ, SEQ), BF), pltpu.VMEM((SEQ, SEQ), BF), pltpu.VMEM((1, SEQ, 128), BF),
            pltpu.VMEM((1, SEQ, 128), BF), pltpu.VMEM((128, SEQ), BF), pltpu.VMEM((SEQ, 2 * QB), F32),
        ] + exchange_sems(3, 1),
        compiler_params=pltpu.CompilerParams(collective_id=ident, has_side_effects=True, vmem_limit_bytes=VMEM_LIMIT),
    )(u, ga, gb, gc, spread, kpos, qpos)


def backward_kernel(active, g_ref, f_ref, r_ref, u_ref, o_ref, x_ref, lse_ref, kpos_ref, qpos_ref, e_ref,
                    w_ref, wf_ref, wp_ref, gu_ref, da_ref, db_ref, dc_ref, low_ref,
                    pad, acc, dr, small, gain, to_sorted, to_stored, sent, landed, sorted_do, sorted_out, dqkv, dx, kt, dk, dv, bias, *sems):
    step = pl.program_id(0)
    ex = Exchange(sems[0:2], sems[2:4], sems[4])
    mine = lax.axis_index("section") == active

    @pl.when((step == 0) & mine)
    def _():
        ex.greet()

    @pl.when(step == 0)
    def _():
        acc[...] = jnp.zeros_like(acc)
        triangle(bias)
        permutations(kpos_ref, qpos_ref, to_sorted, to_stored)
        more = extras(flat(w_ref[...]))
        n, scale = normal(r_ref[...])
        pad[...] = padded((n * more[0:1] + more[1:2]).astype(BF), e_ref[...])

    @pl.when(step < 4)
    def _():
        dm = g_ref[...]
        f = f_ref[...]
        t, act = gelu_parts(f)
        slope = 0.5 * (1.0 + t) + 0.5 * f * (1.0 - t * t) * (ROOT * (1.0 + 3 * CUBIC * f * f))
        df = (dot(dm, wp_ref[...], NT) * slope).astype(BF)
        dc_ref[...] = dot(act.astype(BF), dm, TN).astype(BF)
        db_ref[...] = dot(pad[...], df, TN).astype(BF).reshape(64, 16, WIDTH)
        acc[...] += dot(df, flat(wf_ref[...]), NT)

    @pl.when(step == 3)
    def _():
        dm = g_ref[...].astype(F32)
        wo = flat(w_ref[...])
        more = extras(wo)
        n, scale = normal(r_ref[...])
        db = unpadded(acc[...], e_ref[...])
        dr[...] = dm + norm_back(more[0:1] * db, n, scale)
        do = dot(dr[...].astype(BF), wo, NT).astype(BF)
        split_into(sent, dot(do, e_ref[...], NT).astype(BF))
        small[0:1] = jnp.sum(db * n, 0, keepdims=True)
        small[1:2] = jnp.sum(db, 0, keepdims=True)
        small[2:3] = jnp.sum(dm, 0, keepdims=True)

    @pl.when((step == 3) & mine)
    def _():
        ex.greeted()
        ex.spread_out(0, sent, landed)

        @pl.when(ex.me < UNITS)
        def _():
            kt[...] = x_ref[1].astype(F32).T.astype(BF)
            dk[...] = jnp.zeros_like(dk)
            dv[...] = jnp.zeros_like(dv)
            ex.spread_in(0, sent, landed)
            permuted(to_sorted, landed, sorted_do)
            attend_back(sorted_do, x_ref, lse_ref, sorted_out, kt, dk, dv, bias)
            permuted(to_stored, sorted_out, dqkv)
            for kind in range(3):
                for target in range(16):
                    ex.return_to(kind, target, dqkv, dx)

        for kind in range(3):
            ex.return_in(kind, dqkv, dx)
        ex.spread_done(0, sent, landed)
        for kind in range(3):
            ex.return_done(kind, dqkv, dx)

    def stored(grad, rows):
        grad = grad.reshape(64, 16, WIDTH)
        if rows is not None:
            at = lax.broadcasted_iota(jnp.int32, (16, WIDTH), 0)
            add = jnp.zeros((16, WIDTH), F32)
            for i, row in enumerate(rows):
                add = add + jnp.where(at == 13 + i, row, 0.0)
            grad = grad + add[None]
        da_ref[...] = grad.astype(BF)

    @pl.when(step == 4)
    def _():
        more = extras(flat(w_ref[...]))
        gain[...] = jnp.broadcast_to(more[0:1], gain.shape)
        n, scale = normal(u_ref[...].astype(F32))
        pad[...] = padded((n * more[0:1] + more[1:2]).astype(BF), e_ref[...])

    for kind in range(3):
        @pl.when(step == 4 + kind)
        def _():
            grad = joined(dx, kind)
            back = dot(grad, flat(w_ref[...]), NT)
            if kind == 0:
                acc[...] = back
            else:
                acc[...] += back
            stored(dot(pad[...], grad, TN), [small[i:i + 1] for i in range(3)] if kind == 0 else None)

    @pl.when(step == 7)
    def _():
        n, scale = normal(u_ref[...].astype(F32))
        da = unpadded(acc[...], e_ref[...])
        gu = dr[...] + norm_back(gain[0:1] * da, n, scale)
        gu_ref[...] = gu
        low_ref[...] = gu.astype(BF)
        grad = dot(padded(joined(o_ref), e_ref[...]), dr[...].astype(BF), TN)
        stored(grad, [jnp.sum(da * n, 0, keepdims=True), jnp.sum(da, 0, keepdims=True)])


def backward_call(active, ident, saved, g, weights, spread, kpos, qpos):
    u, x, lse, o, r, f = saved
    ga, gb, gc = weights
    early = lambda s: jnp.minimum(s, 3)
    late = lambda s: jnp.maximum(s - 4, 0)
    return pl.pallas_call(
        functools.partial(backward_kernel, active),
        grid=(8,),
        out_shape=[
            jax.ShapeDtypeStruct((ROWS, WIDTH), F32), jax.ShapeDtypeStruct((64, 64, WIDTH), BF),
            jax.ShapeDtypeStruct((64, 64, WIDTH), BF), jax.ShapeDtypeStruct((FF, WIDTH), BF),
            jax.ShapeDtypeStruct((ROWS, WIDTH), BF),
        ],
        in_specs=[
            whole((ROWS, WIDTH)), pl.BlockSpec((ROWS, WIDTH), lambda s: (0, early(s))), whole((ROWS, WIDTH)),
            whole((ROWS, WIDTH)), whole((UNITS, 1, 64, 128)), whole((3, SEQ, 128)), whole((8, SEQ)),
            whole((SEQ, 1)), whole((1, SEQ)), whole((WIDTH, PADDED)),
            piece(lambda s: (0, jnp.where(s < 4, 3, jnp.minimum(s - 4, 2)), 0)),
            piece(lambda s: (0, early(s), 0)), pl.BlockSpec((WIDTH, WIDTH), lambda s: (early(s), 0)),
        ],
        out_specs=[
            whole((ROWS, WIDTH)), piece(lambda s: (0, late(s), 0)), piece(lambda s: (0, early(s), 0)),
            pl.BlockSpec((WIDTH, WIDTH), lambda s: (early(s), 0)), whole((ROWS, WIDTH)),
        ],
        scratch_shapes=[
            pltpu.VMEM((ROWS, PADDED), BF), pltpu.VMEM((ROWS, PADDED), F32), pltpu.VMEM((ROWS, WIDTH), F32),
            pltpu.VMEM((8, WIDTH), F32), pltpu.VMEM((8, WIDTH), F32),
            pltpu.VMEM((SEQ, SEQ), BF), pltpu.VMEM((SEQ, SEQ), BF),
            pltpu.VMEM((UNITS, 1, 64, 128), BF), pltpu.VMEM((1, SEQ, 128), BF), pltpu.VMEM((1, SEQ, 128), BF),
            pltpu.VMEM((3, SEQ, 128), BF), pltpu.VMEM((3, SEQ, 128), BF), pltpu.VMEM((UNITS, 3, 64, 128), BF), pltpu.VMEM((128, SEQ), BF), pltpu.VMEM((SEQ, 128), F32),
            pltpu.VMEM((SEQ, 128), F32), pltpu.VMEM((SEQ, 2 * QB), F32),
        ] + exchange_sems(1, 3),
        compiler_params=pltpu.CompilerParams(collective_id=ident, has_side_effects=True, vmem_limit_bytes=VMEM_LIMIT),
    )(g, f, r, u, o, x, lse, kpos, qpos, spread, ga, gb, gc)


def positions(block_order):
    index = jnp.arange(SEQ, dtype=jnp.int32)
    blocks = block_order.shape[0]
    length = SEQ // blocks
    table = jnp.arange(blocks, dtype=jnp.int32)
    chosen = jnp.sum(jnp.where((index // length)[:, None] == table[None, :], block_order[None, :], 0), axis=1)
    return chosen * length + index % length


def placed(chunk, gains, biases, fc_bias):
    wide_rows = lax.dynamic_update_slice(
        jnp.zeros((8, WIDTH), F32), jnp.concatenate([gains, biases], 0).astype(F32), (0, 12 * chunk))
    line_rows = lax.dynamic_update_slice(jnp.zeros((FF,), F32), fc_bias.astype(F32), (48 * chunk,))
    return wide_rows, line_rows.reshape(4, WIDTH)


def local(boundary, block_order, qkv_weight, out_weight, fc_weight, proj_weight, gains, biases, fc_bias):
    section = lax.axis_index("section")
    chunk = lax.axis_index("fsdp") * 16 + lax.axis_index("ctx")
    key_pos = positions(block_order)
    kpos, qpos = key_pos[:, None], key_pos[None, :]
    shards = (qkv_weight[0], out_weight[0], fc_weight[0], proj_weight[0]) + placed(chunk, gains[0], biases[0], fc_bias[0])

    def shaped(gathered):
        ga, gb, gc = gathered
        return ga.reshape(64, 64, WIDTH), gb.reshape(64, 64, WIDTH), gc.reshape(FF, WIDTH)

    def split(grads):
        return [x.reshape(4, 4, 4, r, WIDTH) for x, r in zip(grads, ROWS_OF)]

    held = boundary[0].reshape(ROWS, WIDTH)
    *gathered, spread = gather_all(0, 0, shards)

    def forward(active, ident, weights, u):
        x, lse, o, y, r, f, low = forward_call(active, ident, u, weights, spread, kpos, qpos)
        return y, low, (u, x, lse, o, r, f)

    _, first, saved_lower = forward(0, 2, shaped(gathered), held)
    gathered = gather_all(1, 6, shards, (*gathered, first))
    first, *gathered = lax.optimization_barrier((first, *gathered))
    weights = shaped(gathered)
    sent = lax.ppermute(first, "section", [(0, 1)])
    y, _, saved_upper = forward(1, 3, weights, sent)
    *grads, back = backward_call(1, 4, saved_upper, held, weights, spread, kpos, qpos)[1:]
    returned = lax.ppermute(back, "section", [(1, 0)])
    returned, *grads = lax.optimization_barrier((returned, *grads))
    upper = scatter_all(1, 1, split(grads))
    returned, *upper = lax.optimization_barrier((returned, *upper))
    gu, *grads, _ = backward_call(0, 5, saved_lower, returned, weights, spread, kpos, qpos)
    qkv_grad, out_grad, fc_grad, proj_grad, small, line = scatter_all(0, 7, split(grads), upper)
    ends = jnp.where(section == 0, gu, y).reshape(1, 2, 1, 64, WIDTH)
    small = lax.dynamic_slice(small, (0, 12 * chunk), (8, 12))
    fc_small = lax.dynamic_slice(line.reshape(FF), (48 * chunk,), (48,))
    return (
        ends, qkv_grad[None], out_grad[None], fc_grad[None], proj_grad[None],
        small[0:2][None], small[2:8][None], fc_small[None],
    )


def solution(mesh):
    rows = P("section", ("fsdp", "ctx"), None)
    lanes = P("section", None, ("fsdp", "ctx"))
    ends = P("section", None, "fsdp", "ctx", None)
    flat_rows = P("section", ("fsdp", "ctx"))
    return jax.shard_map(
        local, mesh=mesh,
        in_specs=(ends, P(), rows, rows, rows, rows, lanes, lanes, flat_rows),
        out_specs=(ends, rows, rows, rows, rows, lanes, lanes, flat_rows),
        check_vma=False)
```
